32 devices in a mesh: dp: 4 (over z), blk: 4 (over y, x), tensor: 2 (over core).
Axes of the slice: x: 2, y: 2, z: 4, core: 2. Of those that a mesh axis runs over, the one named last changes fastest.
Arguments:
- tokens: bfloat16 [8192, 896], P(('dp', 'blk')), may hold values from -6 to 6
- lengths: int32 [4, 3], P('dp'), may hold values from 1 to 1537, 2016 in all within a row
- norm1_gain: bfloat16 [896], replicated, may hold values from 0.5 to 1.5
- w_query: bfloat16 [896, 896], P(None, 'tensor'), may hold values from -0.1875 to 0.1875
- b_query: bfloat16 [896], P('tensor'), may hold values from -3 to 3
- w_key: bfloat16 [896, 128], P(None, 'tensor'), may hold values from -0.1875 to 0.1875
- b_key: bfloat16 [128], P('tensor'), may hold values from -3 to 3
- w_value: bfloat16 [896, 128], P(None, 'tensor'), may hold values from -0.1875 to 0.1875
- b_value: bfloat16 [128], P('tensor'), may hold values from -3 to 3
- w_out: bfloat16 [896, 896], P('tensor'), may hold values from -6 to 6
- norm2_gain: bfloat16 [896], replicated, may hold values from 0.5 to 1.5
- w_gate: bfloat16 [896, 4864], P(None, 'tensor'), may hold values from -0.1875 to 0.1875
- w_up: bfloat16 [896, 4864], P(None, 'tensor'), may hold values from -0.1875 to 0.1875
- w_down: bfloat16 [4864, 896], P('tensor'), may hold values from -0.078125 to 0.078125
- cotangent: bfloat16 [8192, 896], P(('dp', 'blk')), may hold values from -6 to 6
Outputs:
- layer_out: bfloat16 [8192, 896], P(('dp', 'blk'))
- grad_tokens: float32 [8192, 896], P(('dp', 'blk'))
- grad_norm1: float32 [896], replicated
- grad_w_query: float32 [896, 896], P(None, 'tensor')
- grad_b_query: float32 [896], P('tensor')
- grad_w_key: float32 [896, 128], P(None, 'tensor')
- grad_b_key: float32 [128], P('tensor')
- grad_w_value: float32 [896, 128], P(None, 'tensor')
- grad_b_value: float32 [128], P('tensor')
- grad_w_out: float32 [896, 896], P('tensor')
- grad_norm2: float32 [896], replicated
- grad_w_gate: float32 [896, 4864], P(None, 'tensor')
- grad_w_up: float32 [896, 4864], P(None, 'tensor')
- grad_w_down: float32 [4864, 896], P('tensor')
The draws below stay inside these ranges and needn't reach their ends.
Inputs may be any that keep to these rules, and one draw needn't show every extreme that they name: Row g lists the lengths of group g's sequences in packing order; they sum to 2016, the remaining rows of the group being padding, and the longest is exactly 1537.
All inputs are finite; a program needn't handle non-finite values.
Results may differ from the reference program's by a relative error of at most 0.03.
Values may be sent and summed in bfloat16 or wider, within the bound.
No kernel may reach another device: no remote copies, remote signals or barrier semaphores. Data moves between devices by JAX's collectives and lax.ppermute only.
A program may use at most 192 MiB of HBM per device.

```python
import math
import jax
import jax.numpy as jnp
import numpy as np
from jax import lax

D = 896
HEADS = 14
KV_HEADS = 2
HEAD_DIM = 64
FF = 4864
TOK_DEV = 512
NSEQ = 3
PAD = 32
GROUP = 2048
TOKENS = 8192
N_DP = 4


def level_of(key, extent, split, least, top_value):
    def one(dim, shards_of):
        heights = jax.random.uniform(jax.random.fold_in(jax.random.fold_in(key, 6), dim), (shards_of,), jnp.float32, least / len(split), top_value / len(split))
        return jnp.repeat(jnp.exp(heights), extent[dim] // shards_of).reshape((-1,) + (1,) * (len(extent) - dim - 1))

    level = one(*split[0])
    for cut in split[1:]:
        level = level * one(*cut)
    return level


def profile(amount, total, limit, lean):
    portions = [(1 << 20) // math.isqrt(standing ** lean) + 1 for standing in range(2, amount + 1)]
    spare, counts = total - limit - (amount - 1), [1] * (amount - 1)
    while spare > 0:
        free = [i for i in range(amount - 1) if counts[i] < limit]
        pool, remaining = sum([portions[i] for i in free]), spare
        for i in free:
            extra = min(limit - counts[i], max(1, remaining * portions[i] // pool), spare)
            counts[i] = counts[i] + extra
            spare = spare - extra
    return np.array([limit] + counts)


def uneven_parts(stream_key, amount, total, reach, slope):
    if amount == 2:
        one = jax.random.randint(stream_key, (), max(1, total - reach), min(reach, total - 1) + 1)
        return jnp.stack([one, total - one])
    sizes = jnp.asarray(profile(amount, total, reach, slope), jnp.int32)
    pairs = (amount - 1) // 2
    giver, receiver = sizes[1:1 + 2 * pairs:2], sizes[2:2 + 2 * pairs:2]
    slack = jnp.minimum(giver - 1, reach - receiver)
    shifted = jax.random.randint(jax.random.fold_in(stream_key, 1), (pairs,), 0, 1 << 20) % (slack + 1)
    sizes = sizes.at[1:1 + 2 * pairs:2].set(giver - shifted).at[2:2 + 2 * pairs:2].set(receiver + shifted)
    return sizes[jax.random.permutation(jax.random.fold_in(stream_key, 2), amount)]


def scatter_about(rng, dims, width, bound, shards=(), kind=jnp.bfloat16):
    result = width * jax.random.normal(rng, dims, jnp.float32)
    if shards:
        result = result * level_of(rng, dims, shards, -0.22, 0.18)
    return jnp.clip(result, -bound, bound).astype(kind)


def setup_inputs(seed: int = 0) -> dict:
    key_list = jax.random.split(jax.random.key(seed), 16)
    return {
        "tokens": scatter_about(key_list[0], (TOKENS, D), 1.0, 6.0, ((0, 16),)),
        "lengths": jax.vmap(lambda own: uneven_parts(own, NSEQ, GROUP - PAD, GROUP - TOK_DEV + 1, 1))(jax.random.split(key_list[1], N_DP)).reshape((N_DP, NSEQ)).astype(jnp.int32),
        "norm1_gain": jnp.clip(1.0 + 0.1 * jax.random.normal(key_list[2], (D,), jnp.float32), 0.5, 1.5).astype(jnp.bfloat16),
        "w_query": scatter_about(key_list[3], (D, HEADS * HEAD_DIM), D ** -0.5, 0.1875, ((1, 2),)),
        "b_query": scatter_about(key_list[4], (HEADS * HEAD_DIM,), 0.5, 3.0, ((0, 2),)),
        "w_key": scatter_about(key_list[5], (D, KV_HEADS * HEAD_DIM), D ** -0.5, 0.1875, ((1, 2),)),
        "b_key": scatter_about(key_list[6], (KV_HEADS * HEAD_DIM,), 0.5, 3.0, ((0, 2),)),
        "w_value": scatter_about(key_list[7], (D, KV_HEADS * HEAD_DIM), D ** -0.5, 0.1875, ((1, 2),)),
        "b_value": scatter_about(key_list[8], (KV_HEADS * HEAD_DIM,), 0.5, 3.0, ((0, 2),)),
        "w_out": scatter_about(key_list[9], (HEADS * HEAD_DIM, D), (0.25 * GROUP ** 0.5 / (HEADS * HEAD_DIM) ** 0.5), 6.0, ((0, 2),)),
        "norm2_gain": jnp.clip(1.0 + 0.1 * jax.random.normal(key_list[10], (D,), jnp.float32), 0.5, 1.5).astype(jnp.bfloat16),
        "w_gate": scatter_about(key_list[11], (D, FF), D ** -0.5, 0.1875, ((1, 2),)),
        "w_up": scatter_about(key_list[12], (D, FF), D ** -0.5, 0.1875, ((1, 2),)),
        "w_down": scatter_about(key_list[13], (FF, D), FF ** -0.5, 0.078125, ((0, 2),)),
        "cotangent": scatter_about(key_list[14], (TOKENS, D), 1.0, 6.0, ((0, 16),)),
    }


epsilon = 1e-06
rope_base = 1000000.0
masked_value = -1e+30
highest = lax.Precision.HIGHEST

@jax.custom_vjp
def low(v):
    return lax.optimization_barrier(v.astype(jnp.bfloat16)).astype(jnp.float32)

@jax.custom_vjp
def low_back(v):
    return v

def low_keep(v):
    return (low(v), None)

def low_pass(kept, grad):
    return (grad,)

def back_keep(v):
    return (v, None)

def back_low(kept, grad):
    return (low(grad),)
low.defvjp(low_keep, low_pass)
low_back.defvjp(back_keep, back_low)

def layout(length_row, row_index):
    seq_ends = jnp.cumsum(length_row, dtype=jnp.int32)
    passed = (row_index[:, None] >= seq_ends[None, :]).astype(jnp.int32)
    segment = lax.optimization_barrier(jnp.sum(passed, axis=1, dtype=jnp.int32))
    offset = lax.optimization_barrier(jnp.sum(passed * length_row[None, :], axis=1, dtype=jnp.int32))
    return (segment, row_index - offset)

def rotary(vector, position, direction):
    half_dim = vector.shape[-1] // 2
    frequency = rope_base ** (-2.0 * jnp.arange(half_dim, dtype=jnp.float32) / vector.shape[-1])
    angles = position.astype(jnp.float32)[:, None] * frequency[None, :]
    cosine = jnp.cos(angles)[:, None, :]
    sine_part = direction * jnp.sin(angles)[:, None, :]
    first_half = vector[..., :half_dim]
    second_half = vector[..., half_dim:]
    return jnp.concatenate([first_half * cosine - second_half * sine_part, second_half * cosine + first_half * sine_part], axis=-1)

def rms_norm(vector, scale_gain):
    return vector * lax.rsqrt(lax.optimization_barrier(jnp.mean(vector * vector, axis=1, keepdims=True)) + epsilon) * scale_gain

def attend(queries, key_rows, values, segment):
    row_count = queries.shape[0]
    block_rows = math.gcd(row_count, 512)
    factor = queries.shape[-1] ** (-0.5)
    row_index = jnp.arange(row_count, dtype=jnp.int32)

    def one_block(block_item):
        block_query, block_segment, block_index = block_item
        raw_scores = low_back(jnp.einsum('qcgd,kcd->qcgk', block_query, key_rows, precision=highest) * factor)
        allowed = (block_segment[:, None] == segment[None, :]) & (row_index[None, :] <= block_index[:, None])
        masked = jnp.where(allowed[:, None, None, :], raw_scores, masked_value)
        row_max = lax.optimization_barrier(jnp.max(masked, axis=-1, keepdims=True))
        weight = jnp.exp(masked - row_max)
        probability = weight / lax.optimization_barrier(jnp.sum(weight, axis=-1, keepdims=True))
        return jnp.einsum('qcgk,kcd->qcgd', low(probability), values, precision=highest)
    shaped = (queries.reshape(row_count // block_rows, block_rows, queries.shape[1], queries.shape[2], queries.shape[3]), segment.reshape(row_count // block_rows, block_rows), row_index.reshape(row_count // block_rows, block_rows))
    attn_out = lax.map(jax.checkpoint(one_block), shaped)
    return attn_out.reshape(row_count, -1)

def forward(hidden_in, norm1_gain, w_query, b_query, w_key, b_key, w_value, b_value, w_out, norm2_gain, w_gate, w_up, w_down, segment, position):
    row_count = hidden_in.shape[0]
    kv_heads = w_key.shape[1] // HEAD_DIM
    group_share = w_query.shape[1] // w_key.shape[1]
    normed_one = low(rms_norm(hidden_in, norm1_gain))
    q_lin = low_back(jnp.dot(normed_one, w_query, precision=highest) + b_query)
    k_lin = low_back(jnp.dot(normed_one, w_key, precision=highest) + b_key)
    values = low(low_back(jnp.dot(normed_one, w_value, precision=highest) + b_value))
    q_rot = low(rotary(q_lin.reshape(row_count, kv_heads * group_share, HEAD_DIM), position, 1.0))
    k_rot = low(rotary(k_lin.reshape(row_count, kv_heads, HEAD_DIM), position, 1.0))
    group_rows = row_count // N_DP
    q_group = q_rot.reshape(N_DP, group_rows, kv_heads, group_share, HEAD_DIM)
    k_group = k_rot.reshape(N_DP, group_rows, kv_heads, HEAD_DIM)
    v_group = values.reshape(N_DP, group_rows, kv_heads, HEAD_DIM)
    s_group = segment.reshape(N_DP, group_rows)
    attention = lax.map(lambda group_item: attend(group_item[0], group_item[1], group_item[2], group_item[3]), (q_group, k_group, v_group, s_group))
    out_low = low(low_back(attention.reshape(row_count, -1)))
    hidden_mid = hidden_in + low_back(jnp.dot(out_low, w_out, precision=highest))
    normed_two = low(rms_norm(hidden_mid, norm2_gain))
    gate_val = low_back(jnp.dot(normed_two, w_gate, precision=highest))
    up_val = low_back(jnp.dot(normed_two, w_up, precision=highest))
    mixed_low = low(jax.nn.silu(gate_val) * up_val)
    return hidden_mid + jnp.dot(mixed_low, w_down, precision=highest)

def reference(tokens, lengths, norm1_gain, w_query, b_query, w_key, b_key, w_value, b_value, w_out, norm2_gain, w_gate, w_up, w_down, cotangent):
    group_rows = tokens.shape[0] // N_DP
    row_index = jnp.arange(group_rows, dtype=jnp.int32)
    segment, position = jax.vmap(lambda length_row: layout(length_row, row_index))(lengths)
    valid_rows = (segment < lengths.shape[1]).reshape(-1).astype(jnp.float32)
    segment = segment.reshape(-1)
    position = position.reshape(-1)
    floats = [item.astype(jnp.float32) for item in (tokens, norm1_gain, w_query, b_query, w_key, b_key, w_value, b_value, w_out, norm2_gain, w_gate, w_up, w_down)]
    output, pull_back = jax.vjp(lambda *weights: forward(*weights, segment, position), *floats)
    gradients = pull_back(cotangent.astype(jnp.float32) * valid_rows[:, None])
    return (output.astype(jnp.bfloat16), gradients[0], gradients[1], gradients[2], gradients[3], gradients[4], gradients[5], gradients[6], gradients[7], gradients[8], gradients[9], gradients[10], gradients[11], gradients[12])
```

```python
import functools
import math

import jax
import jax.numpy as jnp
from jax import lax
from jax.experimental import pallas as pl
from jax.experimental.pallas import tpu as pltpu
from jax.sharding import PartitionSpec as P

HEAD_DIM = 64

epsilon = 1e-06
rope_base = 1000000.0
masked_value = -1e30

low = jnp.bfloat16
wide = jnp.float32
vmem_limit = 50 * 1024 * 1024


def dot_nn(left, right):
    return lax.dot_general(left, right, (((1,), (0,)), ((), ())), preferred_element_type=wide)


def dot_nt(left, right):
    return lax.dot_general(left, right, (((1,), (1,)), ((), ())), preferred_element_type=wide)


def dot_tn(left, right):
    return lax.dot_general(left, right, (((0,), (0,)), ((), ())), preferred_element_type=wide)


def partner(value, axis, step):
    count = lax.axis_size(axis)
    return lax.ppermute(value, axis, [(i, i ^ step) for i in range(count)])


def gather_blocks(piece):
    count = lax.axis_size("blk")
    return [piece] + [partner(piece, "blk", r) for r in range(1, count)]


def gather_relayed(piece):
    count = lax.axis_size("blk")
    rows = piece.shape[0] // 2
    first, second = [piece[:rows]], [piece[rows:]]
    for r in range(1, count):
        low_bit = r & -r
        high_bit = 1 << (r.bit_length() - 1)
        if low_bit == r:
            whole = partner(piece, "blk", r)
            first.append(whole[:rows])
            second.append(whole[rows:])
        else:
            first.append(partner(first[r ^ high_bit], "blk", high_bit))
            second.append(partner(second[r ^ low_bit], "blk", low_bit))
    return first, second


def scatter_blocks(stacked):
    return [stacked[0]] + [partner(stacked[r], "blk", r) for r in range(1, stacked.shape[0])]


def line_sum(value):
    count = lax.axis_size("dp")
    middle = count // 2
    index = lax.axis_index("dp")
    total = value.astype(low)
    for s in range(middle - 1):
        passed = lax.ppermute(total, "dp", [(s, s + 1), (count - 1 - s, count - 2 - s)])
        total = (total.astype(wide) + passed.astype(wide)).astype(low)
    passed = lax.ppermute(total, "dp", [(middle - 1, middle), (middle, middle - 1)])
    total = (total.astype(wide) + passed.astype(wide)).astype(low)
    for s in range(middle - 1):
        passed = lax.ppermute(
            total, "dp", [(middle - 1 - s, middle - 2 - s), (middle + s, middle + s + 1)]
        )
        arrived = (index == middle - 2 - s) | (index == middle + s + 1)
        total = jnp.where(arrived, passed, total)
    return total


def call(body, outs, ins, scratch=(), grid=None, in_specs=None, out_specs=None, flops=0):
    whole = pl.BlockSpec(memory_space=pltpu.VMEM)
    moved = sum(math.prod(v.shape) * v.dtype.itemsize for v in list(outs) + list(ins))
    extra = {} if grid is None else {"grid": grid}
    return pl.pallas_call(
        body,
        out_shape=tuple(outs),
        in_specs=in_specs or [whole] * len(ins),
        out_specs=out_specs or tuple([whole] * len(outs)),
        scratch_shapes=list(scratch),
        cost_estimate=pl.CostEstimate(flops=flops, bytes_accessed=moved, transcendentals=0),
        compiler_params=pltpu.CompilerParams(vmem_limit_bytes=vmem_limit),
        **extra,
    )(*ins)


def shape(dims, kind):
    return jax.ShapeDtypeStruct(dims, kind)


in_smem = pl.BlockSpec(memory_space=pltpu.SMEM)
in_vmem = pl.BlockSpec(memory_space=pltpu.VMEM)


def segment_start(lengths_ref, rows):
    start = jnp.zeros_like(rows)
    end = jnp.int32(0)
    for i in range(lengths_ref.shape[1]):
        end = end + lengths_ref[0, i]
        start = jnp.where(rows >= end, end, start)
    return start


def rotate(pair, cosine, sine):
    half = HEAD_DIM // 2
    first, second = pair[:half], pair[half:]
    return jnp.concatenate(
        [first * cosine - second * sine, second * cosine + first * sine], axis=0
    )


def enter_kernel(
    lengths_ref, place_ref, tokens_ref, gain_ref, wq_ref, wk_ref, wv_ref, bq_ref, bk_ref, bv_ref,
    turn_ref, q_ref, kv_ref, normed_ref, tokens_t_ref, cos_ref, sin_ref,
):
    rows = tokens_ref.shape[0]
    hidden = tokens_ref[...].astype(wide)
    inverse = lax.rsqrt(jnp.mean(hidden * hidden, axis=1, keepdims=True) + epsilon)
    normed = (hidden * inverse * gain_ref[...].astype(wide)).astype(low)
    tokens_t_ref[...] = hidden.T.astype(low)
    normed_ref[...] = normed.astype(wide).T.astype(low)
    index = place_ref[0] * rows + lax.broadcasted_iota(jnp.int32, (1, rows), 1)
    position = (index - segment_start(lengths_ref, index)).astype(wide)
    angles = turn_ref[...] * position
    cosine, sine = jnp.cos(angles), jnp.sin(angles)
    cos_ref[...] = cosine
    sin_ref[...] = sine
    q_lin = dot_nn(normed, wq_ref[...]) + bq_ref[...].astype(wide)
    width = q_lin.shape[1]
    padded = -(-width // 128) * 128
    if padded != width:
        q_lin = jnp.concatenate([q_lin, jnp.zeros((rows, padded - width), wide)], axis=1)
    q_turned = q_lin.T
    for h in range(width // HEAD_DIM):
        head = rotate(q_turned[h * HEAD_DIM : (h + 1) * HEAD_DIM], cosine, sine)
        q_ref[h * HEAD_DIM : (h + 1) * HEAD_DIM, :] = head.astype(low) * low(HEAD_DIM**-0.5)
    k_lin = dot_nn(normed, wk_ref[...]) + bk_ref[...].astype(wide)
    v_lin = dot_nn(normed, wv_ref[...]) + bv_ref[...].astype(wide)
    both = jnp.concatenate([k_lin, v_lin], axis=1).T
    both = jnp.concatenate([rotate(both[:HEAD_DIM], cosine, sine), both[HEAD_DIM:]], axis=0)
    kv_ref[...] = both.T.astype(low)


def mask_bias(key_base, key_rows, q_index, q_start):
    keys = key_base + lax.broadcasted_iota(jnp.int32, (key_rows, q_index.shape[1]), 0)
    return jnp.where((keys >= q_start) & (keys <= q_index), 0.0, masked_value)


def attend_kernel(
    lengths_ref, place_ref, q_ref, kv_ref, w_out_ref,
    out_ref, log_ref, part_ref,
    acc_ref, max_ref, bias_ref,
):
    rows = q_ref.shape[1]
    heads = q_ref.shape[0] // HEAD_DIM
    own = place_ref[0]
    q_index = own * rows + lax.broadcasted_iota(jnp.int32, (1, rows), 1)
    q_start = segment_start(lengths_ref, q_index)
    base = own * rows
    first_key = jnp.int32(0)
    end = jnp.int32(0)
    for i in range(lengths_ref.shape[1]):
        end = end + lengths_ref[0, i]
        first_key = jnp.where(base >= end, end, first_key)
    acc_ref[...] = jnp.zeros_like(acc_ref)
    max_ref[...] = jnp.full_like(max_ref, masked_value)

    def visit(block, carry):
        key_base = pl.multiple_of(block * rows, rows)
        pair = kv_ref[pl.ds(key_base, rows), :]
        keys = pair[:, :HEAD_DIM]
        values = pair.astype(wide).T[HEAD_DIM:].astype(low)
        values = jnp.concatenate([values, jnp.ones((16, rows), low)], axis=0)
        bias_ref[...] = mask_bias(key_base, rows, q_index, q_start)
        for h in range(heads):
            scores = dot_nn(keys, q_ref[h * HEAD_DIM : (h + 1) * HEAD_DIM, :]) + bias_ref[...]
            old = max_ref[h : h + 1, :]
            new = jnp.maximum(old, jnp.max(scores, axis=0, keepdims=True))
            weight = jnp.exp(scores - new).astype(low)
            acc_ref[h] = acc_ref[h] * jnp.exp(old - new) + dot_nn(values, weight)
            max_ref[h : h + 1, :] = new
        return carry

    lax.fori_loop(first_key // rows, own + 1, visit, 0)
    for h in range(heads):
        total = acc_ref[h, HEAD_DIM : HEAD_DIM + 1, :]
        out_ref[h * HEAD_DIM : (h + 1) * HEAD_DIM, :] = acc_ref[h, :HEAD_DIM, :] / total
        log_ref[h : h + 1, :] = max_ref[h : h + 1, :] + jnp.log(total)
    part_ref[...] = dot_tn(w_out_ref[...], out_ref[...].astype(low))


def middle_kernel(place_ref, tokens_ref, part_ref, passed_ref, gain_ref, hidden_ref, normed_ref):
    half = hidden_ref.shape[1]
    mine = pl.ds(pl.multiple_of(place_ref[1] * half, half), half)
    hidden = tokens_ref[:, mine].astype(wide) + part_ref[:, mine] + passed_ref[...].astype(wide)
    hidden_ref[...] = hidden
    inverse = lax.rsqrt(jnp.mean(hidden * hidden, axis=0, keepdims=True) + epsilon)
    normed_ref[...] = (hidden * inverse * gain_ref[...].astype(wide)).astype(low)


def hidden_kernel(
    x_ref, gy_ref, gate_t_ref, up_t_ref, down_ref, gate_ref, up_ref,
    mixed_ref, grad_gate_ref, grad_up_ref, grad_x_ref,
):
    x = x_ref[0]
    gate = dot_nn(gate_t_ref[...], x)
    up = dot_nn(up_t_ref[...], x)
    grad_mixed = dot_nt(down_ref[...], gy_ref[...])
    sigmoid = 1.0 / (1.0 + jnp.exp(-gate))
    silu = gate * sigmoid
    mixed_ref[0] = (silu * up).astype(low)
    grad_gate = (grad_mixed * up * sigmoid * (1.0 + gate * (1.0 - sigmoid))).astype(low)
    grad_up = (grad_mixed * silu).astype(low)
    grad_gate_ref[0] = grad_gate
    grad_up_ref[0] = grad_up
    grad_x_ref[0] = (dot_nn(gate_ref[...], grad_gate) + dot_nn(up_ref[...], grad_up)).astype(low)


def weight_kernel(dot, *refs):
    pairs, out_ref, acc_ref = refs[:-2], refs[-2], refs[-1]
    step = pl.program_id(0)

    def both(ref):
        return ref[0] if len(ref.shape) == 3 else ref[...]

    total = dot(both(pairs[0]), both(pairs[1]))
    for i in range(2, len(pairs), 2):
        total = total + dot(both(pairs[i]), both(pairs[i + 1]))

    @pl.when(step == 0)
    def _():
        acc_ref[...] = total

    @pl.when(step > 0)
    def _():
        acc_ref[...] += total

    @pl.when(step == pl.num_programs(0) - 1)
    def _():
        out_ref[...] = acc_ref[...].astype(low)


def project_kernel(weight_ref, mixed_ref, out_ref):
    out_ref[0] = dot_nn(weight_ref[...], mixed_ref[0]).astype(low)


def sum_blocks(refs):
    total = refs[0][...].astype(wide)
    for ref in refs[1:]:
        total = total + ref[...].astype(wide)
    return total


def layer_kernel(hidden_ref, *refs):
    out_ref = refs[-1]
    out_ref[...] = (hidden_ref[...] + sum_blocks(refs[:-1])).T.astype(low)


def grad_middle_kernel(hidden_ref, gain_ref, gy_ref, *refs):
    grad_ref, grad_low_ref, grad_gain_ref = refs[-3:]
    hidden = hidden_ref[...]
    inverse = lax.rsqrt(jnp.mean(hidden * hidden, axis=0, keepdims=True) + epsilon)
    grad_normed = sum_blocks(refs[:-3])
    weighted = gain_ref[...].astype(wide) * grad_normed
    inner = jnp.mean(weighted * hidden, axis=0, keepdims=True)
    grad = inverse * weighted - hidden * (inverse * inverse * inverse * inner)
    grad = grad + gy_ref[...].astype(wide).T
    grad_ref[...] = grad
    grad_low_ref[...] = grad.astype(low)
    grad_gain_ref[...] = jnp.sum(grad_normed * hidden * inverse, axis=1, keepdims=True)


def attend_back_kernel(
    lengths_ref, place_ref, gm_mine_ref, gm_other_ref, w_out_ref, out_ref, log_ref, q_ref, kv_ref, cos_ref, sin_ref,
    grad_w_out_ref, grad_q_ref, grad_kv_ref,
    gm_ref, go_ref, delta_ref, bias_ref, dq_ref, dk_ref, dv_ref,
):
    rows = q_ref.shape[1]
    half = rows // 2
    heads = q_ref.shape[0] // HEAD_DIM
    blocks = kv_ref.shape[0] // rows
    own, core = place_ref[0], place_ref[1]
    gm_ref[:, pl.ds(pl.multiple_of(core * half, half), half)] = gm_mine_ref[...]
    gm_ref[:, pl.ds(pl.multiple_of((1 - core) * half, half), half)] = gm_other_ref[...]
    grad_out = dot_nn(w_out_ref[...], gm_ref[...]).astype(low)
    go_ref[...] = grad_out
    grad_w_out_ref[...] = dot_nt(out_ref[...].astype(low), gm_ref[...]).astype(low)
    product = grad_out.astype(wide) * out_ref[...]
    for h in range(heads):
        delta_ref[h : h + 1, :] = jnp.sum(
            product[h * HEAD_DIM : (h + 1) * HEAD_DIM], axis=0, keepdims=True
        )
    dq_ref[...] = jnp.zeros_like(dq_ref)
    q_index = own * rows + lax.broadcasted_iota(jnp.int32, (1, rows), 1)
    q_start = segment_start(lengths_ref, q_index)
    base = own * rows
    first_key = jnp.int32(0)
    end = jnp.int32(0)
    for i in range(lengths_ref.shape[1]):
        end = end + lengths_ref[0, i]
        first_key = jnp.where(base >= end, end, first_key)
    first_block = first_key // rows

    def clear(block, carry):
        grad_kv_ref[block ^ own] = jnp.zeros((rows, 2 * HEAD_DIM), low)
        return carry

    lax.fori_loop(0, first_block, clear, 0)
    lax.fori_loop(own + 1, blocks, clear, 0)

    def visit(block, carry):
        key_base = pl.multiple_of(block * rows, rows)
        pair = kv_ref[pl.ds(key_base, rows), :]
        keys = pair[:, :HEAD_DIM]
        values = pair[:, HEAD_DIM:]
        keys_t = pair.astype(wide).T[:HEAD_DIM].astype(low)
        bias_ref[...] = mask_bias(key_base, rows, q_index, q_start)
        for h in range(heads):
            span = slice(h * HEAD_DIM, (h + 1) * HEAD_DIM)
            scores = dot_nn(keys, q_ref[span, :]) + bias_ref[...]
            weight = jnp.exp(scores - log_ref[h : h + 1, :])
            grad_weight = dot_nn(values, go_ref[span, :])
            grad_scores = (weight * (grad_weight - delta_ref[h : h + 1, :])).astype(low)
            dq_ref[span, :] += dot_nn(keys_t, grad_scores)
            dk = dot_nt(grad_scores, q_ref[span, :])
            dv = dot_nt(weight.astype(low), go_ref[span, :])
            if h == 0:
                dk_ref[...] = dk
                dv_ref[...] = dv
            else:
                dk_ref[...] += dk
                dv_ref[...] += dv
        grad_kv_ref[block ^ own] = jnp.concatenate([dk_ref[...], dv_ref[...]], axis=1).astype(low)
        return carry

    lax.fori_loop(first_block, own + 1, visit, 0)
    for h in range(heads):
        span = slice(h * HEAD_DIM, (h + 1) * HEAD_DIM)
        turned = rotate(dq_ref[span, :] * HEAD_DIM**-0.5, cos_ref[...], -sin_ref[...])
        grad_q_ref[span, :] = turned.astype(low)


def query_kernel(normed_ref, grad_q_ref, wq_ref, grad_wq_ref, part_ref, grad_bq_ref):
    grad_q = grad_q_ref[...]
    grad_wq_ref[...] = dot_nt(normed_ref[...], grad_q).astype(low)
    part_ref[...] = dot_nn(wq_ref[...], grad_q)
    grad_bq_ref[...] = jnp.sum(grad_q.astype(wide), axis=1, keepdims=True)


def key_kernel(place_ref, normed_ref, tokens_ref, part_ref, wk_ref, wv_ref, cos_ref, sin_ref, *refs):
    grad_wkv_ref, mine_ref, other_ref, grad_bkv_ref, grad_gain_ref, sum_ref = refs[-6:]
    both = sum_blocks(refs[:-6]).T
    both = jnp.concatenate(
        [rotate(both[:HEAD_DIM], cos_ref[...], -sin_ref[...]), both[HEAD_DIM:]], axis=0
    ).astype(low)
    grad_wkv_ref[...] = dot_nt(normed_ref[...], both).astype(low)
    grad_bkv_ref[...] = jnp.sum(both.astype(wide), axis=1, keepdims=True)
    total = part_ref[...] + dot_nn(wk_ref[...], both[:HEAD_DIM]) + dot_nn(wv_ref[...], both[HEAD_DIM:])
    sum_ref[...] = total
    hidden = tokens_ref[...].astype(wide)
    inverse = lax.rsqrt(jnp.mean(hidden * hidden, axis=0, keepdims=True) + epsilon)
    grad_gain_ref[...] = jnp.sum(total * (hidden * inverse), axis=1, keepdims=True)
    half = mine_ref.shape[1]
    core = place_ref[1]
    mine_ref[...] = sum_ref[:, pl.ds(pl.multiple_of(core * half, half), half)]
    other_ref[...] = sum_ref[:, pl.ds(pl.multiple_of((1 - core) * half, half), half)].astype(low)


def leave_kernel(place_ref, tokens_ref, mine_ref, passed_ref, gain_ref, grad_mid_ref, out_ref):
    half = mine_ref.shape[1]
    hidden = tokens_ref[:, pl.ds(pl.multiple_of(place_ref[1] * half, half), half)].astype(wide)
    inverse = lax.rsqrt(jnp.mean(hidden * hidden, axis=0, keepdims=True) + epsilon)
    weighted = gain_ref[...].astype(wide) * (mine_ref[...] + passed_ref[...].astype(wide))
    inner = jnp.mean(weighted * hidden, axis=0, keepdims=True)
    grad = grad_mid_ref[...] + inverse * weighted - hidden * (inverse * inverse * inverse * inner)
    out_ref[...] = grad.T.astype(low)


def rows_kernel(count, place_ref, *refs):
    out_ref = refs[-1]
    step = pl.program_id(0)
    half = refs[0].shape[0]
    for r in range(count):

        @pl.when((step ^ place_ref[0]) == r)
        def _(r=r):
            out_ref[:half, :] = refs[r][...].astype(wide)
            out_ref[half:, :] = refs[count + r][...].astype(wide)


def columns_kernel(count, place_ref, *refs):
    out_ref = refs[-1]
    step = pl.program_id(0)
    width = refs[0].shape[1]
    half_steps = pl.num_programs(0) // 2
    for k in range(count):
        for first in (True, False):

            @pl.when((place_ref[0] == k) & ((step < half_steps) == first))
            def _(k=k, first=first):
                for r in range(count):
                    j = k ^ r
                    ref = refs[r] if first else refs[count + r]
                    out_ref[:, j * width : (j + 1) * width] = ref[...].astype(wide)


def place_rows(place, piece):
    first, second = gather_relayed(piece)
    count = len(first)
    rows, width = piece.shape
    (whole,) = call(
        functools.partial(rows_kernel, count),
        [shape((count * rows, width), wide)],
        [place] + first + second,
        grid=(count,),
        in_specs=[in_smem] + [in_vmem] * (2 * count),
        out_specs=(pl.BlockSpec((rows, width), lambda i: (i, 0)),),
    )
    return whole


def place_columns(place, piece):
    first, second = gather_relayed(piece)
    count = len(first)
    rows, width = piece.shape
    tile = 64
    steps = rows // tile
    half = steps // 2
    early = pl.BlockSpec((tile, width), lambda i: (jnp.minimum(i, half - 1), 0))
    late = pl.BlockSpec((tile, width), lambda i: (jnp.maximum(i - half, 0), 0))
    (whole,) = call(
        functools.partial(columns_kernel, count),
        [shape((rows, count * width), wide)],
        [place] + first + second,
        grid=(steps,),
        in_specs=[in_smem] + [early] * count + [late] * count,
        out_specs=(pl.BlockSpec((tile, count * width), lambda i: (i, 0)),),
    )
    return whole


def local(
    tokens,
    lengths,
    norm1_gain,
    w_query,
    b_query,
    w_key,
    b_key,
    w_value,
    b_value,
    w_out,
    norm2_gain,
    w_gate,
    w_up,
    w_down,
    cotangent,
):
    rows, width = tokens.shape
    half = rows // 2
    blocks = lax.axis_size("blk")
    own_block = lax.axis_index("blk")
    own_core = lax.axis_index("tensor")
    q_width = w_query.shape[1]
    heads = q_width // HEAD_DIM
    units = w_gate.shape[1] // blocks
    place = jnp.stack([own_block, own_core]).astype(jnp.int32)
    gain_two = norm2_gain.reshape(width, 1)

    def whole_rows(mine):
        other = partner(mine, "tensor", 1)
        return jnp.where(
            own_core == 0,
            jnp.concatenate([mine, other], axis=0),
            jnp.concatenate([other, mine], axis=0),
        )

    half_dim = HEAD_DIM // 2
    turn = (rope_base ** (-2.0 * jnp.arange(half_dim, dtype=wide) / HEAD_DIM)).reshape(half_dim, 1)
    q_t, key_value, normed_t, tokens_t, cosine, sine = call(
        enter_kernel,
        [
            shape((q_width, rows), low),
            shape((rows, 2 * HEAD_DIM), low),
            shape((width, rows), low),
            shape((width, rows), low),
            shape((half_dim, rows), wide),
            shape((half_dim, rows), wide),
        ],
        [
            lengths, place, tokens, norm1_gain.reshape(1, width), w_query, w_key, w_value,
            b_query.reshape(1, -1), b_key.reshape(1, -1), b_value.reshape(1, -1), turn,
        ],
        in_specs=[in_smem] * 2 + [in_vmem] * 9,
        flops=2 * rows * width * (q_width + 2 * HEAD_DIM),
    )
    whole_kv = lax.all_gather(key_value, "blk", axis=0, tiled=True)

    row_index = own_block * rows + own_core * half + jnp.arange(half, dtype=jnp.int32)
    real = (row_index < jnp.sum(lengths)).astype(low)
    grad_y = lax.dynamic_slice_in_dim(cotangent, own_core * half, half, 0) * real[:, None]
    grad_y, whole_kv = lax.optimization_barrier((grad_y, whole_kv))
    grad_y_mine = jnp.concatenate(gather_blocks(grad_y), axis=0)
    grad_y_other = partner(grad_y_mine, "tensor", 1)

    out_t, log_total, part = call(
        attend_kernel,
        [
            shape((q_width, rows), wide),
            shape((heads + 1, rows), wide),
            shape((width, rows), wide),
        ],
        [lengths, place, q_t, whole_kv, w_out],
        [
            pltpu.VMEM((heads, HEAD_DIM + 16, rows), wide),
            pltpu.VMEM((heads + 1, rows), wide),
            pltpu.VMEM((rows, rows), wide),
        ],
        in_specs=[in_smem] * 2 + [in_vmem] * 3,
        flops=4 * rows * rows * q_width * blocks,
    )
    part_other = lax.dynamic_slice_in_dim(part, (1 - own_core) * half, half, 1).astype(low)
    hidden, normed_two = call(
        middle_kernel,
        [shape((width, half), wide), shape((width, half), low)],
        [place, tokens_t, part, partner(part_other, "tensor", 1), gain_two],
        in_specs=[in_smem] + [in_vmem] * 4,
    )

    x_mine = jnp.stack(gather_blocks(normed_two))
    x_other = partner(x_mine, "tensor", 1)
    gate_own = lax.dynamic_slice_in_dim(w_gate, own_block * units, units, 1)
    up_own = lax.dynamic_slice_in_dim(w_up, own_block * units, units, 1)
    down_own = lax.dynamic_slice_in_dim(w_down, own_block * units, units, 0)
    gate_t, up_t, down_t = gate_own.T, up_own.T, down_own.T

    def cut(dims):
        return pl.BlockSpec((1,) + dims, lambda i: (i, 0, 0))

    unit_cut, width_cut = cut((units, half)), cut((width, half))
    row_cut = pl.BlockSpec((half, width), lambda i: (i, 0))

    def hidden_units(x, grad_rows):
        kept = shape((blocks, units, half), low)
        return call(
            hidden_kernel,
            [kept, kept, kept, shape((blocks, width, half), low)],
            [x, grad_rows, gate_t, up_t, down_own, gate_own, up_own],
            grid=(blocks,),
            in_specs=[width_cut, row_cut] + [in_vmem] * 5,
            out_specs=(unit_cut, unit_cut, unit_cut, width_cut),
            flops=10 * rows * blocks * width * units // 2,
        )

    mixed_mine, gate_mine, up_mine, back_mine = hidden_units(x_mine, grad_y_mine)
    mixed_other, gate_other, up_other, back_other = hidden_units(x_other, grad_y_other)
    back_passed = partner(back_other, "tensor", 1)

    def hidden_weight(dot, dims, arrays, specs):
        (out,) = call(
            functools.partial(weight_kernel, dot),
            [shape(dims, low)],
            arrays,
            [pltpu.VMEM(dims, wide)],
            grid=(blocks,),
            in_specs=specs,
            out_specs=(pl.BlockSpec(dims, lambda i: (0, 0)),),
            flops=2 * rows * blocks * width * units,
        )
        return out

    grad_w_down = hidden_weight(
        dot_nn,
        (units, width),
        [mixed_mine, grad_y_mine, mixed_other, grad_y_other],
        [unit_cut, row_cut] * 2,
    )
    back = (back_mine.astype(wide) + back_passed.astype(wide)).astype(low)
    back_pieces = scatter_blocks(back)
    grad_w_gate = hidden_weight(
        dot_nt,
        (width, units),
        [x_mine, gate_mine, x_other, gate_other],
        [width_cut, unit_cut] * 2,
    )
    grad_w_up = hidden_weight(
        dot_nt,
        (width, units),
        [x_mine, up_mine, x_other, up_other],
        [width_cut, unit_cut] * 2,
    )

    def project(mixed):
        (out,) = call(
            project_kernel,
            [shape((blocks, width, half), low)],
            [down_t, mixed],
            grid=(blocks,),
            in_specs=[in_vmem, unit_cut],
            out_specs=(width_cut,),
            flops=rows * blocks * width * units,
        )
        return out

    layer_passed = partner(project(mixed_other), "tensor", 1)
    layer_sum = (project(mixed_mine).astype(wide) + layer_passed.astype(wide)).astype(low)
    (layer_half,) = call(
        layer_kernel, [shape((half, width), low)], [hidden] + scatter_blocks(layer_sum)
    )
    layer_out = whole_rows(layer_half)
    grad_w_down = place_rows(place, line_sum(grad_w_down))
    grad_w_gate = place_columns(place, line_sum(grad_w_gate))
    grad_w_up = place_columns(place, line_sum(grad_w_up))

    grad_mid, grad_mid_low, grad_gain_two = call(
        grad_middle_kernel,
        [shape((width, half), wide), shape((width, half), low), shape((width, 1), wide)],
        [hidden, gain_two, grad_y] + back_pieces,
    )
    grad_w_out, grad_q, grad_kv = call(
        attend_back_kernel,
        [
            shape((q_width, width), low),
            shape((q_width, rows), low),
            shape((blocks, rows, 2 * HEAD_DIM), low),
        ],
        [
            lengths, place, grad_mid_low, partner(grad_mid_low, "tensor", 1), w_out, out_t, log_total, q_t,
            whole_kv, cosine, sine,
        ],
        [
            pltpu.VMEM((width, rows), low),
            pltpu.VMEM((q_width, rows), low),
            pltpu.VMEM((heads + 1, rows), wide),
            pltpu.VMEM((rows, rows), wide),
            pltpu.VMEM((q_width, rows), wide),
            pltpu.VMEM((rows, HEAD_DIM), wide),
            pltpu.VMEM((rows, HEAD_DIM), wide),
        ],
        in_specs=[in_smem] * 2 + [in_vmem] * 9,
        flops=10 * rows * rows * q_width * blocks,
    )
    kv_pieces = scatter_blocks(grad_kv)
    grad_w_query, normed_part, grad_b_query = call(
        query_kernel,
        [shape((width, q_width), low), shape((width, rows), wide), shape((q_width, 1), wide)],
        [normed_t, grad_q, w_query],
        flops=4 * rows * width * q_width,
    )
    grad_w_kv, normed_mine, normed_other, grad_b_kv, grad_gain_one = call(
        key_kernel,
        [
            shape((width, 2 * HEAD_DIM), low),
            shape((width, half), wide),
            shape((width, half), low),
            shape((2 * HEAD_DIM, 1), wide),
            shape((width, 1), wide),
        ],
        [place, normed_t, tokens_t, normed_part, w_key, w_value, cosine, sine] + kv_pieces,
        [pltpu.VMEM((width, rows), wide)],
        in_specs=[in_smem] + [in_vmem] * (7 + blocks),
    )
    (grad_half,) = call(
        leave_kernel,
        [shape((half, width), low)],
        [
            place, tokens_t, normed_mine, partner(normed_other, "tensor", 1),
            norm1_gain.reshape(width, 1), grad_mid,
        ],
        in_specs=[in_smem] + [in_vmem] * 5,
    )
    grad_tokens = whole_rows(grad_half).astype(wide)

    def total_blocks(partial):
        share = partial.shape[0] // blocks
        parts = jnp.stack(
            [
                lax.dynamic_slice_in_dim(partial, (own_block ^ r) * share, share, 0)
                for r in range(blocks)
            ]
        )
        pieces = scatter_blocks(parts)
        total = pieces[0].astype(wide)
        for piece in pieces[1:]:
            total = total + piece.astype(wide)
        stacked = jnp.stack(gather_blocks(line_sum(total)))
        ordered = [
            lax.dynamic_index_in_dim(stacked, own_block ^ j, 0, keepdims=False)
            for j in range(blocks)
        ]
        return jnp.concatenate(ordered, axis=0).astype(wide)

    grad_w_out = total_blocks(grad_w_out)
    grad_w_qkv = total_blocks(jnp.concatenate([grad_w_query, grad_w_kv], axis=1))
    gains = jnp.concatenate([grad_gain_one, grad_gain_two], axis=0).reshape(-1)
    gains = gains + partner(gains, "tensor", 1)
    small = jnp.concatenate([gains, grad_b_query.reshape(-1), grad_b_kv.reshape(-1)])
    for axis in ("blk", "dp"):
        step = 1
        while step < lax.axis_size(axis):
            small = small + partner(small, axis, step)
            step = 2 * step
    grad_b = small[2 * width :]
    return (
        layer_out,
        grad_tokens,
        small[:width],
        grad_w_qkv[:, :q_width],
        grad_b[:q_width],
        grad_w_qkv[:, q_width : q_width + HEAD_DIM],
        grad_b[q_width : q_width + HEAD_DIM],
        grad_w_qkv[:, q_width + HEAD_DIM :],
        grad_b[q_width + HEAD_DIM :],
        grad_w_out,
        small[width : 2 * width],
        grad_w_gate,
        grad_w_up,
        grad_w_down,
    )


def solution(mesh):
    placed = (
        P(("dp", "blk"), None),
        P("dp", None),
        P(),
        P(None, "tensor"),
        P("tensor"),
        P(None, "tensor"),
        P("tensor"),
        P(None, "tensor"),
        P("tensor"),
        P("tensor", None),
        P(),
        P(None, "tensor"),
        P(None, "tensor"),
        P("tensor", None),
        P(("dp", "blk"), None),
    )
    return jax.shard_map(
        local,
        mesh=mesh,
        in_specs=placed,
        out_specs=(
            P(("dp", "blk"), None),
            P(("dp", "blk"), None),
            P(),
            P(None, "tensor"),
            P("tensor"),
            P(None, "tensor"),
            P("tensor"),
            P(None, "tensor"),
            P("tensor"),
            P("tensor", None),
            P(),
            P(None, "tensor"),
            P(None, "tensor"),
            P("tensor", None),
        ),
        check_vma=False,
    )
```

```python
import functools
import math

import jax
import jax.numpy as jnp
from jax import lax
from jax.experimental import pallas as pl
from jax.experimental.pallas import tpu as pltpu
from jax.sharding import PartitionSpec as P

HEAD_DIM = 64

epsilon = 1e-06
rope_base = 1000000.0
masked_value = -1e30

low = jnp.bfloat16
wide = jnp.float32
vmem_limit = 50 * 1024 * 1024


def dot_nn(left, right):
    return lax.dot_general(left, right, (((1,), (0,)), ((), ())), preferred_element_type=wide)


def dot_nt(left, right):
    return lax.dot_general(left, right, (((1,), (1,)), ((), ())), preferred_element_type=wide)


def dot_tn(left, right):
    return lax.dot_general(left, right, (((0,), (0,)), ((), ())), preferred_element_type=wide)


def partner(value, axis, step, name):
    count = lax.axis_size(axis)
    with jax.named_scope(name):
        return lax.ppermute(value, axis, [(i, i ^ step) for i in range(count)])


def gather_blocks(piece, name):
    count = lax.axis_size("blk")
    return [piece] + [partner(piece, "blk", r, name) for r in range(1, count)]


def relay_far(near, own, name):
    count = lax.axis_size("blk")
    rows = own.shape[0]
    halved = rows % 32 == 0
    cuts = [slice(0, rows // 2), slice(rows // 2, rows)] if halved else [slice(0, rows)]
    pieces = {}
    for r in range(1, count):
        if r in near:
            pieces[r] = [near[r]]
            continue
        low_bit = r & -r
        high_bit = 1 << (r.bit_length() - 1)
        pieces[r] = []
        for i, (bit, rows_cut) in enumerate(zip((high_bit, low_bit), cuts)):
            source = pieces[r ^ bit]
            part = source[i] if len(source) > 1 else source[0][rows_cut]
            pieces[r].append(partner(part, "blk", bit, name + "_relay"))
    return pieces


def gather_relayed(piece, name):
    count = lax.axis_size("blk")
    near = {r: partner(piece, "blk", r, name) for r in range(1, count) if r & (r - 1) == 0}
    pieces = relay_far(near, piece, name)
    return [[piece]] + [pieces[r] for r in range(1, count)]


def scatter_blocks(pieces, name):
    return [pieces[0]] + [partner(pieces[r], "blk", r, name) for r in range(1, len(pieces))]


def hop(value, stage, name):
    routes = ([(0, 1), (3, 2)], [(1, 2), (2, 1)], [(1, 0), (2, 3)])
    with jax.named_scope(f"{name}_hop{stage}"):
        return lax.ppermute(value, "dp", routes[stage])


def call(body, outs, ins, scratch=(), in_specs=None, after=(), carry=()):
    whole = pl.BlockSpec(memory_space=pltpu.VMEM)
    anywhere = pl.BlockSpec(memory_space=pl.ANY)
    in_specs = list(in_specs or [whole] * len(ins))
    given, waited, made = len(ins), len(after) + len(carry), len(outs)

    def run(*refs):
        results = given + waited
        body(*refs[:given], *refs[results : results + made], *refs[results + made + len(carry) :])

    return pl.pallas_call(
        run,
        name=getattr(body, "func", body).__name__,
        out_shape=tuple(outs) + tuple(shape(value.shape, value.dtype) for value in carry),
        in_specs=in_specs + [anywhere] * waited,
        out_specs=tuple([whole] * made + [anywhere] * len(carry)),
        scratch_shapes=list(scratch),
        input_output_aliases={given + len(after) + i: made + i for i in range(len(carry))},
        cost_estimate=pl.CostEstimate(flops=0, bytes_accessed=0, transcendentals=0),
        compiler_params=pltpu.CompilerParams(vmem_limit_bytes=vmem_limit),
    )(*ins, *after, *carry)


def shape(dims, kind):
    return jax.ShapeDtypeStruct(dims, kind)


in_smem = pl.BlockSpec(memory_space=pltpu.SMEM)
in_vmem = pl.BlockSpec(memory_space=pltpu.VMEM)


def as_row(column):
    return jnp.broadcast_to(column, (column.shape[0], 128)).T[:1]


def as_column(row):
    width = row.shape[1]
    padded = -(-width // 128) * 128
    row = row.astype(wide)
    if padded != width:
        row = jnp.concatenate([row, jnp.zeros((1, padded - width), wide)], axis=1)
    return jnp.broadcast_to(row, (128, padded)).T[:width, :1]


def segment_start(lengths_ref, rows):
    start = jnp.zeros_like(rows)
    end = jnp.int32(0)
    for i in range(lengths_ref.shape[1]):
        end = end + lengths_ref[0, i]
        start = jnp.where(rows >= end, end, start)
    return start


def rotate(pair, cosine, sine):
    half = HEAD_DIM // 2
    first, second = pair[:half], pair[half:]
    return jnp.concatenate(
        [first * cosine - second * sine, second * cosine + first * sine], axis=0
    )


def enter_kernel(
    lengths_ref, place_ref, tokens_ref, gain_ref, wq_ref, wk_ref, wv_ref, bq_ref, bk_ref, bv_ref,
    turn_ref, q_ref, kv_ref, normed_ref, tokens_t_ref, cos_ref, sin_ref,
):
    rows = tokens_ref.shape[0]
    hidden = tokens_ref[...].astype(wide)
    inverse = lax.rsqrt(jnp.mean(hidden * hidden, axis=1, keepdims=True) + epsilon)
    normed = (hidden * inverse * gain_ref[...].astype(wide)).astype(low)
    tokens_t_ref[...] = hidden.T.astype(low)
    normed_ref[...] = normed.astype(wide).T.astype(low)
    index = place_ref[0] * rows + lax.broadcasted_iota(jnp.int32, (1, rows), 1)
    position = (index - segment_start(lengths_ref, index)).astype(wide)
    angles = turn_ref[...] * position
    cosine, sine = jnp.cos(angles), jnp.sin(angles)
    cos_ref[...] = cosine
    sin_ref[...] = sine
    q_lin = dot_nt(wq_ref[...], normed) + as_column(bq_ref[...])
    for h in range(q_lin.shape[0] // HEAD_DIM):
        head = rotate(q_lin[h * HEAD_DIM : (h + 1) * HEAD_DIM], cosine, sine)
        q_ref[h * HEAD_DIM : (h + 1) * HEAD_DIM, :] = head.astype(low) * low(HEAD_DIM**-0.5)
    k_lin = dot_nt(wk_ref[...], normed) + as_column(bk_ref[...])
    v_lin = dot_nt(wv_ref[...], normed) + as_column(bv_ref[...])
    kv_ref[...] = jnp.concatenate([rotate(k_lin, cosine, sine), v_lin], axis=0).T.astype(low)


def weights_kernel(
    lengths_ref, place_ref, gate_ref, up_ref, down_ref, cotangent_ref,
    gate_t_ref, gate_own_ref, up_t_ref, up_own_ref, down_t_ref, mine_ref, other_ref, turned_ref, grad_ref,
):
    units = gate_t_ref.shape[0]
    width, hidden = gate_ref.shape
    window = turned_ref.shape[0]
    first = place_ref[0] * units
    base = pl.multiple_of(jnp.minimum(first // 128 * 128, hidden - window), 128)
    for ref, turned, own in ((gate_ref, gate_t_ref, gate_own_ref), (up_ref, up_t_ref, up_own_ref)):
        turned_ref[...] = ref[:, pl.ds(base, window)].astype(wide).T
        part = turned_ref[pl.ds(pl.multiple_of(first - base, 8), units), :]
        turned[...] = part.astype(low)
        own[...] = part.T.astype(low)
    down_t_ref[...] = down_ref[...].astype(wide).T.astype(low)
    rows = cotangent_ref.shape[0]
    half = rows // 2
    row = place_ref[0] * rows + lax.broadcasted_iota(jnp.int32, (rows, 1), 0)
    end = jnp.int32(0)
    for i in range(lengths_ref.shape[1]):
        end = end + lengths_ref[0, i]
    grad_ref[...] = jnp.where(row < end, cotangent_ref[...].astype(wide), 0.0)
    core = place_ref[1]
    mine_ref[...] = grad_ref[pl.ds(pl.multiple_of(core * half, half), half), :].astype(low)
    other_ref[...] = grad_ref[pl.ds(pl.multiple_of((1 - core) * half, half), half), :].astype(low)


def mask_bias(key_base, key_rows, q_index, q_start):
    keys = key_base + lax.broadcasted_iota(jnp.int32, (key_rows, q_index.shape[1]), 0)
    return jnp.where((keys >= q_start) & (keys <= q_index), 0.0, masked_value)


def first_row(lengths_ref, row):
    start = jnp.int32(0)
    end = jnp.int32(0)
    for i in range(lengths_ref.shape[1]):
        end = end + lengths_ref[0, i]
        start = jnp.where(row >= end, end, start)
    return start


def attend_kernel(blocks, lengths_ref, place_ref, q_ref, w_out_ref, *refs):
    kv_refs = refs[:blocks]
    out_ref, log_ref, mine_ref, other_ref, kv_ref, acc_ref, max_ref, bias_ref, part_ref = refs[blocks:]
    rows = q_ref.shape[1]
    heads = q_ref.shape[0] // HEAD_DIM
    own, core = place_ref[0], place_ref[1]
    for r in range(blocks):
        kv_ref[r] = kv_refs[r][...]
    q_index = own * rows + lax.broadcasted_iota(jnp.int32, (1, rows), 1)
    q_start = segment_start(lengths_ref, q_index)
    acc_ref[...] = jnp.zeros_like(acc_ref)
    max_ref[...] = jnp.full_like(max_ref, masked_value)

    def visit(block, carry):
        pair = kv_ref[block ^ own]
        keys = pair[:, :HEAD_DIM]
        values = pair.astype(wide).T[HEAD_DIM:].astype(low)
        values = jnp.concatenate([values, jnp.ones((16, rows), low)], axis=0)
        bias_ref[...] = mask_bias(block * rows, rows, q_index, q_start)
        for h in range(heads):
            scores = dot_nn(keys, q_ref[h * HEAD_DIM : (h + 1) * HEAD_DIM, :]) + bias_ref[...]
            old = max_ref[h : h + 1, :]
            new = jnp.maximum(old, jnp.max(scores, axis=0, keepdims=True))
            weight = jnp.exp(scores - new).astype(low)
            acc_ref[h] = acc_ref[h] * jnp.exp(old - new) + dot_nn(values, weight)
            max_ref[h : h + 1, :] = new
        return carry

    lax.fori_loop(first_row(lengths_ref, own * rows) // rows, own + 1, visit, 0)
    for h in range(heads):
        total = acc_ref[h, HEAD_DIM : HEAD_DIM + 1, :]
        out_ref[h * HEAD_DIM : (h + 1) * HEAD_DIM, :] = acc_ref[h, :HEAD_DIM, :] / total
        log_ref[h : h + 1, :] = max_ref[h : h + 1, :] + jnp.log(total)
    part_ref[...] = dot_tn(w_out_ref[...], out_ref[...].astype(low))
    half = mine_ref.shape[1]
    mine_ref[...] = part_ref[:, pl.ds(pl.multiple_of(core * half, half), half)]
    other_ref[...] = part_ref[:, pl.ds(pl.multiple_of((1 - core) * half, half), half)].astype(low)


def middle_kernel(place_ref, tokens_ref, part_ref, passed_ref, gain_ref, hidden_ref, normed_ref):
    half = hidden_ref.shape[1]
    mine = pl.ds(pl.multiple_of(place_ref[1] * half, half), half)
    hidden = tokens_ref[:, mine].astype(wide) + part_ref[...] + passed_ref[...].astype(wide)
    hidden_ref[...] = hidden
    inverse = lax.rsqrt(jnp.mean(hidden * hidden, axis=0, keepdims=True) + epsilon)
    normed_ref[...] = (hidden * inverse * as_column(gain_ref[...])).astype(low)


def hidden_kernel(parts, *refs):
    gy_refs, x_refs, refs = refs[: 2 * parts], refs[2 * parts : 4 * parts], refs[4 * parts :]
    gate_t_ref, up_t_ref, down_ref, gate_ref, up_ref = refs[:5]
    x_ref, gy_ref, mixed_ref, grad_gate_ref, grad_up_ref, other_ref, mine_ref = refs[5:]
    half = other_ref.shape[1]
    for k in range(2):
        at = 0
        for part in x_refs[k * parts : (k + 1) * parts]:
            x_ref[at : at + part.shape[0], k * half : (k + 1) * half] = part[...]
            at += part.shape[0]
    at = 0
    for part in gy_refs:
        gy_ref[at : at + part.shape[0], :] = part[...]
        at += part.shape[0]
    x = x_ref[...]
    gate = dot_nn(gate_t_ref[...], x)
    up = dot_nn(up_t_ref[...], x)
    grad_mixed = dot_nt(down_ref[...], gy_ref[...])
    sigmoid = 1.0 / (1.0 + jnp.exp(-gate))
    silu = gate * sigmoid
    mixed_ref[...] = (silu * up).astype(low)
    grad_gate = (grad_mixed * up * sigmoid * (1.0 + gate * (1.0 - sigmoid))).astype(low)
    grad_up = (grad_mixed * silu).astype(low)
    grad_gate_ref[...] = grad_gate
    grad_up_ref[...] = grad_up
    back = (dot_nn(gate_ref[...], grad_gate) + dot_nn(up_ref[...], grad_up)).astype(low)
    other_ref[...] = back[:, :half]
    mine_ref[...] = back[:, half:]


def weight_kernel(transposed, *refs):
    pairs, out_refs = refs[:-2], refs[-2:]
    at = 0
    for out_ref in out_refs:
        rows, columns = out_ref.shape
        tile = rows // 2 if rows % 32 == 0 else rows
        cols = slice(at, at + columns)
        for t in range(0, rows, tile):
            span = slice(t, t + tile)
            total = None
            for i in range(0, len(pairs), 2):
                left = pairs[i][span, :]
                part = dot_nt(left, pairs[i + 1][cols, :]) if transposed else dot_nn(left, pairs[i + 1][:, cols])
                total = part if total is None else total + part
            out_ref[span, :] = total.astype(low)
        at += columns


def wait_kernel(*refs):
    pass


def step_kernel(adds, place_ref, *refs):
    count = len(refs) // 3
    end = (place_ref[2] == 0) | (place_ref[2] == 3)
    for i in range(count):
        left, right, out_ref = refs[2 * i], refs[2 * i + 1], refs[2 * count + i]
        if i < adds:
            out_ref[...] = (left[...].astype(wide) + right[...].astype(wide)).astype(low)
        else:
            out_ref[...] = jnp.where(end, left[...], right[...])


def project_kernel(blocks, weight_ref, *refs):
    other_ref, mine_refs = refs[blocks], refs[blocks + 1 :]
    half = other_ref.shape[2]
    for r in range(blocks):
        part = dot_nn(weight_ref[...], refs[r][...]).astype(low)
        other_ref[r] = part[:, :half]
        mine_refs[r][...] = part[:, half:]


def add_kernel(*refs):
    count = (len(refs) - 1) // 2
    for i in range(count):
        own = refs[1 + i][...] if len(refs[1 + i].shape) == 2 else refs[1 + i][0]
        refs[1 + count + i][...] = (own.astype(wide) + refs[0][i].astype(wide)).astype(low)


def pair_kernel(*refs):
    count = len(refs) // 3
    for i in range(count):
        refs[2 * count + i][...] = (refs[2 * i][...].astype(wide) + refs[2 * i + 1][...].astype(wide)).astype(low)


def sum_blocks(refs):
    total = refs[0][...].astype(wide)
    for ref in refs[1:]:
        total = total + ref[...].astype(wide)
    return total


def layer_kernel(hidden_ref, *refs):
    out_ref = refs[-1]
    out_ref[...] = (hidden_ref[...] + sum_blocks(refs[:-1])).T.astype(low)


def grad_middle_kernel(hidden_ref, gain_ref, gy_ref, *refs):
    grad_ref, grad_low_ref, grad_gain_ref = refs[-3:]
    hidden = hidden_ref[...]
    inverse = lax.rsqrt(jnp.mean(hidden * hidden, axis=0, keepdims=True) + epsilon)
    grad_normed = sum_blocks(refs[:-3])
    weighted = as_column(gain_ref[...]) * grad_normed
    inner = jnp.mean(weighted * hidden, axis=0, keepdims=True)
    grad = inverse * weighted - hidden * (inverse * inverse * inverse * inner)
    grad = grad + gy_ref[...].astype(wide).T
    grad_ref[...] = grad
    grad_low_ref[...] = grad.astype(low)
    grad_gain_ref[...] = as_row(jnp.sum(grad_normed * hidden * inverse, axis=1, keepdims=True))


def back_enter_kernel(
    place_ref, gm_mine_ref, gm_other_ref, w_out_ref, out_ref, go_ref, delta_ref, gm_ref
):
    half = gm_mine_ref.shape[1]
    core = place_ref[1]
    gm_ref[:, pl.ds(pl.multiple_of(core * half, half), half)] = gm_mine_ref[...]
    gm_ref[:, pl.ds(pl.multiple_of((1 - core) * half, half), half)] = gm_other_ref[...]
    grad_out = dot_nn(w_out_ref[...], gm_ref[...]).astype(low)
    go_ref[...] = grad_out
    product = grad_out.astype(wide) * out_ref[...]
    for h in range(product.shape[0] // HEAD_DIM):
        delta_ref[h : h + 1, :] = jnp.sum(
            product[h * HEAD_DIM : (h + 1) * HEAD_DIM], axis=0, keepdims=True
        )


def attend_back_kernel(
    blocks, first_head, earlier, lengths_ref, place_ref, go_ref, delta_ref, log_ref, q_ref, cos_ref, sin_ref, *refs,
):
    kv_refs, refs = refs[:blocks], refs[blocks:]
    if earlier:
        earlier_refs, refs = refs[:blocks], refs[blocks:]
    (grad_q_ref, *grad_kv_refs), refs = refs[: blocks + 1], refs[blocks + 1 :]
    kv_ref, bias_ref, dq_ref, dk_ref, dv_ref, grad_kv_ref = refs
    rows = q_ref.shape[1]
    heads = grad_q_ref.shape[0] // HEAD_DIM
    own = place_ref[0]
    for r in range(blocks):
        kv_ref[r] = kv_refs[r][...]
        if earlier:
            grad_kv_ref[r] = earlier_refs[r][...].astype(wide)
        else:
            grad_kv_ref[r] = jnp.zeros_like(grad_kv_ref[r])
    dq_ref[...] = jnp.zeros_like(dq_ref)
    q_index = own * rows + lax.broadcasted_iota(jnp.int32, (1, rows), 1)
    q_start = segment_start(lengths_ref, q_index)

    def visit(block, carry):
        pair = kv_ref[block ^ own]
        keys = pair[:, :HEAD_DIM]
        values = pair[:, HEAD_DIM:]
        keys_t = pair.astype(wide).T[:HEAD_DIM].astype(low)
        bias_ref[...] = mask_bias(block * rows, rows, q_index, q_start)
        for i in range(heads):
            h = first_head + i
            span = slice(h * HEAD_DIM, (h + 1) * HEAD_DIM)
            scores = dot_nn(keys, q_ref[span, :]) + bias_ref[...]
            weight = jnp.exp(scores - log_ref[h : h + 1, :])
            grad_weight = dot_nn(values, go_ref[span, :])
            grad_scores = (weight * (grad_weight - delta_ref[h : h + 1, :])).astype(low)
            dq_ref[i * HEAD_DIM : (i + 1) * HEAD_DIM, :] += dot_nn(keys_t, grad_scores)
            dk = dot_nt(grad_scores, q_ref[span, :])
            dv = dot_nt(weight.astype(low), go_ref[span, :])
            if i == 0:
                dk_ref[...] = dk
                dv_ref[...] = dv
            else:
                dk_ref[...] += dk
                dv_ref[...] += dv
        grad_kv_ref[block ^ own] += jnp.concatenate([dk_ref[...], dv_ref[...]], axis=1)
        return carry

    lax.fori_loop(first_row(lengths_ref, own * rows) // rows, own + 1, visit, 0)
    for r in range(blocks):
        grad_kv_refs[r][...] = grad_kv_ref[r].astype(grad_kv_refs[r].dtype)
    for i in range(heads):
        span = slice(i * HEAD_DIM, (i + 1) * HEAD_DIM)
        turned = rotate(dq_ref[span, :] * HEAD_DIM**-0.5, cos_ref[...], -sin_ref[...])
        grad_q_ref[span, :] = turned.astype(low)


def query_kernel(
    place_ref, normed_ref, grad_q_a_ref, grad_q_b_ref, wq_ref, gm_mine_ref, gm_other_ref, out_ref,
    grad_wq_ref, part_ref, grad_bq_ref, grad_w_out_ref, gm_ref,
):
    half = gm_mine_ref.shape[1]
    core = place_ref[1]
    gm_ref[:, pl.ds(pl.multiple_of(core * half, half), half)] = gm_mine_ref[...]
    gm_ref[:, pl.ds(pl.multiple_of((1 - core) * half, half), half)] = gm_other_ref[...]
    grad_w_out_ref[...] = dot_nt(out_ref[...].astype(low), gm_ref[...]).astype(low)
    grad_q = jnp.concatenate([grad_q_a_ref[...], grad_q_b_ref[...]], axis=0)
    grad_wq_ref[...] = dot_nt(grad_q, normed_ref[...]).astype(low)
    part_ref[...] = dot_tn(wq_ref[...], grad_q)
    grad_bq_ref[...] = dot_nt(jnp.ones((16, grad_q.shape[1]), low), grad_q)


def key_kernel(
    blocks, place_ref, normed_ref, tokens_ref, part_ref, wk_ref, wv_ref, cos_ref, sin_ref,
    grad_wq_ref, grad_bq_ref, grad_w_out_ref, grad_gain_two_ref, *refs,
):
    kv_refs, share_refs, (mine_ref, other_ref, sum_ref, pack_ref) = refs[:blocks], refs[blocks : 2 * blocks], refs[2 * blocks :]
    both = sum_blocks(kv_refs).T
    both = jnp.concatenate(
        [rotate(both[:HEAD_DIM], cos_ref[...], -sin_ref[...]), both[HEAD_DIM:]], axis=0
    ).astype(low)
    total = part_ref[...] + dot_tn(wk_ref[...], both[:HEAD_DIM]) + dot_tn(wv_ref[...], both[HEAD_DIM:])
    sum_ref[...] = total
    half = mine_ref.shape[1]
    core = place_ref[1]
    mine_ref[...] = sum_ref[:, pl.ds(pl.multiple_of(core * half, half), half)]
    other_ref[...] = sum_ref[:, pl.ds(pl.multiple_of((1 - core) * half, half), half)].astype(low)
    hidden = tokens_ref[...].astype(wide)
    inverse = lax.rsqrt(jnp.mean(hidden * hidden, axis=0, keepdims=True) + epsilon)
    q_width, width = grad_wq_ref.shape
    kv_width = both.shape[0]
    at = 0
    pack_ref[at : at + q_width, :] = grad_wq_ref[...]
    at += q_width
    pack_ref[at : at + kv_width, :] = dot_nt(both, normed_ref[...]).astype(low)
    at += kv_width
    pack_ref[at : at + q_width, :] = grad_w_out_ref[...]
    at += q_width
    grad_gain = as_row(jnp.sum(total * (hidden * inverse), axis=1, keepdims=True))
    grad_bkv = dot_nt(jnp.ones((16, both.shape[1]), low), both)[:1]
    biases = jnp.concatenate(
        [grad_bq_ref[:1, :], grad_bkv, jnp.zeros((1, width - q_width - kv_width), wide)], axis=1
    )
    small = jnp.concatenate(
        [grad_gain, grad_gain_two_ref[...], biases, jnp.zeros((pack_ref.shape[0] - at - 3, width), wide)], axis=0
    )
    pack_ref[at:, :] = small.astype(low)
    share = pack_ref.shape[0] // blocks
    for r in range(blocks):
        start = pl.multiple_of((place_ref[0] ^ r) * share, share)
        share_refs[r][...] = pack_ref[pl.ds(start, share), :]


def share_kernel(*refs):
    refs[-1][...] = sum_blocks(refs[:-1]).astype(low)


def unpack_kernel(counts, place_ref, *refs):
    total = sum(counts)
    pieces, outs, pack_ref = refs[:total], refs[total:-1], refs[-1]
    share = pack_ref.shape[0] // len(counts)
    at = 0
    for r, count in enumerate(counts):
        start = (place_ref[0] ^ r) * share
        for ref in pieces[at : at + count]:
            pack_ref[pl.ds(pl.multiple_of(start, 8), ref.shape[0]), :] = ref[...].astype(wide)
            start = start + ref.shape[0]
        at += count
    at = 0
    for out_ref in outs:
        out_ref[...] = pack_ref[at : at + out_ref.shape[0], :]
        at += out_ref.shape[0]


def leave_kernel(place_ref, tokens_ref, mine_ref, passed_ref, gain_ref, grad_mid_ref, out_ref):
    half = mine_ref.shape[1]
    hidden = tokens_ref[:, pl.ds(pl.multiple_of(place_ref[1] * half, half), half)].astype(wide)
    inverse = lax.rsqrt(jnp.mean(hidden * hidden, axis=0, keepdims=True) + epsilon)
    weighted = as_column(gain_ref[...]) * (mine_ref[...] + passed_ref[...].astype(wide))
    inner = jnp.mean(weighted * hidden, axis=0, keepdims=True)
    grad = grad_mid_ref[...] + inverse * weighted - hidden * (inverse * inverse * inverse * inner)
    out_ref[...] = grad.T.astype(low)


def put_pieces(counts, place_ref, refs, all_ref):
    rows = all_ref.shape[0] // len(counts)
    at = 0
    for r, count in enumerate(counts):
        start = (place_ref[0] ^ r) * rows
        for ref in refs[at : at + count]:
            all_ref[pl.ds(pl.multiple_of(start, 8), ref.shape[0]), :] = ref[...].astype(wide)
            start = start + ref.shape[0]
        at += count


def rows_kernel(counts, place_ref, *refs):
    put_pieces(counts, place_ref, refs[:-1], refs[-1])


def columns_kernel(counts, place_ref, *refs):
    put_pieces(counts, place_ref, refs[:-2], refs[-1])
    refs[-2][...] = refs[-1][...].T


def place_share(place, share, transposed, width, at, whole, last):
    tile = 128
    counts = [len(parts) for parts in share]
    pieces = sum(share, [])
    whole_rows = sum(p.shape[0] for p in pieces)
    first = at // tile
    total = len(pieces)
    ins = [place] + pieces + last
    specs = (
        [in_smem]
        + [pl.BlockSpec((p.shape[0], tile), lambda i: (0, i)) for p in pieces]
        + [pl.BlockSpec(memory_space=pl.ANY)] * len(last)
    )
    aliases = {}
    if whole is not None:
        aliases = {len(ins): 0}
        ins.append(whole)
        specs.append(pl.BlockSpec(memory_space=pl.ANY))
    kernel = columns_kernel if transposed else rows_kernel

    def body(*refs):
        kernel(counts, *refs[: total + 1], *refs[len(ins) :])

    if transposed:
        dims = (width, whole_rows)
        out_spec = pl.BlockSpec((tile, whole_rows), lambda i: (i + first, 0))
        scratch = [pltpu.VMEM((whole_rows, tile), wide)]
    else:
        dims = (whole_rows, width)
        out_spec = pl.BlockSpec((whole_rows, tile), lambda i: (0, i + first))
        scratch = []
    return pl.pallas_call(
        body,
        name=kernel.__name__,
        out_shape=shape(dims, wide),
        grid=(pieces[0].shape[1] // tile,),
        in_specs=specs,
        out_specs=out_spec,
        scratch_shapes=scratch,
        input_output_aliases=aliases,
        cost_estimate=pl.CostEstimate(flops=0, bytes_accessed=0, transcendentals=0),
        compiler_params=pltpu.CompilerParams(vmem_limit_bytes=vmem_limit),
    )(*ins)


def local(
    tokens,
    lengths,
    norm1_gain,
    w_query,
    b_query,
    w_key,
    b_key,
    w_value,
    b_value,
    w_out,
    norm2_gain,
    w_gate,
    w_up,
    w_down,
    cotangent,
):
    rows, width = tokens.shape
    half = rows // 2
    blocks = lax.axis_size("blk")
    own_block = lax.axis_index("blk")
    own_core = lax.axis_index("tensor")
    q_width = w_query.shape[1]
    heads = q_width // HEAD_DIM
    units = w_gate.shape[1] // blocks
    place = jnp.stack([own_block, own_core, lax.axis_index("dp")]).astype(jnp.int32)
    gain_two = norm2_gain.reshape(1, width)

    def whole_rows(mine):
        other = partner(mine, "tensor", 1, "rows_core")
        return jnp.where(
            own_core == 0,
            jnp.concatenate([mine, other], axis=0),
            jnp.concatenate([other, mine], axis=0),
        )

    half_dim = HEAD_DIM // 2
    turn = (rope_base ** (-2.0 * jnp.arange(half_dim, dtype=wide) / HEAD_DIM)).reshape(half_dim, 1)
    q_t, key_value, normed_t, tokens_t, cosine, sine = call(
        enter_kernel,
        [
            shape((q_width, rows), low),
            shape((rows, 2 * HEAD_DIM), low),
            shape((width, rows), low),
            shape((width, rows), low),
            shape((half_dim, rows), wide),
            shape((half_dim, rows), wide),
        ],
        [
            lengths, place, tokens, norm1_gain.reshape(1, width), w_query.T, w_key.T, w_value.T,
            b_query.reshape(1, -1), b_key.reshape(1, -1), b_value.reshape(1, -1), turn,
        ],
        in_specs=[in_smem] * 2 + [in_vmem] * 9,
    )
    kv_blocks = gather_blocks(key_value, "kv")

    down_own = lax.dynamic_slice_in_dim(w_down, own_block * units, units, 0)
    window = -(-(units + 127) // 128) * 128
    gate_t, gate_own, up_t, up_own, down_t, grad_y_mine, grad_y_other = call(
        weights_kernel,
        [
            shape((units, width), low),
            shape((width, units), low),
            shape((units, width), low),
            shape((width, units), low),
            shape((width, units), low),
            shape((half, width), low),
            shape((half, width), low),
        ],
        [lengths, place, w_gate, w_up, down_own, cotangent],
        [pltpu.VMEM((window, width), wide), pltpu.VMEM((rows, width), wide)],
        in_specs=[in_smem] * 2 + [in_vmem] * 4,
        after=[q_t],
    )
    gy_near = {r: partner(grad_y_mine, "blk", r, "gy") for r in range(1, blocks) if r & (r - 1) == 0}

    out_t, log_total, part_mine, part_other = call(
        functools.partial(attend_kernel, blocks),
        [
            shape((q_width, rows), wide),
            shape((heads + 1, rows), wide),
            shape((width, half), wide),
            shape((width, half), low),
        ],
        [lengths, place, q_t, w_out] + kv_blocks,
        [
            pltpu.VMEM((blocks, rows, 2 * HEAD_DIM), low),
            pltpu.VMEM((heads, HEAD_DIM + 16, rows), wide),
            pltpu.VMEM((heads + 1, rows), wide),
            pltpu.VMEM((rows, rows), wide),
            pltpu.VMEM((width, rows), wide),
        ],
        in_specs=[in_smem] * 2 + [in_vmem] * (2 + blocks),
        after=[gate_t],
    )
    hidden, normed_two = call(
        middle_kernel,
        [shape((width, half), wide), shape((width, half), low)],
        [place, tokens_t, part_mine, partner(part_other, "tensor", 1, "part_core"), gain_two],
        in_specs=[in_smem] + [in_vmem] * 4,
        after=list(gy_near.values()),
    )

    last = [normed_two]

    def ordered(body, outs, ins, needs=(), **more):
        nonlocal last
        carry = more.get("carry", ())
        after = [v for v in last + list(needs) if not any(v is c for c in carry)]
        results = call(body, outs, ins, after=after, **more)
        last = [results[0]]
        return results

    def wait(carry, needs=()):
        return list(ordered(wait_kernel, [], [], needs=needs, carry=carry))

    def near(pieces):
        return [p for r, parts in enumerate(pieces) if r and r & (r - 1) == 0 for p in parts]

    def far(pieces):
        return [p for r, parts in enumerate(pieces) if r & (r - 1) for p in parts]

    kept = shape((units, rows), low)
    piece = shape((width, half), low)
    runs, back, passed = [], [None] * blocks, [None] * blocks

    def cores(parts, name):
        return [partner(part, "tensor", 1, name) for part in parts]

    def hidden_units(r, x_mine, x_other, gy_mine, gy_other):
        runs.append(
            ordered(
                functools.partial(hidden_kernel, len(x_mine)),
                [shape((width, rows), low), shape((rows, width), low), kept, kept, kept, piece, piece],
                gy_other + gy_mine + x_other + x_mine + [gate_t, up_t, down_own, gate_own, up_own],
            )
        )
        return runs[-1][5]

    def add_back(members, carry, needs=()):
        results = ordered(
            pair_kernel,
            [piece] * len(members),
            [value for r in members for value in (runs[r][6], passed[r])],
            needs=needs,
            carry=carry,
        )
        for r, value in zip(members, results):
            back[r] = partner(value, "blk", r, "back") if r else value
        return results[len(members) :]

    def hidden_weight(transposed, left, right, cuts):
        return ordered(
            functools.partial(weight_kernel, transposed),
            [shape((units, columns), low) for columns in cuts],
            [run[k] for run in runs for k in (left, right)],
        )

    def step(adds, takes, needs=(), carry=()):
        pairs = list(adds) + list(takes)
        return ordered(
            functools.partial(step_kernel, len(adds)),
            [shape(pair[0].shape, low) for pair in pairs],
            [place] + [value for pair in pairs for value in pair],
            in_specs=[in_smem] + [in_vmem] * (2 * len(pairs)),
            needs=needs,
            carry=carry,
        )

    x_near = {r: partner(normed_two, "blk", r, "x") for r in range(1, blocks) if r & (r - 1) == 0}
    other = hidden_units(
        0, [normed_two], cores([normed_two], "x_core"), [grad_y_mine], [grad_y_other]
    )
    other, *arrived = wait([other] + list(x_near.values()))
    passed[0] = partner(other, "tensor", 1, "back_core")
    x_near = dict(zip(x_near, arrived))
    x_mine = relay_far(x_near, normed_two, "x")
    gy_mine = relay_far(gy_near, grad_y_mine, "gy")
    x_other = {r: cores(parts, "x_core") for r, parts in x_mine.items() if r in x_near}
    gy_other = {r: cores(parts, "gy_core") for r, parts in gy_mine.items() if r in x_near}
    waiting, out_of = [], list(range(1, blocks))
    for i, r in enumerate(out_of):
        other = hidden_units(r, x_mine[r], x_other[r], gy_mine[r], gy_other[r])
        ready = [k for k in out_of if k not in x_near] if i == 0 else []
        fars = [part for k in ready for part in x_mine[k] + gy_mine[k]]
        if i == 0:
            other, *fars = wait([other] + fars)
        else:
            other, *fars = add_back([out_of[i - 1]], [other])
        passed[r] = partner(other, "tensor", 1, "back_core")
        for k in ready:
            count = len(x_mine[k])
            x_mine[k], fars = fars[:count], fars[count:]
            count = len(gy_mine[k])
            gy_mine[k], fars = fars[:count], fars[count:]
            x_other[k] = cores(x_mine[k], "x_core")
            gy_other[k] = cores(gy_mine[k], "gy_core")
    d1, d2 = hidden_weight(False, 2, 1, [384, width - 384])
    layer_other, *layer_mine = ordered(
        functools.partial(project_kernel, blocks),
        [shape((blocks, width, half), low)] + [piece] * blocks,
        [down_t] + [run[2] for run in runs],
    )
    d1, d2, layer_other = add_back([blocks - 1, 0], [d1, d2, layer_other], needs=back[1 : blocks - 1])
    d1_in, d2_in = hop(d1, 0, "d1"), hop(d2, 0, "d2")
    layer_passed = partner(layer_other, "tensor", 1, "layer_core")
    g1, g2 = hidden_weight(True, 3, 0, [512, width - 512])
    u1, u2 = hidden_weight(True, 4, 0, [512, width - 512])
    (d1,) = step([(d1, d1_in)], [], needs=back[1:])
    grad_mid, grad_mid_low, grad_gain_two = ordered(
        grad_middle_kernel,
        [shape((width, half), wide), piece, shape((1, width), wide)],
        [hidden, gain_two, grad_y_mine] + back,
    )
    *layer_pieces, grad_mid_low, d1, g1 = ordered(
        add_kernel, [piece] * blocks, [layer_passed] + layer_mine, carry=[grad_mid_low, d1, g1]
    )
    grad_mid_other = partner(grad_mid_low, "tensor", 1, "mid_core")
    layer_pieces = scatter_blocks(layer_pieces, "layer")
    d1_in, g1_in = hop(d1, 1, "d1"), hop(g1, 0, "g1")

    grad_out, delta = ordered(
        back_enter_kernel,
        [shape((q_width, rows), low), shape((heads + 1, rows), wide)],
        [place, grad_mid_low, grad_mid_other, w_out, out_t],
        scratch=[pltpu.VMEM((width, rows), low)],
        in_specs=[in_smem] + [in_vmem] * 4,
    )

    def attend_back(first, count, earlier, kind):
        return ordered(
            functools.partial(attend_back_kernel, blocks, first, bool(earlier)),
            [shape((count * HEAD_DIM, rows), low)] + [shape((rows, 2 * HEAD_DIM), kind)] * blocks,
            [lengths, place, grad_out, delta, log_total, q_t, cosine, sine] + kv_blocks + earlier,
            scratch=[
                pltpu.VMEM((blocks, rows, 2 * HEAD_DIM), low),
                pltpu.VMEM((rows, rows), wide),
                pltpu.VMEM((count * HEAD_DIM, rows), wide),
                pltpu.VMEM((rows, HEAD_DIM), wide),
                pltpu.VMEM((rows, HEAD_DIM), wide),
                pltpu.VMEM((blocks, rows, 2 * HEAD_DIM), wide),
            ],
            in_specs=[in_smem] * 2 + [in_vmem] * (6 + blocks + len(earlier)),
        )

    early_heads = (heads + 1) // 2
    grad_q_a, *grad_kv = attend_back(0, early_heads, [], wide)
    d1, d2 = step([(d1, d1_in), (d2, d2_in)], [], needs=layer_pieces[1:])
    d1_in, d2_in = hop(d1, 2, "d1"), hop(d2, 1, "d2")
    grad_q_b, *grad_kv = attend_back(early_heads, heads - early_heads, grad_kv, low)
    d2, g1, d1, g2, *grad_kv = step(
        [(d2, d2_in), (g1, g1_in)], [(d1_in, d1)], carry=[g2] + grad_kv
    )
    d1_all = gather_relayed(d1, "all_d1")
    kv_pieces = scatter_blocks(grad_kv, "grad_kv")
    d2_in, g1_in, g2_in = hop(d2, 2, "d2"), hop(g1, 1, "g1"), hop(g2, 0, "g2")
    grad_w_query, normed_part, grad_b_query, grad_w_out = ordered(
        query_kernel,
        [
            shape((q_width, width), low),
            shape((width, rows), wide),
            shape((16, q_width), wide),
            shape((q_width, width), low),
        ],
        [place, normed_t, grad_q_a, grad_q_b, w_query.T, grad_mid_low, grad_mid_other, out_t],
        scratch=[pltpu.VMEM((width, rows), low)],
        in_specs=[in_smem] + [in_vmem] * 7,
    )
    (layer_half,) = ordered(layer_kernel, [shape((half, width), low)], [hidden] + layer_pieces)
    g1, g2, d2, layer_half, u1 = step(
        [(g1, g1_in), (g2, g2_in)], [(d2_in, d2)], needs=near(d1_all) + kv_pieces[1:], carry=[layer_half, u1]
    )
    d2_all = gather_relayed(d2, "all_d2")
    g1_in, g2_in, u1_in = hop(g1, 2, "g1"), hop(g2, 1, "g2"), hop(u1, 0, "u1")
    layer_out = whole_rows(layer_half)
    pack_rows = -(-(2 * q_width + 2 * HEAD_DIM + 3) // (16 * blocks)) * 16 * blocks
    share = pack_rows // blocks
    *shares, normed_mine, normed_other = ordered(
        functools.partial(key_kernel, blocks),
        [shape((share, width), low)] * blocks + [shape((width, half), wide), shape((width, half), low)],
        [
            place, normed_t, tokens_t, normed_part, w_key.T, w_value.T, cosine, sine,
            grad_w_query, grad_b_query, grad_w_out, grad_gain_two,
        ] + kv_pieces,
        scratch=[pltpu.VMEM((width, rows), wide), pltpu.VMEM((pack_rows, width), low)],
        in_specs=[in_smem] + [in_vmem] * (11 + blocks),
    )
    g2, u1, g1, u2, normed_other, *shares = step(
        [(g2, g2_in), (u1, u1_in)],
        [(g1_in, g1)],
        needs=far(d1_all) + near(d2_all),
        carry=[u2, normed_other] + shares,
    )
    g1_all = gather_relayed(g1, "all_g1")
    shares = scatter_blocks(shares, "shares")
    g2_in, u1_in, u2_in = hop(g2, 2, "g2"), hop(u1, 1, "u1"), hop(u2, 0, "u2")
    normed_passed = partner(normed_other, "tensor", 1, "normed_core")
    grad_w_down = place_share(place, d1_all, False, width, 0, None, last)
    last = [grad_w_down]
    (own_share,) = ordered(share_kernel, [shape((share, width), low)], shares)
    u1, u2, g2, own_share = step(
        [(u1, u1_in), (u2, u2_in)],
        [(g2_in, g2)],
        needs=far(d2_all) + near(g1_all),
        carry=[own_share],
    )
    g2_all = gather_relayed(g2, "all_g2")
    u1_in, u2_in, share_in = hop(u1, 2, "u1"), hop(u2, 1, "u2"), hop(own_share, 0, "share")
    (grad_half,) = ordered(
        leave_kernel,
        [shape((half, width), low)],
        [place, tokens_t, normed_mine, normed_passed, norm1_gain.reshape(1, width), grad_mid],
        in_specs=[in_smem] + [in_vmem] * 5,
    )
    grad_w_down = place_share(place, d2_all, False, width, d1.shape[1], grad_w_down, [grad_half])
    last = [grad_w_down]
    u2, own_share, u1, grad_half = step(
        [(u2, u2_in), (own_share, share_in)],
        [(u1_in, u1)],
        needs=far(g1_all) + near(g2_all),
        carry=[grad_half],
    )
    u1_all = gather_relayed(u1, "all_u1")
    u2_in, share_in = hop(u2, 2, "u2"), hop(own_share, 1, "share")
    grad_tokens = whole_rows(grad_half).astype(wide)
    grad_w_gate = place_share(place, g1_all, True, width, 0, None, last)
    last = [grad_w_gate]
    own_share, u2 = step(
        [(own_share, share_in)], [(u2_in, u2)], needs=far(g2_all) + near(u1_all)
    )
    u2_all = gather_relayed(u2, "all_u2")
    share_in = hop(own_share, 2, "share")
    grad_w_gate = place_share(place, g2_all, True, width, g1.shape[1], grad_w_gate, last)
    last = [grad_w_gate]
    (own_share,) = step([], [(share_in, own_share)], needs=far(u1_all) + near(u2_all))
    pieces = gather_relayed(own_share, "all_share")
    grad_w_up = place_share(place, u1_all, True, width, 0, None, last)
    last = [grad_w_up]
    grad_w_up = place_share(
        place, u2_all, True, width, u1.shape[1], grad_w_up, near(pieces)
    )

    counts = [len(parts) for parts in pieces]
    small_rows = pack_rows - 2 * q_width - 2 * HEAD_DIM
    grad_w_query, grad_w_key, grad_w_value, grad_w_out, small = call(
        functools.partial(unpack_kernel, counts),
        [
            shape((q_width, width), wide),
            shape((HEAD_DIM, width), wide),
            shape((HEAD_DIM, width), wide),
            shape((q_width, width), wide),
            shape((small_rows, width), wide),
        ],
        [place] + sum(pieces, []),
        [pltpu.VMEM((pack_rows, width), wide)],
        in_specs=[in_smem] + [in_vmem] * sum(counts),
    )
    gains = small[:2]
    gains = gains + partner(gains, "tensor", 1, "gains_core")
    grad_b = small[2]
    return (
        layer_out,
        grad_tokens,
        gains[0],
        grad_w_query.T,
        grad_b[:q_width],
        grad_w_key.T,
        grad_b[q_width : q_width + HEAD_DIM],
        grad_w_value.T,
        grad_b[q_width + HEAD_DIM : q_width + 2 * HEAD_DIM],
        grad_w_out,
        gains[1],
        grad_w_gate,
        grad_w_up,
        grad_w_down,
    )


def solution(mesh):
    placed = (
        P(("dp", "blk"), None),
        P("dp", None),
        P(),
        P(None, "tensor"),
        P("tensor"),
        P(None, "tensor"),
        P("tensor"),
        P(None, "tensor"),
        P("tensor"),
        P("tensor", None),
        P(),
        P(None, "tensor"),
        P(None, "tensor"),
        P("tensor", None),
        P(("dp", "blk"), None),
    )
    return jax.shard_map(
        local,
        mesh=mesh,
        in_specs=placed,
        out_specs=(
            P(("dp", "blk"), None),
            P(("dp", "blk"), None),
            P(),
            P(None, "tensor"),
            P("tensor"),
            P(None, "tensor"),
            P("tensor"),
            P(None, "tensor"),
            P("tensor"),
            P("tensor", None),
            P(),
            P(None, "tensor"),
            P(None, "tensor"),
            P("tensor", None),
        ),
        check_vma=False,
    )
```

```python
import functools
import math

import jax
import jax.numpy as jnp
from jax import lax
from jax.experimental import pallas as pl
from jax.experimental.pallas import tpu as pltpu
from jax.sharding import PartitionSpec as P

HEAD_DIM = 64

epsilon = 1e-06
rope_base = 1000000.0
masked_value = -1e30

low = jnp.bfloat16
wide = jnp.float32
vmem_limit = 40 * 1024 * 1024


def dot_nn(left, right):
    return lax.dot_general(left, right, (((1,), (0,)), ((), ())), preferred_element_type=wide)


def dot_nt(left, right):
    return lax.dot_general(left, right, (((1,), (1,)), ((), ())), preferred_element_type=wide)


def dot_tn(left, right):
    return lax.dot_general(left, right, (((0,), (0,)), ((), ())), preferred_element_type=wide)


def partner(value, axis, step, name):
    count = lax.axis_size(axis)
    with jax.named_scope(name):
        return lax.ppermute(value, axis, [(i, i ^ step) for i in range(count)])


def gather_blocks(piece, name):
    count = lax.axis_size("blk")
    return [piece] + [partner(piece, "blk", r, name) for r in range(1, count)]


def relay_far(near, own, name):
    count = lax.axis_size("blk")
    rows = own.shape[0]
    halved = rows % 32 == 0
    cuts = [slice(0, rows // 2), slice(rows // 2, rows)] if halved else [slice(0, rows)]
    pieces = {}
    for r in range(1, count):
        if r in near:
            pieces[r] = [near[r]]
            continue
        low_bit = r & -r
        high_bit = 1 << (r.bit_length() - 1)
        pieces[r] = []
        for i, (bit, rows_cut) in enumerate(zip((high_bit, low_bit), cuts)):
            source = pieces[r ^ bit]
            part = source[i] if len(source) > 1 else source[0][rows_cut]
            pieces[r].append(partner(part, "blk", bit, name + "_relay"))
    return pieces


def gather_relayed(piece, name):
    count = lax.axis_size("blk")
    near = {r: partner(piece, "blk", r, name) for r in range(1, count) if r & (r - 1) == 0}
    pieces = relay_far(near, piece, name)
    return [[piece]] + [pieces[r] for r in range(1, count)]


def scatter_blocks(pieces, name):
    return [pieces[0]] + [partner(pieces[r], "blk", r, name) for r in range(1, len(pieces))]


def swap(value, name):
    with jax.named_scope(name):
        return lax.ppermute(value, "dp", [(0, 1), (1, 0), (2, 3), (3, 2)])


def cross(value, name):
    with jax.named_scope(name):
        return lax.ppermute(value, "dp", [(1, 2), (2, 1)])


def call(body, outs, ins, scratch=(), in_specs=None, after=(), carry=(), moves=None):
    anywhere = pl.BlockSpec(memory_space=pl.ANY)
    whole = pl.BlockSpec(memory_space=pltpu.VMEM)
    in_specs = list(in_specs or [anywhere if moves else whole] * len(ins))
    given, waited, made = len(ins), len(after) + len(carry), len(outs)

    def run(*refs):
        results = given + waited
        body(*refs[:given], *refs[results : results + made], *refs[results + made + len(carry) :])

    return pl.pallas_call(
        run,
        name=getattr(body, "func", body).__name__,
        out_shape=tuple(outs) + tuple(shape(value.shape, value.dtype) for value in carry),
        in_specs=in_specs + [anywhere] * waited,
        out_specs=tuple([anywhere if moves == "all" else whole] * made + [anywhere] * len(carry)),
        scratch_shapes=list(scratch),
        input_output_aliases={given + len(after) + i: made + i for i in range(len(carry))},
        cost_estimate=pl.CostEstimate(flops=0, bytes_accessed=0, transcendentals=0),
        compiler_params=pltpu.CompilerParams(vmem_limit_bytes=vmem_limit),
    )(*ins, *after, *carry)


def shape(dims, kind):
    return jax.ShapeDtypeStruct(dims, kind)


in_smem = pl.BlockSpec(memory_space=pltpu.SMEM)
in_vmem = pl.BlockSpec(memory_space=pltpu.VMEM)


def as_row(column):
    return jnp.broadcast_to(column, (column.shape[0], 128)).T[:1]


def as_column(row):
    width = row.shape[1]
    padded = -(-width // 128) * 128
    row = row.astype(wide)
    if padded != width:
        row = jnp.concatenate([row, jnp.zeros((1, padded - width), wide)], axis=1)
    return jnp.broadcast_to(row, (128, padded)).T[:width, :1]


def segment_start(lengths_ref, rows):
    start = jnp.zeros_like(rows)
    end = jnp.int32(0)
    for i in range(lengths_ref.shape[1]):
        end = end + lengths_ref[0, i]
        start = jnp.where(rows >= end, end, start)
    return start


def rotate(pair, cosine, sine):
    half = HEAD_DIM // 2
    first, second = pair[:half], pair[half:]
    return jnp.concatenate(
        [first * cosine - second * sine, second * cosine + first * sine], axis=0
    )


def enter_kernel(
    lengths_ref, place_ref, tokens_ref, gain_ref, wq_ref, wk_ref, wv_ref, bq_ref, bk_ref, bv_ref,
    turn_ref, q_ref, kv_ref, normed_ref, tokens_t_ref, cos_ref, sin_ref,
):
    rows = tokens_ref.shape[0]
    hidden = tokens_ref[...].astype(wide)
    inverse = lax.rsqrt(jnp.mean(hidden * hidden, axis=1, keepdims=True) + epsilon)
    normed = (hidden * inverse * gain_ref[...].astype(wide)).astype(low)
    tokens_t_ref[...] = hidden.T.astype(low)
    normed_ref[...] = normed.astype(wide).T.astype(low)
    index = place_ref[0] * rows + lax.broadcasted_iota(jnp.int32, (1, rows), 1)
    position = (index - segment_start(lengths_ref, index)).astype(wide)
    angles = turn_ref[...] * position
    cosine, sine = jnp.cos(angles), jnp.sin(angles)
    cos_ref[...] = cosine
    sin_ref[...] = sine
    q_lin = dot_nt(wq_ref[...], normed) + as_column(bq_ref[...])
    for h in range(q_lin.shape[0] // HEAD_DIM):
        head = rotate(q_lin[h * HEAD_DIM : (h + 1) * HEAD_DIM], cosine, sine)
        q_ref[h * HEAD_DIM : (h + 1) * HEAD_DIM, :] = head.astype(low) * low(HEAD_DIM**-0.5)
    k_lin = dot_nt(wk_ref[...], normed) + as_column(bk_ref[...])
    v_lin = dot_nt(wv_ref[...], normed) + as_column(bv_ref[...])
    kv_ref[...] = jnp.concatenate([rotate(k_lin, cosine, sine), v_lin], axis=0).T.astype(low)


def weights_kernel(
    lengths_ref, place_ref, gate_ref, up_ref, down_ref, cotangent_ref,
    gate_t_ref, gate_own_ref, up_t_ref, up_own_ref, down_t_ref, mine_ref, other_ref, turned_ref, grad_ref,
):
    units = gate_t_ref.shape[0]
    width, hidden = gate_ref.shape
    window = turned_ref.shape[0]
    first = place_ref[0] * units
    base = pl.multiple_of(jnp.minimum(first // 128 * 128, hidden - window), 128)
    for ref, turned, own in ((gate_ref, gate_t_ref, gate_own_ref), (up_ref, up_t_ref, up_own_ref)):
        turned_ref[...] = ref[:, pl.ds(base, window)].astype(wide).T
        part = turned_ref[pl.ds(pl.multiple_of(first - base, 8), units), :]
        turned[...] = part.astype(low)
        own[...] = part.T.astype(low)
    down_t_ref[...] = down_ref[...].astype(wide).T.astype(low)
    rows = cotangent_ref.shape[0]
    half = rows // 2
    row = place_ref[0] * rows + lax.broadcasted_iota(jnp.int32, (rows, 1), 0)
    end = jnp.int32(0)
    for i in range(lengths_ref.shape[1]):
        end = end + lengths_ref[0, i]
    grad_ref[...] = jnp.where(row < end, cotangent_ref[...].astype(wide), 0.0)
    core = place_ref[1]
    mine_ref[...] = grad_ref[pl.ds(pl.multiple_of(core * half, half), half), :].astype(low)
    other_ref[...] = grad_ref[pl.ds(pl.multiple_of((1 - core) * half, half), half), :].astype(low)


def mask_bias(key_base, key_rows, q_index, q_start):
    keys = key_base + lax.broadcasted_iota(jnp.int32, (key_rows, q_index.shape[1]), 0)
    return jnp.where((keys >= q_start) & (keys <= q_index), 0.0, masked_value)


def first_row(lengths_ref, row):
    start = jnp.int32(0)
    end = jnp.int32(0)
    for i in range(lengths_ref.shape[1]):
        end = end + lengths_ref[0, i]
        start = jnp.where(row >= end, end, start)
    return start


def attend_kernel(blocks, lengths_ref, place_ref, q_ref, w_out_ref, *refs):
    kv_refs = refs[:blocks]
    out_ref, log_ref, mine_ref, other_ref, kv_ref, acc_ref, max_ref, bias_ref, part_ref = refs[blocks:]
    rows = q_ref.shape[1]
    heads = q_ref.shape[0] // HEAD_DIM
    own, core = place_ref[0], place_ref[1]
    for r in range(blocks):
        kv_ref[r] = kv_refs[r][...]
    q_index = own * rows + lax.broadcasted_iota(jnp.int32, (1, rows), 1)
    q_start = segment_start(lengths_ref, q_index)
    acc_ref[...] = jnp.zeros_like(acc_ref)
    max_ref[...] = jnp.full_like(max_ref, masked_value)

    def visit(block, carry):
        pair = kv_ref[block ^ own]
        keys = pair[:, :HEAD_DIM]
        values = pair.astype(wide).T[HEAD_DIM:].astype(low)
        values = jnp.concatenate([values, jnp.ones((16, rows), low)], axis=0)
        bias_ref[...] = mask_bias(block * rows, rows, q_index, q_start)
        for h in range(heads):
            scores = dot_nn(keys, q_ref[h * HEAD_DIM : (h + 1) * HEAD_DIM, :]) + bias_ref[...]
            old = max_ref[h : h + 1, :]
            new = jnp.maximum(old, jnp.max(scores, axis=0, keepdims=True))
            weight = jnp.exp(scores - new).astype(low)
            acc_ref[h] = acc_ref[h] * jnp.exp(old - new) + dot_nn(values, weight)
            max_ref[h : h + 1, :] = new
        return carry

    lax.fori_loop(first_row(lengths_ref, own * rows) // rows, own + 1, visit, 0)
    for h in range(heads):
        total = acc_ref[h, HEAD_DIM : HEAD_DIM + 1, :]
        out_ref[h * HEAD_DIM : (h + 1) * HEAD_DIM, :] = acc_ref[h, :HEAD_DIM, :] / total
        log_ref[h : h + 1, :] = max_ref[h : h + 1, :] + jnp.log(total)
    part_ref[...] = dot_tn(w_out_ref[...], out_ref[...].astype(low))
    half = mine_ref.shape[1]
    mine_ref[...] = part_ref[:, pl.ds(pl.multiple_of(core * half, half), half)]
    other_ref[...] = part_ref[:, pl.ds(pl.multiple_of((1 - core) * half, half), half)].astype(low)


def middle_kernel(place_ref, tokens_ref, part_ref, passed_ref, gain_ref, hidden_ref, normed_ref):
    half = hidden_ref.shape[1]
    mine = pl.ds(pl.multiple_of(place_ref[1] * half, half), half)
    hidden = tokens_ref[:, mine].astype(wide) + part_ref[...] + passed_ref[...].astype(wide)
    hidden_ref[...] = hidden
    inverse = lax.rsqrt(jnp.mean(hidden * hidden, axis=0, keepdims=True) + epsilon)
    normed_ref[...] = (hidden * inverse * as_column(gain_ref[...])).astype(low)


def hidden_kernel(parts, *refs):
    gy_refs, x_refs, refs = refs[: 2 * parts], refs[2 * parts : 4 * parts], refs[4 * parts :]
    gate_t_ref, up_t_ref, down_ref, gate_ref, up_ref = refs[:5]
    mixed_ref, grad_gate_ref, grad_up_ref, other_ref, mine_ref, x_ref, gy_ref = refs[5:]
    half = other_ref.shape[1]
    row = 0
    for k in range(2):
        at = 0
        for x, gy in zip(x_refs[k * parts : (k + 1) * parts], gy_refs[k * parts : (k + 1) * parts]):
            x_ref[at : at + x.shape[0], k * half : (k + 1) * half] = x[...]
            gy_ref[row : row + gy.shape[0], :] = gy[...]
            at += x.shape[0]
            row += gy.shape[0]
    x = x_ref[...]
    gate = dot_nn(gate_t_ref[...], x)
    up = dot_nn(up_t_ref[...], x)
    grad_mixed = dot_nt(down_ref[...], gy_ref[...])
    sigmoid = 1.0 / (1.0 + jnp.exp(-gate))
    silu = gate * sigmoid
    mixed_ref[...] = (silu * up).astype(low)
    grad_gate = (grad_mixed * up * sigmoid * (1.0 + gate * (1.0 - sigmoid))).astype(low)
    grad_up = (grad_mixed * silu).astype(low)
    grad_gate_ref[...] = grad_gate
    grad_up_ref[...] = grad_up
    back = (dot_nn(gate_ref[...], grad_gate) + dot_nn(up_ref[...], grad_up)).astype(low)
    other_ref[...] = back[:, :half]
    mine_ref[...] = back[:, half:]


def weight_kernel(transposed, first, counts, outputs, *refs):
    blocks = len(counts)
    lefts, parts, out_refs, right_ref = refs[:blocks], refs[blocks : -outputs - 1], refs[-outputs - 1 : -1], refs[-1]
    units = lefts[0].shape[0]
    columns = sum(ref.shape[0] for ref in out_refs) // units * 128
    last = first + columns
    total, at = None, 0
    for r in range(blocks):
        row = 0
        for k in range(2):
            place = 0
            for part in parts[at : at + counts[r]]:
                if transposed:
                    half = part.shape[1]
                    start, end = max(place, first), min(place + part.shape[0], last)
                    if start < end:
                        right_ref[r, start - first : end - first, k * half : (k + 1) * half] = part[
                            start - place : end - place, :
                        ]
                    place += part.shape[0]
                else:
                    right_ref[r, row : row + part.shape[0], :] = part[:, first:last]
                    row += part.shape[0]
            at += counts[r]
        left, right = lefts[r][...], right_ref[r]
        product = dot_nt(left, right) if transposed else dot_nn(left, right)
        total = product if total is None else total + product
    at = 0
    for out_ref in out_refs:
        for t in range(out_ref.shape[0] // units):
            out_ref[t * units : (t + 1) * units, :] = total[:, at : at + 128].astype(low)
            at += 128


def project_kernel(blocks, weight_ref, *refs):
    other_ref, mine_refs = refs[blocks], refs[blocks + 1 :]
    half = other_ref.shape[2]
    for r in range(blocks):
        part = dot_nn(weight_ref[...], refs[r][...]).astype(low)
        other_ref[r] = part[:, :half]
        mine_refs[r][...] = part[:, half:]


def add_kernel(*refs):
    count = (len(refs) - 1) // 2
    for i in range(count):
        refs[1 + count + i][...] = (refs[1 + i][...].astype(wide) + refs[0][i].astype(wide)).astype(low)


def pair_kernel(*refs):
    count = len(refs) // 3
    for i in range(count):
        refs[2 * count + i][...] = (refs[2 * i][...].astype(wide) + refs[2 * i + 1][...].astype(wide)).astype(low)


def wait_kernel(*refs):
    pass


def tick_kernel(ops, place_ref, *refs):
    ins, outs = refs[: -len(ops)], refs[-len(ops) :]
    end = (place_ref[2] == 0) | (place_ref[2] == 3)
    for (kind, args), out_ref in zip(ops, outs):
        sources = [(ins if given else outs)[i] for given, i, *_ in args]
        if kind == "add":
            out_ref[...] = (sources[0][...].astype(wide) + sources[1][...].astype(wide)).astype(low)
        elif kind == "pick":
            out_ref[...] = jnp.where(end, sources[0][...], sources[1][...])
        else:
            at = 0
            for source, (_, _, start, rows) in zip(sources, args):
                out_ref[at : at + rows, :] = source[start : start + rows, :]
                at += rows


def sum_blocks(refs, starts=None, rows=None):
    total = None
    for i, ref in enumerate(refs):
        value = ref[...] if starts is None else ref[starts[i] : starts[i] + rows, :]
        total = value.astype(wide) if total is None else total + value.astype(wide)
    return total


def layer_kernel(hidden_ref, *refs):
    out_ref = refs[-1]
    out_ref[...] = (hidden_ref[...] + sum_blocks(refs[:-1])).T.astype(low)


def grad_middle_kernel(hidden_ref, gain_ref, gy_ref, *refs):
    grad_ref, grad_low_ref, grad_gain_ref = refs[-3:]
    hidden = hidden_ref[...]
    inverse = lax.rsqrt(jnp.mean(hidden * hidden, axis=0, keepdims=True) + epsilon)
    grad_normed = sum_blocks(refs[:-3])
    weighted = as_column(gain_ref[...]) * grad_normed
    inner = jnp.mean(weighted * hidden, axis=0, keepdims=True)
    grad = inverse * weighted - hidden * (inverse * inverse * inverse * inner)
    grad = grad + gy_ref[...].astype(wide).T
    grad_ref[...] = grad
    grad_low_ref[...] = grad.astype(low)
    grad_gain_ref[...] = as_row(jnp.sum(grad_normed * hidden * inverse, axis=1, keepdims=True))


def back_enter_kernel(
    place_ref, gm_mine_ref, gm_other_ref, w_out_ref, out_ref, go_ref, delta_ref, gm_ref
):
    half = gm_mine_ref.shape[1]
    core = place_ref[1]
    gm_ref[:, pl.ds(pl.multiple_of(core * half, half), half)] = gm_mine_ref[...]
    gm_ref[:, pl.ds(pl.multiple_of((1 - core) * half, half), half)] = gm_other_ref[...]
    grad_out = dot_nn(w_out_ref[...], gm_ref[...]).astype(low)
    go_ref[...] = grad_out
    product = grad_out.astype(wide) * out_ref[...]
    for h in range(product.shape[0] // HEAD_DIM):
        delta_ref[h : h + 1, :] = jnp.sum(
            product[h * HEAD_DIM : (h + 1) * HEAD_DIM], axis=0, keepdims=True
        )


def attend_back_kernel(
    blocks, lengths_ref, place_ref, go_ref, delta_ref, log_ref, q_ref, cos_ref, sin_ref, *refs,
):
    kv_refs, refs = refs[:blocks], refs[blocks:]
    (grad_q_ref, *grad_kv_refs), refs = refs[: blocks + 1], refs[blocks + 1 :]
    kv_ref, bias_ref, dq_ref, dk_ref, dv_ref, grad_kv_ref = refs
    rows = q_ref.shape[1]
    heads = grad_q_ref.shape[0] // HEAD_DIM
    own = place_ref[0]
    for r in range(blocks):
        kv_ref[r] = kv_refs[r][...]
        grad_kv_ref[r] = jnp.zeros_like(grad_kv_ref[r])
    dq_ref[...] = jnp.zeros_like(dq_ref)
    q_index = own * rows + lax.broadcasted_iota(jnp.int32, (1, rows), 1)
    q_start = segment_start(lengths_ref, q_index)

    def visit(block, carry):
        pair = kv_ref[block ^ own]
        keys = pair[:, :HEAD_DIM]
        values = pair[:, HEAD_DIM:]
        keys_t = pair.astype(wide).T[:HEAD_DIM].astype(low)
        bias_ref[...] = mask_bias(block * rows, rows, q_index, q_start)
        for h in range(heads):
            span = slice(h * HEAD_DIM, (h + 1) * HEAD_DIM)
            scores = dot_nn(keys, q_ref[span, :]) + bias_ref[...]
            weight = jnp.exp(scores - log_ref[h : h + 1, :])
            grad_weight = dot_nn(values, go_ref[span, :])
            grad_scores = (weight * (grad_weight - delta_ref[h : h + 1, :])).astype(low)
            dq_ref[span, :] += dot_nn(keys_t, grad_scores)
            dk = dot_nt(grad_scores, q_ref[span, :])
            dv = dot_nt(weight.astype(low), go_ref[span, :])
            if h == 0:
                dk_ref[...] = dk
                dv_ref[...] = dv
            else:
                dk_ref[...] += dk
                dv_ref[...] += dv
        grad_kv_ref[block ^ own] = jnp.concatenate([dk_ref[...], dv_ref[...]], axis=1).astype(low)
        return carry

    lax.fori_loop(first_row(lengths_ref, own * rows) // rows, own + 1, visit, 0)
    for r in range(blocks):
        grad_kv_refs[r][...] = grad_kv_ref[r]
    for h in range(heads):
        span = slice(h * HEAD_DIM, (h + 1) * HEAD_DIM)
        turned = rotate(dq_ref[span, :] * HEAD_DIM**-0.5, cos_ref[...], -sin_ref[...])
        grad_q_ref[span, :] = turned.astype(low)


def query_kernel(
    place_ref, normed_ref, grad_q_ref, wq_ref, gm_mine_ref, gm_other_ref, out_ref,
    grad_wq_ref, part_ref, grad_bq_ref, grad_w_out_ref, gm_ref,
):
    half = gm_mine_ref.shape[1]
    core = place_ref[1]
    gm_ref[:, pl.ds(pl.multiple_of(core * half, half), half)] = gm_mine_ref[...]
    gm_ref[:, pl.ds(pl.multiple_of((1 - core) * half, half), half)] = gm_other_ref[...]
    grad_w_out_ref[...] = dot_nt(out_ref[...].astype(low), gm_ref[...]).astype(low)
    grad_q = grad_q_ref[...]
    grad_wq_ref[...] = dot_nt(grad_q, normed_ref[...]).astype(low)
    part_ref[...] = dot_tn(wq_ref[...], grad_q)
    grad_bq_ref[...] = dot_nt(jnp.ones((16, grad_q.shape[1]), low), grad_q)


def key_kernel(
    blocks, starts, place_ref, normed_ref, tokens_ref, part_ref, wk_ref, wv_ref, cos_ref, sin_ref,
    grad_wq_ref, grad_bq_ref, grad_w_out_ref, grad_gain_two_ref, *refs,
):
    kv_refs, share_refs, (mine_ref, other_ref, sum_ref, pack_ref) = refs[:blocks], refs[blocks : 2 * blocks], refs[2 * blocks :]
    both = sum_blocks(kv_refs, starts, tokens_ref.shape[1]).T
    both = jnp.concatenate(
        [rotate(both[:HEAD_DIM], cos_ref[...], -sin_ref[...]), both[HEAD_DIM:]], axis=0
    ).astype(low)
    total = part_ref[...] + dot_tn(wk_ref[...], both[:HEAD_DIM]) + dot_tn(wv_ref[...], both[HEAD_DIM:])
    sum_ref[...] = total
    half = mine_ref.shape[1]
    core = place_ref[1]
    mine_ref[...] = sum_ref[:, pl.ds(pl.multiple_of(core * half, half), half)]
    other_ref[...] = sum_ref[:, pl.ds(pl.multiple_of((1 - core) * half, half), half)].astype(low)
    hidden = tokens_ref[...].astype(wide)
    inverse = lax.rsqrt(jnp.mean(hidden * hidden, axis=0, keepdims=True) + epsilon)
    q_width, width = grad_wq_ref.shape
    kv_width = both.shape[0]
    at = 0
    pack_ref[at : at + q_width, :] = grad_wq_ref[...]
    at += q_width
    pack_ref[at : at + kv_width, :] = dot_nt(both, normed_ref[...]).astype(low)
    at += kv_width
    pack_ref[at : at + q_width, :] = grad_w_out_ref[...]
    at += q_width
    grad_gain = as_row(jnp.sum(total * (hidden * inverse), axis=1, keepdims=True))
    grad_bkv = dot_nt(jnp.ones((16, both.shape[1]), low), both)[:1]
    biases = jnp.concatenate(
        [grad_bq_ref[:1, :], grad_bkv, jnp.zeros((1, width - q_width - kv_width), wide)], axis=1
    )
    small = jnp.concatenate(
        [grad_gain, grad_gain_two_ref[...], biases, jnp.zeros((pack_ref.shape[0] - at - 3, width), wide)], axis=0
    )
    pack_ref[at:, :] = small.astype(low)
    share = pack_ref.shape[0] // blocks
    for r in range(blocks):
        start = pl.multiple_of((place_ref[0] ^ r) * share, share)
        for t in range(width // 128):
            share_refs[r][t * share : (t + 1) * share, :] = pack_ref[pl.ds(start, share), t * 128 : (t + 1) * 128]


def share_kernel(starts, *refs):
    refs[-1][...] = sum_blocks(refs[:-1], starts, refs[-1].shape[0]).astype(low)


def unpack_kernel(share, sources, place_ref, *refs):
    pieces, outs, (stack_ref, pack_ref) = refs[: len(sources)], refs[len(sources) : -2], refs[-2:]
    for ref, (r, first, rows, start) in zip(pieces, sources):
        stack_ref[r, first : first + rows, :] = ref[start : start + rows, :].astype(wide)
    for r in range(stack_ref.shape[0]):
        at = pl.ds(pl.multiple_of((place_ref[0] ^ r) * share, 8), share)
        for t in range(stack_ref.shape[1] // share):
            pack_ref[at, t * 128 : (t + 1) * 128] = stack_ref[r, t * share : (t + 1) * share, :]
    at = 0
    for out_ref in outs:
        out_ref[...] = pack_ref[at : at + out_ref.shape[0], :]
        at += out_ref.shape[0]


def leave_kernel(place_ref, tokens_ref, mine_ref, passed_ref, gain_ref, grad_mid_ref, out_ref):
    half = mine_ref.shape[1]
    hidden = tokens_ref[:, pl.ds(pl.multiple_of(place_ref[1] * half, half), half)].astype(wide)
    inverse = lax.rsqrt(jnp.mean(hidden * hidden, axis=0, keepdims=True) + epsilon)
    weighted = as_column(gain_ref[...]) * (mine_ref[...] + passed_ref[...].astype(wide))
    inner = jnp.mean(weighted * hidden, axis=0, keepdims=True)
    grad = grad_mid_ref[...] + inverse * weighted - hidden * (inverse * inverse * inverse * inner)
    out_ref[...] = grad.T.astype(low)


def place_kernel(transposed, tiles, place_ref, *refs):
    own_ref, near_x_ref, near_y_ref, *far_refs = refs[:7]
    out_ref = refs[-2] if transposed else refs[-1]
    all_ref = refs[-1]
    step = pl.program_id(0)
    units = own_ref.shape[0]
    half = units // 2
    for r, ref in enumerate((own_ref, near_x_ref, near_y_ref)):
        start = pl.multiple_of((place_ref[0] ^ r) * units, 8)
        all_ref[pl.ds(start, units), :] = ref[...].astype(wide)
    for k in range(2):
        start = pl.multiple_of((place_ref[0] ^ 3) * units + k * half, 8)
        part = 2 * step + k

        @pl.when(part < tiles)
        def _(start=start, k=k):
            all_ref[pl.ds(start, half), :] = far_refs[k][...].astype(wide)

        @pl.when(part >= tiles)
        def _(start=start, k=k):
            all_ref[pl.ds(start, half), :] = far_refs[2 + k][...].astype(wide)

    if transposed:
        out_ref[...] = all_ref[...].T


def place_share(place, own, near_x, near_y, far_y, far_x, units, transposed, width, at, whole, last):
    tile, half = 128, units // 2
    tiles = own.shape[0] // units
    first = at // tile
    piece = pl.BlockSpec((units, tile), lambda i: (i, 0))

    def halves(start, k, later):
        base = start // half

        def index(i):
            part = 2 * i + k - (tiles if later else 0)
            return (base + jnp.clip(part, 0, tiles - 1), 0)

        return pl.BlockSpec((half, tile), index)

    ins = [place, own, near_x, near_y, far_y[0], far_y[0], far_x[0], far_x[0]] + last
    specs = (
        [in_smem, piece, piece, piece]
        + [halves(far_y[1], k, False) for k in range(2)]
        + [halves(far_x[1], k, True) for k in range(2)]
        + [pl.BlockSpec(memory_space=pl.ANY)] * len(last)
    )
    aliases = {}
    if whole is not None:
        aliases = {len(ins): 0}
        ins.append(whole)
        specs.append(pl.BlockSpec(memory_space=pl.ANY))

    def body(*refs):
        place_kernel(transposed, tiles, *refs[:8], *refs[len(ins) :])

    if transposed:
        dims = (width, 4 * units)
        out_spec = pl.BlockSpec((tile, 4 * units), lambda i: (i + first, 0))
        scratch = [pltpu.VMEM((4 * units, tile), wide)]
    else:
        dims = (4 * units, width)
        out_spec = pl.BlockSpec((4 * units, tile), lambda i: (0, i + first))
        scratch = []
    return pl.pallas_call(
        body,
        name="place_kernel",
        out_shape=shape(dims, wide),
        grid=(tiles,),
        in_specs=specs,
        out_specs=out_spec,
        scratch_shapes=scratch,
        input_output_aliases=aliases,
        cost_estimate=pl.CostEstimate(flops=0, bytes_accessed=0, transcendentals=0),
        compiler_params=pltpu.CompilerParams(vmem_limit_bytes=vmem_limit),
    )(*ins)


def local(
    tokens,
    lengths,
    norm1_gain,
    w_query,
    b_query,
    w_key,
    b_key,
    w_value,
    b_value,
    w_out,
    norm2_gain,
    w_gate,
    w_up,
    w_down,
    cotangent,
):
    rows, width = tokens.shape
    half = rows // 2
    blocks = lax.axis_size("blk")
    own_block = lax.axis_index("blk")
    own_core = lax.axis_index("tensor")
    q_width = w_query.shape[1]
    heads = q_width // HEAD_DIM
    units = w_gate.shape[1] // blocks
    place = jnp.stack([own_block, own_core, lax.axis_index("dp")]).astype(jnp.int32)
    gain_two = norm2_gain.reshape(1, width)

    def whole_rows(mine):
        other = partner(mine, "tensor", 1, "rows_core")
        return jnp.where(
            own_core == 0,
            jnp.concatenate([mine, other], axis=0),
            jnp.concatenate([other, mine], axis=0),
        )

    half_dim = HEAD_DIM // 2
    turn = (rope_base ** (-2.0 * jnp.arange(half_dim, dtype=wide) / HEAD_DIM)).reshape(half_dim, 1)
    q_t, key_value, normed_t, tokens_t, cosine, sine = call(
        enter_kernel,
        [
            shape((q_width, rows), low),
            shape((rows, 2 * HEAD_DIM), low),
            shape((width, rows), low),
            shape((width, rows), low),
            shape((half_dim, rows), wide),
            shape((half_dim, rows), wide),
        ],
        [
            lengths, place, tokens, norm1_gain.reshape(1, width), w_query.T, w_key.T, w_value.T,
            b_query.reshape(1, -1), b_key.reshape(1, -1), b_value.reshape(1, -1), turn,
        ],
        in_specs=[in_smem] * 2 + [in_vmem] * 9,
    )
    kv_blocks = gather_blocks(key_value, "kv")

    down_own = lax.dynamic_slice_in_dim(w_down, own_block * units, units, 0)
    window = -(-(units + 127) // 128) * 128
    gate_t, gate_own, up_t, up_own, down_t, grad_y_mine, grad_y_other = call(
        weights_kernel,
        [
            shape((units, width), low),
            shape((width, units), low),
            shape((units, width), low),
            shape((width, units), low),
            shape((width, units), low),
            shape((half, width), low),
            shape((half, width), low),
        ],
        [lengths, place, w_gate, w_up, down_own, cotangent],
        [pltpu.VMEM((window, width), wide), pltpu.VMEM((rows, width), wide)],
        in_specs=[in_smem] * 2 + [in_vmem] * 4,
        after=[q_t],
    )
    gy_near = {r: partner(grad_y_mine, "blk", r, "gy") for r in range(1, blocks) if r & (r - 1) == 0}

    out_t, log_total, part_mine, part_other = call(
        functools.partial(attend_kernel, blocks),
        [
            shape((q_width, rows), wide),
            shape((heads + 1, rows), wide),
            shape((width, half), wide),
            shape((width, half), low),
        ],
        [lengths, place, q_t, w_out] + kv_blocks,
        [
            pltpu.VMEM((blocks, rows, 2 * HEAD_DIM), low),
            pltpu.VMEM((heads, HEAD_DIM + 16, rows), wide),
            pltpu.VMEM((heads + 1, rows), wide),
            pltpu.VMEM((rows, rows), wide),
            pltpu.VMEM((width, rows), wide),
        ],
        in_specs=[in_smem] * 2 + [in_vmem] * (2 + blocks),
        after=[gate_t],
    )
    hidden, normed_two = call(
        middle_kernel,
        [shape((width, half), wide), shape((width, half), low)],
        [place, tokens_t, part_mine, partner(part_other, "tensor", 1, "part_core"), gain_two],
        in_specs=[in_smem] + [in_vmem] * 4,
        after=list(gy_near.values()),
    )

    last = [normed_two]

    def ordered(body, outs, ins, needs=(), **more):
        nonlocal last
        carry = more.get("carry", ())
        after = [v for v in last + list(needs) if not any(v is c for c in carry)]
        results = call(body, outs, ins, after=after, **more)
        last = [results[0]]
        return results

    def wait(carry, needs=()):
        return list(ordered(wait_kernel, [], [], needs=needs, carry=carry))

    def near(pieces):
        return [p for r, parts in enumerate(pieces) if r and r & (r - 1) == 0 for p in parts]

    def far(pieces):
        return [p for r, parts in enumerate(pieces) if r & (r - 1) for p in parts]

    kept = shape((units, rows), low)
    piece = shape((width, half), low)
    runs, back, passed = [], [None] * blocks, [None] * blocks

    def cores(parts, name):
        return [partner(part, "tensor", 1, name) for part in parts]

    x_parts, gy_parts = [], []

    def hidden_units(r, x_mine, x_other, gy_mine, gy_other):
        x_parts.append(x_other + x_mine)
        gy_parts.append(gy_other + gy_mine)
        runs.append(
            ordered(
                functools.partial(hidden_kernel, len(x_mine)),
                [kept, kept, kept, piece, piece],
                gy_parts[-1] + x_parts[-1] + [gate_t, up_t, down_own, gate_own, up_own],
                scratch=[pltpu.VMEM((width, rows), low), pltpu.VMEM((rows, width), low)],
            )
        )
        return runs[-1][3]

    def add_back(members, carry, needs=()):
        results = ordered(
            pair_kernel,
            [piece] * len(members),
            [value for r in members for value in (runs[r][4], passed[r])],
            needs=needs,
            carry=carry,
        )
        for r, value in zip(members, results):
            back[r] = partner(value, "blk", r, "back") if r else value
        return results[len(members) :]

    def hidden_weight(transposed, left, parts, first, shares):
        counts = [len(part) // 2 for part in parts]
        columns = sum(shares)
        dims = (columns, rows) if transposed else (rows, columns)
        return ordered(
            functools.partial(weight_kernel, transposed, first, counts, len(shares)),
            [shape((share // 128 * units, 128), low) for share in shares],
            [run[left] for run in runs] + sum(parts, []),
            scratch=[pltpu.VMEM((blocks,) + dims, low)],
        )

    def tick(ops, needs=(), carry=()):
        given, outs, listed = [], [], []
        for kind, *args in ops:
            spans = [arg if isinstance(arg, tuple) else (arg, 0, None) for arg in args]
            named, size = [], 0
            for value, start, count in spans:
                if isinstance(value, int):
                    entry, total = (False, value), outs[value].shape[0]
                else:
                    found = [i for i, known in enumerate(given) if known is value]
                    if not found:
                        given.append(value)
                    entry = (True, found[0] if found else len(given) - 1)
                    total = value.shape[0]
                count = total if count is None else count
                named.append(entry + (start, count))
                size = size + count if kind == "cat" else count
            listed.append((kind, named))
            outs.append(shape((size, 128), low))
        return ordered(
            functools.partial(tick_kernel, listed),
            outs,
            [place] + given,
            in_specs=[in_smem] + [in_vmem] * len(given),
            needs=needs,
            carry=carry,
        )

    x_near = {r: partner(normed_two, "blk", r, "x") for r in range(1, blocks) if r & (r - 1) == 0}
    other = hidden_units(
        0, [normed_two], cores([normed_two], "x_core"), [grad_y_mine], [grad_y_other]
    )
    other, *arrived = wait([other] + list(x_near.values()))
    passed[0] = partner(other, "tensor", 1, "back_core")
    x_near = dict(zip(x_near, arrived))
    x_mine = relay_far(x_near, normed_two, "x")
    gy_mine = relay_far(gy_near, grad_y_mine, "gy")
    x_other = {r: cores(parts, "x_core") for r, parts in x_mine.items() if r in x_near}
    gy_other = {r: cores(parts, "gy_core") for r, parts in gy_mine.items() if r in x_near}
    waiting, out_of = [], list(range(1, blocks))
    for i, r in enumerate(out_of):
        other = hidden_units(r, x_mine[r], x_other[r], gy_mine[r], gy_other[r])
        ready = [k for k in out_of if k not in x_near] if i == 0 else []
        fars = [part for k in ready for part in x_mine[k] + gy_mine[k]]
        if i == 0:
            other, *fars = wait([other] + fars)
        else:
            other, *fars = add_back([out_of[i - 1]], [other])
        passed[r] = partner(other, "tensor", 1, "back_core")
        for k in ready:
            count = len(x_mine[k])
            x_mine[k], fars = fars[:count], fars[count:]
            count = len(gy_mine[k])
            gy_mine[k], fars = fars[:count], fars[count:]
            x_other[k] = cores(x_mine[k], "x_core")
            gy_other[k] = cores(gy_mine[k], "gy_core")
    cut_at = width // 2 // 128 * 128
    (d1,) = hidden_weight(False, 0, gy_parts, 0, [cut_at])
    d1_swap = swap(d1, "swap_d1")
    (d2,) = hidden_weight(False, 0, gy_parts, cut_at, [width - cut_at])
    layer_other, *layer_mine = ordered(
        functools.partial(project_kernel, blocks),
        [shape((blocks, width, half), low)] + [piece] * blocks,
        [down_t] + [run[0] for run in runs],
    )
    d2, layer_other = add_back(
        [blocks - 1, 0], [d2, layer_other], needs=back[1 : blocks - 1] + [d1_swap]
    )
    (d1_sum,) = tick([("add", d1, d1_swap)])
    d1_cross, d2_swap = cross(d1_sum, "cross_d1"), swap(d2, "swap_d2")
    layer_passed = partner(layer_other, "tensor", 1, "layer_core")
    g1, g2 = hidden_weight(True, 1, x_parts, 0, [cut_at, width - cut_at])
    u1, u2 = hidden_weight(True, 2, x_parts, 0, [cut_at, width - cut_at])
    d1_sum, d2_sum, d1_g1 = tick(
        [("add", d1_sum, d1_cross), ("add", d2, d2_swap), ("pick", g1, 0)], needs=back[1:]
    )
    grad_mid, grad_mid_low, grad_gain_two = ordered(
        grad_middle_kernel,
        [shape((width, half), wide), piece, shape((1, width), wide)],
        [hidden, gain_two, grad_y_mine] + back,
    )
    *layer_pieces, grad_mid_low, d1_g1, d2_sum = ordered(
        add_kernel, [piece] * blocks, [layer_passed] + layer_mine, carry=[grad_mid_low, d1_g1, d2_sum]
    )
    grad_mid_other = partner(grad_mid_low, "tensor", 1, "mid_core")
    layer_pieces = scatter_blocks(layer_pieces, "layer")
    d1_g1_swap, d2_cross = swap(d1_g1, "swap_d1_g1"), cross(d2_sum, "cross_d2")

    grad_out, delta = ordered(
        back_enter_kernel,
        [shape((q_width, rows), low), shape((heads + 1, rows), wide)],
        [place, grad_mid_low, grad_mid_other, w_out, out_t],
        scratch=[pltpu.VMEM((width, rows), low)],
        in_specs=[in_smem] + [in_vmem] * 4,
    )

    grad_q, *grad_kv = ordered(
        functools.partial(attend_back_kernel, blocks),
        [shape((q_width, rows), low)] + [shape((rows, 2 * HEAD_DIM), low)] * blocks,
        [lengths, place, grad_out, delta, log_total, q_t, cosine, sine] + kv_blocks,
        scratch=[
            pltpu.VMEM((blocks, rows, 2 * HEAD_DIM), low),
            pltpu.VMEM((rows, rows), wide),
            pltpu.VMEM((q_width, rows), wide),
            pltpu.VMEM((rows, HEAD_DIM), wide),
            pltpu.VMEM((rows, HEAD_DIM), wide),
            pltpu.VMEM((blocks, rows, 2 * HEAD_DIM), low),
        ],
        in_specs=[in_smem] * 2 + [in_vmem] * (6 + blocks),
    )
    pack_rows = -(-(2 * q_width + 2 * HEAD_DIM + 3) // (16 * blocks)) * 16 * blocks
    share = pack_rows // blocks
    stack_rows = share * (width // 128)

    def query_back():
        return ordered(
            query_kernel,
            [
                shape((q_width, width), low),
                shape((width, rows), wide),
                shape((16, q_width), wide),
                shape((q_width, width), low),
            ],
            [place, normed_t, grad_q, w_query.T, grad_mid_low, grad_mid_other, out_t],
            scratch=[pltpu.VMEM((width, rows), low)],
            in_specs=[in_smem] + [in_vmem] * 6,
        )

    def key_back(kv_pieces, starts):
        return ordered(
            functools.partial(key_kernel, blocks, starts),
            [shape((stack_rows, 128), low)] * blocks + [shape((width, half), wide), shape((width, half), low)],
            [
                place, normed_t, tokens_t, normed_part, w_key.T, w_value.T, cosine, sine,
                grad_w_query, grad_b_query, grad_w_out, grad_gain_two,
            ] + kv_pieces,
            scratch=[pltpu.VMEM((width, rows), wide), pltpu.VMEM((pack_rows, width), low)],
            in_specs=[in_smem] + [in_vmem] * (11 + blocks),
        )

    def sum_share(pieces, starts):
        (own,) = ordered(
            functools.partial(share_kernel, starts), [shape((stack_rows, 128), low)], pieces
        )
        return own

    def leave(normed_mine, normed_passed):
        (grad_half,) = ordered(
            leave_kernel,
            [shape((half, width), low)],
            [place, tokens_t, normed_mine, normed_passed, norm1_gain.reshape(1, width), grad_mid],
            in_specs=[in_smem] + [in_vmem] * 5,
        )
        return grad_half

    def layer_leave():
        (layer_half,) = ordered(layer_kernel, [shape((half, width), low)], [hidden] + layer_pieces)
        return layer_half

    def unpack(pieces, sources):
        return ordered(
            functools.partial(unpack_kernel, share, sources),
            [
                shape((q_width, width), wide),
                shape((HEAD_DIM, width), wide),
                shape((HEAD_DIM, width), wide),
                shape((q_width, width), wide),
                shape((pack_rows - 2 * q_width - 2 * HEAD_DIM, width), wide),
            ],
            [place] + pieces,
            scratch=[pltpu.VMEM((blocks, stack_rows, 128), wide), pltpu.VMEM((pack_rows, width), wide)],
            in_specs=[in_smem] + [in_vmem] * len(pieces),
        )

    if blocks != 4:
        kv_pieces = scatter_blocks(grad_kv, "grad_kv")
        grad_w_query, normed_part, grad_b_query, grad_w_out = query_back()
        *shares, normed_mine, normed_other = key_back(kv_pieces, [0] * blocks)
        layer_out = whole_rows(layer_leave())
        grad_half = leave(normed_mine, partner(normed_other, "tensor", 1, "normed_core"))
        own_share = sum_share(scatter_blocks(shares, "shares"), [0] * blocks)
        own_share = lax.psum(own_share, "dp")
        pieces = gather_blocks(own_share, "all_share")
        grad_w_query, grad_w_key, grad_w_value, grad_w_out, small = unpack(
            pieces, [(r, 0, stack_rows, 0) for r in range(blocks)]
        )

        def gather_weight(first, second, transposed):
            stacked = lax.psum(jnp.concatenate([first, second], axis=0), "dp")
            every = lax.all_gather(stacked, "blk").reshape(blocks, width // 128, units, 128)
            order = (1, 3, 0, 2) if transposed else (0, 2, 1, 3)
            dims = (width, blocks * units) if transposed else (blocks * units, width)
            return every.transpose(order).reshape(dims).astype(wide)

        grad_w_down = gather_weight(d1, d2, False)
        grad_w_gate = gather_weight(g1, g2, True)
        grad_w_up = gather_weight(u1, u2, True)
    else:
        r1, r2 = d1.shape[0], d2.shape[0]
        h1, h2 = r1 // 2, r2 // 2

        def both_ways(x_buffer, y_buffer, name):
            return partner(x_buffer, "blk", 1, name + "_x"), partner(y_buffer, "blk", 2, name + "_y")

        d1_all, g1_sum, d2_sum, d2_g2, x1, y1, kv_far = tick(
            [
                ("pick", d1_g1_swap, d1_sum),
                ("add", g1, d1_g1_swap),
                ("add", d2_sum, d2_cross),
                ("pick", g2, 2),
                ("cat", 0, grad_kv[1]),
                ("cat", 0, grad_kv[2]),
            ],
            needs=layer_pieces[1:],
            carry=[grad_kv[3]],
        )
        x1, y1 = both_ways(x1, y1, "d1")
        kv_far = partner(kv_far, "blk", 3, "grad_kv")
        d2_g2_swap, g1_cross = swap(d2_g2, "swap_d2_g2"), cross(g1_sum, "cross_g1")
        grad_w_query, normed_part, grad_b_query, grad_w_out = query_back()
        layer_half = layer_leave()
        d2_all, g2_sum, g1_sum, g1_u1, x2, y2, layer_half = tick(
            [
                ("pick", d2_g2_swap, d2_sum),
                ("add", g2, d2_g2_swap),
                ("add", g1_sum, g1_cross),
                ("pick", u1, 2),
                ("cat", 0, (y1, h1, h1)),
                ("cat", 0, (x1, 0, h1)),
            ],
            needs=[x1, y1, kv_far],
            carry=[layer_half],
        )
        x2, y2 = both_ways(x2, y2, "d2")
        g1_u1_swap, g2_cross = swap(g1_u1, "swap_g1_u1"), cross(g2_sum, "cross_g2")
        layer_out = whole_rows(layer_half)
        *shares, normed_mine, normed_other = key_back([grad_kv[0], x1, y1, kv_far], [0, r1, r1, 0])
        g1_all, u1_sum, g2_sum, g2_u2, x3, y3, share_far, normed_other = tick(
            [
                ("pick", g1_u1_swap, g1_sum),
                ("add", u1, g1_u1_swap),
                ("add", g2_sum, g2_cross),
                ("pick", u2, 2),
                ("cat", 0, (y2, h2, h2), shares[1]),
                ("cat", 0, (x2, 0, h2), shares[2]),
            ],
            needs=[x2, y2],
            carry=[shares[3], normed_other],
        )
        x3, y3 = both_ways(x3, y3, "g1")
        share_far = partner(share_far, "blk", 3, "shares")
        g2_u2_swap, u1_cross = swap(g2_u2, "swap_g2_u2"), cross(u1_sum, "cross_u1")
        normed_passed = partner(normed_other, "tensor", 1, "normed_core")
        grad_w_down = place_share(
            place, d1_all, x1, y1, (y2, r2), (x2, r2), units, False, width, 0, None, last
        )
        last = [grad_w_down]
        grad_half = leave(normed_mine, normed_passed)
        own_share = sum_share([shares[0], x3, y3, share_far], [0, r1 + h2, r1 + h2, 0])
        g2_all, u2_sum, u1_sum, x4, y4, own_share, grad_half = tick(
            [
                ("pick", g2_u2_swap, g2_sum),
                ("add", u2, g2_u2_swap),
                ("add", u1_sum, u1_cross),
                ("cat", 0, (y3, h1, h1)),
                ("cat", 0, (x3, 0, h1)),
            ],
            carry=[own_share, grad_half],
        )
        x4, y4 = both_ways(x4, y4, "g2")
        share_swap = swap(own_share, "swap_share")
        u1_swap, u2_cross = swap(u1_sum, "swap_u1"), cross(u2_sum, "cross_u2")
        grad_tokens = whole_rows(grad_half).astype(wide)
        grad_w_down = place_share(
            place, d2_all, x2, y2, (y3, r1), (x3, r1), units, False, width, cut_at, grad_w_down, [x3]
        )
        last = [grad_w_down]
        u1_all, u2_sum, own_share, x5, y5 = tick(
            [
                ("pick", u1_swap, u1_sum),
                ("add", u2_sum, u2_cross),
                ("add", own_share, share_swap),
                ("cat", 0, (y4, h2, h2)),
                ("cat", 0, (x4, 0, h2)),
            ],
            needs=[x4, y4],
        )
        x5, y5 = both_ways(x5, y5, "u1")
        u2_swap, share_swap = swap(u2_sum, "swap_u2"), partner(own_share, "dp", 2, "share_far")
        grad_w_gate = place_share(
            place, g1_all, x3, y3, (y4, r2), (x4, r2), units, True, width, 0, None, last
        )
        last = [grad_w_gate]
        u2_all, own_share, x6, y6 = tick(
            [
                ("pick", u2_swap, u2_sum),
                ("add", own_share, share_swap),
                ("cat", 0, (y5, h1, h1), 1),
                ("cat", 0, (x5, 0, h1), 1),
            ],
            needs=[x5, y5],
        )
        x6, y6 = both_ways(x6, y6, "u2")
        grad_w_gate = place_share(
            place, g2_all, x4, y4, (y5, r1), (x5, r1), units, True, width, cut_at, grad_w_gate, [x5]
        )
        last = [grad_w_gate]
        first_half = stack_rows // 32 * 16
        share_at = r2 + h1
        x7, y7 = tick(
            [
                ("cat", (y6, h2, h2), (y6, share_at + first_half, stack_rows - first_half)),
                ("cat", (x6, 0, h2), (x6, share_at, first_half)),
            ],
        )
        x7, y7 = both_ways(x7, y7, "far")
        grad_w_up = place_share(
            place, u1_all, x5, y5, (y6, r2), (x6, r2), units, True, width, 0, None, last
        )
        last = [grad_w_up]
        grad_w_up = place_share(
            place, u2_all, x6, y6, (y7, 0), (x7, 0), units, True, width, cut_at, grad_w_up, []
        )
        last = [y7]
        grad_w_query, grad_w_key, grad_w_value, grad_w_out, small = unpack(
            [own_share, x6, y6, y7, x7],
            [
                (0, 0, stack_rows, 0),
                (1, 0, stack_rows, share_at),
                (2, 0, stack_rows, share_at),
                (3, 0, first_half, h2),
                (3, first_half, stack_rows - first_half, h2),
            ],
        )
    if blocks != 4:
        grad_tokens = whole_rows(grad_half).astype(wide)
    gains = small[:2]
    gains = gains + partner(gains, "tensor", 1, "gains_core")
    grad_b = small[2]
    return (
        layer_out,
        grad_tokens,
        gains[0],
        grad_w_query.T,
        grad_b[:q_width],
        grad_w_key.T,
        grad_b[q_width : q_width + HEAD_DIM],
        grad_w_value.T,
        grad_b[q_width + HEAD_DIM : q_width + 2 * HEAD_DIM],
        grad_w_out,
        gains[1],
        grad_w_gate,
        grad_w_up,
        grad_w_down,
    )


def solution(mesh):
    placed = (
        P(("dp", "blk"), None),
        P("dp", None),
        P(),
        P(None, "tensor"),
        P("tensor"),
        P(None, "tensor"),
        P("tensor"),
        P(None, "tensor"),
        P("tensor"),
        P("tensor", None),
        P(),
        P(None, "tensor"),
        P(None, "tensor"),
        P("tensor", None),
        P(("dp", "blk"), None),
    )
    return jax.shard_map(
        local,
        mesh=mesh,
        in_specs=placed,
        out_specs=(
            P(("dp", "blk"), None),
            P(("dp", "blk"), None),
            P(),
            P(None, "tensor"),
            P("tensor"),
            P(None, "tensor"),
            P("tensor"),
            P(None, "tensor"),
            P("tensor"),
            P("tensor", None),
            P(),
            P(None, "tensor"),
            P(None, "tensor"),
            P("tensor", None),
        ),
        check_vma=False,
    )
```

```python
import functools
import math

import jax
import jax.numpy as jnp
from jax import lax
from jax.experimental import pallas as pl
from jax.experimental.pallas import tpu as pltpu
from jax.sharding import PartitionSpec as P

HEAD_DIM = 64

epsilon = 1e-06
rope_base = 1000000.0
masked_value = -1e30

low = jnp.bfloat16
wide = jnp.float32
vmem_limit = 40 * 1024 * 1024


def dot_nn(left, right):
    return lax.dot_general(left, right, (((1,), (0,)), ((), ())), preferred_element_type=wide)


def dot_nt(left, right):
    return lax.dot_general(left, right, (((1,), (1,)), ((), ())), preferred_element_type=wide)


def dot_tn(left, right):
    return lax.dot_general(left, right, (((0,), (0,)), ((), ())), preferred_element_type=wide)


def partner(value, axis, step, name):
    count = lax.axis_size(axis)
    with jax.named_scope(name):
        return lax.ppermute(value, axis, [(i, i ^ step) for i in range(count)])


def gather_blocks(piece, name):
    count = lax.axis_size("blk")
    return [piece] + [partner(piece, "blk", r, name) for r in range(1, count)]


def relay_far(near, own, name):
    count = lax.axis_size("blk")
    rows = own.shape[0]
    halved = rows % 32 == 0
    cuts = [slice(0, rows // 2), slice(rows // 2, rows)] if halved else [slice(0, rows)]
    pieces = {}
    for r in range(1, count):
        if r in near:
            pieces[r] = [near[r]]
            continue
        low_bit = r & -r
        high_bit = 1 << (r.bit_length() - 1)
        pieces[r] = []
        for i, (bit, rows_cut) in enumerate(zip((high_bit, low_bit), cuts)):
            source = pieces[r ^ bit]
            part = source[i] if len(source) > 1 else source[0][rows_cut]
            pieces[r].append(partner(part, "blk", bit, name + "_relay"))
    return pieces


def gather_relayed(piece, name):
    count = lax.axis_size("blk")
    near = {r: partner(piece, "blk", r, name) for r in range(1, count) if r & (r - 1) == 0}
    pieces = relay_far(near, piece, name)
    return [[piece]] + [pieces[r] for r in range(1, count)]


def scatter_blocks(pieces, name):
    return [pieces[0]] + [partner(pieces[r], "blk", r, name) for r in range(1, len(pieces))]


def swap(value, name):
    with jax.named_scope(name):
        return lax.ppermute(value, "dp", [(0, 1), (1, 0), (2, 3), (3, 2)])


def cross(value, name):
    with jax.named_scope(name):
        return lax.ppermute(value, "dp", [(1, 2), (2, 1)])


def call(body, outs, ins, scratch=(), in_specs=None, after=(), carry=(), moves=None):
    anywhere = pl.BlockSpec(memory_space=pl.ANY)
    whole = pl.BlockSpec(memory_space=pltpu.VMEM)
    in_specs = list(in_specs or [anywhere if moves else whole] * len(ins))
    given, waited, made = len(ins), len(after) + len(carry), len(outs)

    def run(*refs):
        results = given + waited
        body(*refs[:given], *refs[results : results + made], *refs[results + made + len(carry) :])

    return pl.pallas_call(
        run,
        name=getattr(body, "func", body).__name__,
        out_shape=tuple(outs) + tuple(shape(value.shape, value.dtype) for value in carry),
        in_specs=in_specs + [anywhere] * waited,
        out_specs=tuple([anywhere if moves == "all" else whole] * made + [anywhere] * len(carry)),
        scratch_shapes=list(scratch),
        input_output_aliases={given + len(after) + i: made + i for i in range(len(carry))},
        cost_estimate=pl.CostEstimate(flops=0, bytes_accessed=0, transcendentals=0),
        compiler_params=pltpu.CompilerParams(vmem_limit_bytes=vmem_limit),
    )(*ins, *after, *carry)


def shape(dims, kind):
    return jax.ShapeDtypeStruct(dims, kind)


in_smem = pl.BlockSpec(memory_space=pltpu.SMEM)
in_vmem = pl.BlockSpec(memory_space=pltpu.VMEM)


def as_row(column):
    return jnp.broadcast_to(column, (column.shape[0], 128)).T[:1]


def as_column(row):
    width = row.shape[1]
    padded = -(-width // 128) * 128
    row = row.astype(wide)
    if padded != width:
        row = jnp.concatenate([row, jnp.zeros((1, padded - width), wide)], axis=1)
    return jnp.broadcast_to(row, (128, padded)).T[:width, :1]


def segment_start(lengths_ref, rows):
    start = jnp.zeros_like(rows)
    end = jnp.int32(0)
    for i in range(lengths_ref.shape[1]):
        end = end + lengths_ref[0, i]
        start = jnp.where(rows >= end, end, start)
    return start


def rotate(pair, cosine, sine):
    half = HEAD_DIM // 2
    first, second = pair[:half], pair[half:]
    return jnp.concatenate(
        [first * cosine - second * sine, second * cosine + first * sine], axis=0
    )


def enter_kernel(
    lengths_ref, place_ref, tokens_ref, gain_ref, wq_ref, wk_ref, wv_ref, bq_ref, bk_ref, bv_ref,
    turn_ref, q_ref, kv_ref, normed_ref, tokens_t_ref, cos_ref, sin_ref,
):
    rows = tokens_ref.shape[0]
    hidden = tokens_ref[...].astype(wide)
    inverse = lax.rsqrt(jnp.mean(hidden * hidden, axis=1, keepdims=True) + epsilon)
    normed = (hidden * inverse * gain_ref[...].astype(wide)).astype(low)
    tokens_t_ref[...] = hidden.T.astype(low)
    normed_ref[...] = normed.astype(wide).T.astype(low)
    index = place_ref[0] * rows + lax.broadcasted_iota(jnp.int32, (1, rows), 1)
    position = (index - segment_start(lengths_ref, index)).astype(wide)
    angles = turn_ref[...] * position
    cosine, sine = jnp.cos(angles), jnp.sin(angles)
    cos_ref[...] = cosine
    sin_ref[...] = sine
    q_lin = dot_nt(wq_ref[...], normed) + as_column(bq_ref[...])
    for h in range(q_lin.shape[0] // HEAD_DIM):
        head = rotate(q_lin[h * HEAD_DIM : (h + 1) * HEAD_DIM], cosine, sine)
        q_ref[h * HEAD_DIM : (h + 1) * HEAD_DIM, :] = head.astype(low) * low(HEAD_DIM**-0.5)
    k_lin = dot_nt(wk_ref[...], normed) + as_column(bk_ref[...])
    v_lin = dot_nt(wv_ref[...], normed) + as_column(bv_ref[...])
    kv_ref[...] = jnp.concatenate([rotate(k_lin, cosine, sine), v_lin], axis=0).T.astype(low)


def weights_kernel(
    lengths_ref, place_ref, gate_ref, up_ref, down_ref, cotangent_ref,
    gate_t_ref, gate_own_ref, up_t_ref, up_own_ref, down_t_ref, mine_ref, other_ref, turned_ref, grad_ref,
):
    units = gate_t_ref.shape[0]
    width, hidden = gate_ref.shape
    window = turned_ref.shape[0]
    first = place_ref[0] * units
    base = pl.multiple_of(jnp.minimum(first // 128 * 128, hidden - window), 128)
    for ref, turned, own in ((gate_ref, gate_t_ref, gate_own_ref), (up_ref, up_t_ref, up_own_ref)):
        turned_ref[...] = ref[:, pl.ds(base, window)].astype(wide).T
        part = turned_ref[pl.ds(pl.multiple_of(first - base, 8), units), :]
        turned[...] = part.astype(low)
        own[...] = part.T.astype(low)
    down_t_ref[...] = down_ref[...].astype(wide).T.astype(low)
    rows = cotangent_ref.shape[0]
    half = rows // 2
    row = place_ref[0] * rows + lax.broadcasted_iota(jnp.int32, (rows, 1), 0)
    end = jnp.int32(0)
    for i in range(lengths_ref.shape[1]):
        end = end + lengths_ref[0, i]
    grad_ref[...] = jnp.where(row < end, cotangent_ref[...].astype(wide), 0.0)
    core = place_ref[1]
    mine_ref[...] = grad_ref[pl.ds(pl.multiple_of(core * half, half), half), :].astype(low)
    other_ref[...] = grad_ref[pl.ds(pl.multiple_of((1 - core) * half, half), half), :].astype(low)


def mask_bias(key_base, key_rows, q_index, q_start):
    keys = key_base + lax.broadcasted_iota(jnp.int32, (key_rows, q_index.shape[1]), 0)
    return jnp.where((keys >= q_start) & (keys <= q_index), 0.0, masked_value)


def first_row(lengths_ref, row):
    start = jnp.int32(0)
    end = jnp.int32(0)
    for i in range(lengths_ref.shape[1]):
        end = end + lengths_ref[0, i]
        start = jnp.where(row >= end, end, start)
    return start


def attend_kernel(blocks, lengths_ref, place_ref, q_ref, w_out_ref, *refs):
    kv_refs = refs[:blocks]
    out_ref, log_ref, mine_ref, other_ref, kv_ref, acc_ref, max_ref, bias_ref, part_ref, score_ref = refs[blocks:]
    rows = q_ref.shape[1]
    heads = q_ref.shape[0] // HEAD_DIM
    own, core = place_ref[0], place_ref[1]
    for r in range(blocks):
        kv_ref[r] = kv_refs[r][...]
    q_index = own * rows + lax.broadcasted_iota(jnp.int32, (1, rows), 1)
    q_start = segment_start(lengths_ref, q_index)
    acc_ref[...] = jnp.zeros_like(acc_ref)
    max_ref[...] = jnp.full_like(max_ref, masked_value)

    def visit(block, carry):
        pair = kv_ref[block ^ own]
        keys = pair[:, :HEAD_DIM]
        values = pair.astype(wide).T[HEAD_DIM:].astype(low)
        values = jnp.concatenate([values, jnp.ones((16, rows), low)], axis=0)
        bias_ref[...] = mask_bias(block * rows, rows, q_index, q_start)

        def scores(h):
            score_ref[h % 2] = dot_nn(keys, q_ref[h * HEAD_DIM : (h + 1) * HEAD_DIM, :])

        def gather(h, weight, shrink):
            acc_ref[h] = acc_ref[h] * shrink + dot_nn(values, weight)

        scores(0)
        waiting = None
        for h in range(heads):
            if h + 1 < heads:
                scores(h + 1)
            masked = score_ref[h % 2] + bias_ref[...]
            old = max_ref[h : h + 1, :]
            new = jnp.maximum(old, jnp.max(masked, axis=0, keepdims=True))
            weight = jnp.exp(masked - new).astype(low)
            max_ref[h : h + 1, :] = new
            if waiting is not None:
                gather(*waiting)
            waiting = (h, weight, jnp.exp(old - new))
        gather(*waiting)
        return carry

    lax.fori_loop(first_row(lengths_ref, own * rows) // rows, own + 1, visit, 0)
    for h in range(heads):
        total = acc_ref[h, HEAD_DIM : HEAD_DIM + 1, :]
        out_ref[h * HEAD_DIM : (h + 1) * HEAD_DIM, :] = acc_ref[h, :HEAD_DIM, :] / total
        log_ref[h : h + 1, :] = max_ref[h : h + 1, :] + jnp.log(total)
    part_ref[...] = dot_tn(w_out_ref[...], out_ref[...].astype(low))
    half = mine_ref.shape[1]
    mine_ref[...] = part_ref[:, pl.ds(pl.multiple_of(core * half, half), half)]
    other_ref[...] = part_ref[:, pl.ds(pl.multiple_of((1 - core) * half, half), half)].astype(low)


def middle_kernel(place_ref, tokens_ref, part_ref, passed_ref, gain_ref, hidden_ref, normed_ref):
    half = hidden_ref.shape[1]
    mine = pl.ds(pl.multiple_of(place_ref[1] * half, half), half)
    hidden = tokens_ref[:, mine].astype(wide) + part_ref[...] + passed_ref[...].astype(wide)
    hidden_ref[...] = hidden
    inverse = lax.rsqrt(jnp.mean(hidden * hidden, axis=0, keepdims=True) + epsilon)
    normed_ref[...] = (hidden * inverse * as_column(gain_ref[...])).astype(low)


def hidden_kernel(parts, *refs):
    gy_refs, x_refs, refs = refs[: 2 * parts], refs[2 * parts : 4 * parts], refs[4 * parts :]
    gate_t_ref, up_t_ref, down_ref, gate_ref, up_ref = refs[:5]
    mixed_ref, grad_gate_ref, grad_up_ref, other_ref, mine_ref, x_ref, gy_ref = refs[5:]
    half = other_ref.shape[1]
    row = 0
    for k in range(2):
        at = 0
        for x, gy in zip(x_refs[k * parts : (k + 1) * parts], gy_refs[k * parts : (k + 1) * parts]):
            x_ref[at : at + x.shape[0], k * half : (k + 1) * half] = x[...]
            gy_ref[row : row + gy.shape[0], :] = gy[...]
            at += x.shape[0]
            row += gy.shape[0]
    x = x_ref[...]
    gate = dot_nn(gate_t_ref[...], x)
    up = dot_nn(up_t_ref[...], x)
    grad_mixed = dot_nt(down_ref[...], gy_ref[...])
    sigmoid = 1.0 / (1.0 + jnp.exp(-gate))
    silu = gate * sigmoid
    mixed_ref[...] = (silu * up).astype(low)
    grad_gate = (grad_mixed * up * sigmoid * (1.0 + gate * (1.0 - sigmoid))).astype(low)
    grad_up = (grad_mixed * silu).astype(low)
    grad_gate_ref[...] = grad_gate
    grad_up_ref[...] = grad_up
    back = (dot_nn(gate_ref[...], grad_gate) + dot_nn(up_ref[...], grad_up)).astype(low)
    other_ref[...] = back[:, :half]
    mine_ref[...] = back[:, half:]


def weight_kernel(transposed, first, counts, outputs, *refs):
    blocks = len(counts)
    lefts, parts, out_refs, right_ref = refs[:blocks], refs[blocks : -outputs - 1], refs[-outputs - 1 : -1], refs[-1]
    units = lefts[0].shape[0]
    columns = sum(ref.shape[0] for ref in out_refs) // units * 128
    last = first + columns
    total, at = None, 0
    for r in range(blocks):
        row = 0
        for k in range(2):
            place = 0
            for part in parts[at : at + counts[r]]:
                if transposed:
                    half = part.shape[1]
                    start, end = max(place, first), min(place + part.shape[0], last)
                    if start < end:
                        right_ref[r, start - first : end - first, k * half : (k + 1) * half] = part[
                            start - place : end - place, :
                        ]
                    place += part.shape[0]
                else:
                    right_ref[r, row : row + part.shape[0], :] = part[:, first:last]
                    row += part.shape[0]
            at += counts[r]
        left, right = lefts[r][...], right_ref[r]
        product = dot_nt(left, right) if transposed else dot_nn(left, right)
        total = product if total is None else total + product
    at = 0
    for out_ref in out_refs:
        for t in range(out_ref.shape[0] // units):
            out_ref[t * units : (t + 1) * units, :] = total[:, at : at + 128].astype(low)
            at += 128


def project_kernel(blocks, weight_ref, *refs):
    other_ref, mine_refs = refs[blocks], refs[blocks + 1 :]
    half = other_ref.shape[2]
    for r in range(blocks):
        part = dot_nn(weight_ref[...], refs[r][...]).astype(low)
        other_ref[r] = part[:, :half]
        mine_refs[r][...] = part[:, half:]


def add_kernel(*refs):
    count = (len(refs) - 1) // 2
    for i in range(count):
        refs[1 + count + i][...] = (refs[1 + i][...].astype(wide) + refs[0][i].astype(wide)).astype(low)


def pair_kernel(*refs):
    count = len(refs) // 3
    for i in range(count):
        refs[2 * count + i][...] = (refs[2 * i][...].astype(wide) + refs[2 * i + 1][...].astype(wide)).astype(low)


def join_kernel(place_ref, mine_ref, other_ref, out_ref):
    half = mine_ref.shape[0]
    core = place_ref[1]
    out_ref[pl.ds(pl.multiple_of(core * half, half), half), :] = mine_ref[...].astype(out_ref.dtype)
    out_ref[pl.ds(pl.multiple_of((1 - core) * half, half), half), :] = other_ref[...].astype(out_ref.dtype)


def wait_kernel(*refs):
    pass


def tick_kernel(ops, place_ref, *refs):
    ins, outs = refs[: -len(ops)], refs[-len(ops) :]
    end = (place_ref[2] == 0) | (place_ref[2] == 3)
    for (kind, args), out_ref in zip(ops, outs):
        sources = [(ins if given else outs)[i] for given, i, *_ in args]
        if kind == "add":
            out_ref[...] = (sources[0][...].astype(wide) + sources[1][...].astype(wide)).astype(low)
        elif kind == "pick":
            out_ref[...] = jnp.where(end, sources[0][...], sources[1][...])
        else:
            at = 0
            for source, (_, _, start, rows) in zip(sources, args):
                out_ref[at : at + rows, :] = source[start : start + rows, :]
                at += rows


def sum_blocks(refs, starts=None, rows=None):
    total = None
    for i, ref in enumerate(refs):
        value = ref[...] if starts is None else ref[starts[i] : starts[i] + rows, :]
        total = value.astype(wide) if total is None else total + value.astype(wide)
    return total


def layer_kernel(hidden_ref, *refs):
    out_ref = refs[-1]
    out_ref[...] = (hidden_ref[...] + sum_blocks(refs[:-1])).T.astype(low)


def grad_middle_kernel(hidden_ref, gain_ref, gy_ref, *refs):
    grad_ref, grad_low_ref, grad_gain_ref = refs[-3:]
    hidden = hidden_ref[...]
    inverse = lax.rsqrt(jnp.mean(hidden * hidden, axis=0, keepdims=True) + epsilon)
    grad_normed = sum_blocks(refs[:-3])
    weighted = as_column(gain_ref[...]) * grad_normed
    inner = jnp.mean(weighted * hidden, axis=0, keepdims=True)
    grad = inverse * weighted - hidden * (inverse * inverse * inverse * inner)
    grad = grad + gy_ref[...].astype(wide).T
    grad_ref[...] = grad
    grad_low_ref[...] = grad.astype(low)
    grad_gain_ref[...] = as_row(jnp.sum(grad_normed * hidden * inverse, axis=1, keepdims=True))


def back_enter_kernel(
    place_ref, gm_mine_ref, gm_other_ref, w_out_ref, out_ref, go_ref, delta_ref, gm_ref
):
    half = gm_mine_ref.shape[1]
    core = place_ref[1]
    gm_ref[:, pl.ds(pl.multiple_of(core * half, half), half)] = gm_mine_ref[...]
    gm_ref[:, pl.ds(pl.multiple_of((1 - core) * half, half), half)] = gm_other_ref[...]
    grad_out = dot_nn(w_out_ref[...], gm_ref[...]).astype(low)
    go_ref[...] = grad_out
    product = grad_out.astype(wide) * out_ref[...]
    for h in range(product.shape[0] // HEAD_DIM):
        delta_ref[h : h + 1, :] = jnp.sum(
            product[h * HEAD_DIM : (h + 1) * HEAD_DIM], axis=0, keepdims=True
        )


def attend_back_kernel(
    blocks, lengths_ref, place_ref, go_ref, delta_ref, log_ref, q_ref, cos_ref, sin_ref, *refs,
):
    kv_refs, refs = refs[:blocks], refs[blocks:]
    (grad_q_ref, *grad_kv_refs), refs = refs[: blocks + 1], refs[blocks + 1 :]
    kv_ref, bias_ref, dq_ref, q_all_ref, go_all_ref, weight_ref, grad_ref, grad_kv_ref, score_ref, grad_weight_ref = refs
    rows = q_ref.shape[1]
    heads = grad_q_ref.shape[0] // HEAD_DIM
    own = place_ref[0]

    def lanes(h):
        return slice(h * rows, (h + 1) * rows)

    def span(h):
        return slice(h * HEAD_DIM, (h + 1) * HEAD_DIM)

    for r in range(blocks):
        kv_ref[r] = kv_refs[r][...]
        grad_kv_ref[r] = jnp.zeros_like(grad_kv_ref[r])
    for h in range(heads):
        q_all_ref[:, lanes(h)] = q_ref[span(h), :]
        go_all_ref[:, lanes(h)] = go_ref[span(h), :]
    dq_ref[...] = jnp.zeros_like(dq_ref)
    q_index = own * rows + lax.broadcasted_iota(jnp.int32, (1, rows), 1)
    q_start = segment_start(lengths_ref, q_index)

    def visit(block, carry):
        pair = kv_ref[block ^ own]
        keys = pair[:, :HEAD_DIM]
        values = pair[:, HEAD_DIM:]
        keys_t = pair.astype(wide).T[:HEAD_DIM].astype(low)
        bias_ref[...] = mask_bias(block * rows, rows, q_index, q_start)

        def products(h):
            score_ref[h % 2] = dot_nn(keys, q_all_ref[:, lanes(h)])
            grad_weight_ref[h % 2] = dot_nn(values, go_all_ref[:, lanes(h)])

        products(0)
        for h in range(heads):
            if h + 1 < heads:
                products(h + 1)
            weight = jnp.exp(score_ref[h % 2] + bias_ref[...] - log_ref[h : h + 1, :])
            grad = (weight * (grad_weight_ref[h % 2] - delta_ref[h : h + 1, :])).astype(low)
            weight_ref[:, lanes(h)] = weight.astype(low)
            grad_ref[:, lanes(h)] = grad
            dq_ref[span(h), :] += dot_nn(keys_t, grad)
        grad_keys = dot_nt(grad_ref[...], q_all_ref[...])
        grad_values = dot_nt(weight_ref[...], go_all_ref[...])
        grad_kv_ref[block ^ own] = jnp.concatenate([grad_keys, grad_values], axis=1).astype(low)
        return carry

    lax.fori_loop(first_row(lengths_ref, own * rows) // rows, own + 1, visit, 0)
    for r in range(blocks):
        grad_kv_refs[r][...] = grad_kv_ref[r]
    for h in range(heads):
        turned = rotate(dq_ref[span(h), :] * HEAD_DIM**-0.5, cos_ref[...], -sin_ref[...])
        grad_q_ref[span(h), :] = turned.astype(low)


def query_kernel(
    place_ref, normed_ref, grad_q_ref, wq_ref, gm_mine_ref, gm_other_ref, out_ref,
    grad_wq_ref, part_ref, grad_bq_ref, grad_w_out_ref, gm_ref,
):
    half = gm_mine_ref.shape[1]
    core = place_ref[1]
    gm_ref[:, pl.ds(pl.multiple_of(core * half, half), half)] = gm_mine_ref[...]
    gm_ref[:, pl.ds(pl.multiple_of((1 - core) * half, half), half)] = gm_other_ref[...]
    grad_w_out_ref[...] = dot_nt(out_ref[...].astype(low), gm_ref[...]).astype(low)
    grad_q = grad_q_ref[...]
    grad_wq_ref[...] = dot_nt(grad_q, normed_ref[...]).astype(low)
    part_ref[...] = dot_tn(wq_ref[...], grad_q)
    grad_bq_ref[...] = dot_nt(jnp.ones((16, grad_q.shape[1]), low), grad_q)


def key_kernel(
    blocks, starts, place_ref, normed_ref, tokens_ref, part_ref, wk_ref, wv_ref, cos_ref, sin_ref,
    grad_wq_ref, grad_bq_ref, grad_w_out_ref, grad_gain_two_ref, *refs,
):
    kv_refs, share_refs, (mine_ref, other_ref, sum_ref, pack_ref) = refs[:blocks], refs[blocks : 2 * blocks], refs[2 * blocks :]
    both = sum_blocks(kv_refs, starts, tokens_ref.shape[1]).T
    both = jnp.concatenate(
        [rotate(both[:HEAD_DIM], cos_ref[...], -sin_ref[...]), both[HEAD_DIM:]], axis=0
    ).astype(low)
    total = part_ref[...] + dot_tn(wk_ref[...], both[:HEAD_DIM]) + dot_tn(wv_ref[...], both[HEAD_DIM:])
    sum_ref[...] = total
    half = mine_ref.shape[1]
    core = place_ref[1]
    mine_ref[...] = sum_ref[:, pl.ds(pl.multiple_of(core * half, half), half)]
    other_ref[...] = sum_ref[:, pl.ds(pl.multiple_of((1 - core) * half, half), half)].astype(low)
    hidden = tokens_ref[...].astype(wide)
    inverse = lax.rsqrt(jnp.mean(hidden * hidden, axis=0, keepdims=True) + epsilon)
    q_width, width = grad_wq_ref.shape
    kv_width = both.shape[0]
    at = 0
    pack_ref[at : at + q_width, :] = grad_wq_ref[...]
    at += q_width
    pack_ref[at : at + kv_width, :] = dot_nt(both, normed_ref[...]).astype(low)
    at += kv_width
    pack_ref[at : at + q_width, :] = grad_w_out_ref[...]
    at += q_width
    grad_gain = as_row(jnp.sum(total * (hidden * inverse), axis=1, keepdims=True))
    grad_bkv = dot_nt(jnp.ones((16, both.shape[1]), low), both)[:1]
    biases = jnp.concatenate(
        [grad_bq_ref[:1, :], grad_bkv, jnp.zeros((1, width - q_width - kv_width), wide)], axis=1
    )
    small = jnp.concatenate(
        [grad_gain, grad_gain_two_ref[...], biases, jnp.zeros((pack_ref.shape[0] - at - 3, width), wide)], axis=0
    )
    pack_ref[at:, :] = small.astype(low)
    share = pack_ref.shape[0] // blocks
    for r in range(blocks):
        start = pl.multiple_of((place_ref[0] ^ r) * share, share)
        for t in range(width // 128):
            share_refs[r][t * share : (t + 1) * share, :] = pack_ref[pl.ds(start, share), t * 128 : (t + 1) * 128]


def share_kernel(starts, *refs):
    refs[-1][...] = sum_blocks(refs[:-1], starts, refs[-1].shape[0]).astype(low)


def unpack_kernel(share, sources, place_ref, *refs):
    pieces, outs, (stack_ref, pack_ref) = refs[: len(sources)], refs[len(sources) : -2], refs[-2:]
    for ref, (r, first, rows, start) in zip(pieces, sources):
        stack_ref[r, first : first + rows, :] = ref[start : start + rows, :].astype(wide)
    for r in range(stack_ref.shape[0]):
        at = pl.ds(pl.multiple_of((place_ref[0] ^ r) * share, 8), share)
        for t in range(stack_ref.shape[1] // share):
            pack_ref[at, t * 128 : (t + 1) * 128] = stack_ref[r, t * share : (t + 1) * share, :]
    at = 0
    for out_ref in outs:
        out_ref[...] = pack_ref[at : at + out_ref.shape[0], :]
        at += out_ref.shape[0]


def leave_kernel(place_ref, tokens_ref, mine_ref, passed_ref, gain_ref, grad_mid_ref, out_ref):
    half = mine_ref.shape[1]
    hidden = tokens_ref[:, pl.ds(pl.multiple_of(place_ref[1] * half, half), half)].astype(wide)
    inverse = lax.rsqrt(jnp.mean(hidden * hidden, axis=0, keepdims=True) + epsilon)
    weighted = as_column(gain_ref[...]) * (mine_ref[...] + passed_ref[...].astype(wide))
    inner = jnp.mean(weighted * hidden, axis=0, keepdims=True)
    grad = grad_mid_ref[...] + inverse * weighted - hidden * (inverse * inverse * inverse * inner)
    out_ref[...] = grad.T.astype(low)


def place_kernel(transposed, tiles, place_ref, refs, out_ref, all_ref):
    own_ref, near_x_ref, near_y_ref, *far_refs = refs
    step, tiles = tiles
    units = own_ref.shape[0]
    half = units // 2
    for r, ref in enumerate((own_ref, near_x_ref, near_y_ref)):
        start = pl.multiple_of((place_ref[0] ^ r) * units, 8)
        all_ref[pl.ds(start, units), :] = ref[...].astype(wide)
    for k in range(2):
        start = pl.multiple_of((place_ref[0] ^ 3) * units + k * half, 8)
        part = 2 * step + k

        @pl.when(part < tiles)
        def _(start=start, k=k):
            all_ref[pl.ds(start, half), :] = far_refs[k][...].astype(wide)

        @pl.when(part >= tiles)
        def _(start=start, k=k):
            all_ref[pl.ds(start, half), :] = far_refs[2 + k][...].astype(wide)

    if transposed:
        out_ref[...] = all_ref[...].T


def place_shares(place, shares, units, transposed, width, at, whole, last):
    tile, half = 128, units // 2
    counts = [share[0].shape[0] // units for share in shares]
    begins = [sum(counts[:i]) for i in range(len(counts))]
    first = at // tile
    ins, specs = [place], [in_smem]
    for (own, near_x, near_y, far_y, far_x), tiles, begin in zip(shares, counts, begins):

        def step_of(i, tiles=tiles, begin=begin):
            return jnp.clip(i - begin, 0, tiles - 1)

        def halves(start, k, later, tiles=tiles, step_of=step_of):
            def index(i):
                part = 2 * step_of(i) + k - (tiles if later else 0)
                return (start // half + jnp.clip(part, 0, tiles - 1), 0)

            return pl.BlockSpec((half, tile), index)

        ins += [own, near_x, near_y, far_y[0], far_y[0], far_x[0], far_x[0]]
        specs += [pl.BlockSpec((units, tile), lambda i, step_of=step_of: (step_of(i), 0))] * 3
        specs += [halves(far_y[1], k, False) for k in range(2)]
        specs += [halves(far_x[1], k, True) for k in range(2)]
    ins += last
    specs += [pl.BlockSpec(memory_space=pl.ANY)] * len(last)
    aliases = {}
    if whole is not None:
        aliases = {len(ins): 0}
        ins.append(whole)
        specs.append(pl.BlockSpec(memory_space=pl.ANY))

    def body(*refs):
        out_ref, token_ref = refs[len(ins) : len(ins) + 2]
        all_ref = refs[-1] if transposed else out_ref
        token_ref[...] = jnp.zeros_like(token_ref)
        for n, (tiles, begin) in enumerate(zip(counts, begins)):
            step = pl.program_id(0) - begin

            @pl.when((step >= 0) & (step < tiles))
            def _(n=n, step=step, tiles=tiles):
                place_kernel(transposed, (step, tiles), refs[0], refs[1 + 7 * n : 8 + 7 * n], out_ref, all_ref)

    if transposed:
        dims = (width, 4 * units)
        out_spec = pl.BlockSpec((tile, 4 * units), lambda i: (i + first, 0))
        scratch = [pltpu.VMEM((4 * units, tile), wide)]
    else:
        dims = (4 * units, width)
        out_spec = pl.BlockSpec((4 * units, tile), lambda i: (0, i + first))
        scratch = []
    return pl.pallas_call(
        body,
        name="place_kernel",
        out_shape=(shape(dims, wide), shape((8, 128), wide)),
        grid=(sum(counts),),
        in_specs=specs,
        out_specs=(out_spec, pl.BlockSpec((8, 128), lambda i: (0, 0))),
        scratch_shapes=scratch,
        input_output_aliases=aliases,
        cost_estimate=pl.CostEstimate(flops=0, bytes_accessed=0, transcendentals=0),
        compiler_params=pltpu.CompilerParams(vmem_limit_bytes=vmem_limit),
    )(*ins)


def local(
    tokens,
    lengths,
    norm1_gain,
    w_query,
    b_query,
    w_key,
    b_key,
    w_value,
    b_value,
    w_out,
    norm2_gain,
    w_gate,
    w_up,
    w_down,
    cotangent,
):
    rows, width = tokens.shape
    half = rows // 2
    blocks = lax.axis_size("blk")
    own_block = lax.axis_index("blk")
    own_core = lax.axis_index("tensor")
    q_width = w_query.shape[1]
    heads = q_width // HEAD_DIM
    units = w_gate.shape[1] // blocks
    place = jnp.stack([own_block, own_core, lax.axis_index("dp")]).astype(jnp.int32)
    gain_two = norm2_gain.reshape(1, width)

    half_dim = HEAD_DIM // 2
    turn = (rope_base ** (-2.0 * jnp.arange(half_dim, dtype=wide) / HEAD_DIM)).reshape(half_dim, 1)
    q_t, key_value, normed_t, tokens_t, cosine, sine = call(
        enter_kernel,
        [
            shape((q_width, rows), low),
            shape((rows, 2 * HEAD_DIM), low),
            shape((width, rows), low),
            shape((width, rows), low),
            shape((half_dim, rows), wide),
            shape((half_dim, rows), wide),
        ],
        [
            lengths, place, tokens, norm1_gain.reshape(1, width), w_query.T, w_key.T, w_value.T,
            b_query.reshape(1, -1), b_key.reshape(1, -1), b_value.reshape(1, -1), turn,
        ],
        in_specs=[in_smem] * 2 + [in_vmem] * 9,
    )
    kv_blocks = gather_blocks(key_value, "kv")

    down_own = lax.dynamic_slice_in_dim(w_down, own_block * units, units, 0)
    window = -(-(units + 127) // 128) * 128
    gate_t, gate_own, up_t, up_own, down_t, grad_y_mine, grad_y_other = call(
        weights_kernel,
        [
            shape((units, width), low),
            shape((width, units), low),
            shape((units, width), low),
            shape((width, units), low),
            shape((width, units), low),
            shape((half, width), low),
            shape((half, width), low),
        ],
        [lengths, place, w_gate, w_up, down_own, cotangent],
        [pltpu.VMEM((window, width), wide), pltpu.VMEM((rows, width), wide)],
        in_specs=[in_smem] * 2 + [in_vmem] * 4,
        after=[q_t],
    )
    gy_near = {r: partner(grad_y_mine, "blk", r, "gy") for r in range(1, blocks) if r & (r - 1) == 0}

    out_t, log_total, part_mine, part_other = call(
        functools.partial(attend_kernel, blocks),
        [
            shape((q_width, rows), wide),
            shape((heads + 1, rows), wide),
            shape((width, half), wide),
            shape((width, half), low),
        ],
        [lengths, place, q_t, w_out] + kv_blocks,
        [
            pltpu.VMEM((blocks, rows, 2 * HEAD_DIM), low),
            pltpu.VMEM((heads, HEAD_DIM + 16, rows), wide),
            pltpu.VMEM((heads + 1, rows), wide),
            pltpu.VMEM((rows, rows), wide),
            pltpu.VMEM((width, rows), wide),
            pltpu.VMEM((2, rows, rows), wide),
        ],
        in_specs=[in_smem] * 2 + [in_vmem] * (2 + blocks),
        after=[gate_t],
    )
    hidden, normed_two = call(
        middle_kernel,
        [shape((width, half), wide), shape((width, half), low)],
        [place, tokens_t, part_mine, partner(part_other, "tensor", 1, "part_core"), gain_two],
        in_specs=[in_smem] + [in_vmem] * 4,
        after=list(gy_near.values()),
    )

    last = [normed_two]

    def ordered(body, outs, ins, needs=(), **more):
        nonlocal last
        carry = more.get("carry", ())
        after = [v for v in last + list(needs) if not any(v is c for c in carry)]
        results = call(body, outs, ins, after=after, **more)
        last = [results[0]]
        return results

    def wait(carry, needs=()):
        return list(ordered(wait_kernel, [], [], needs=needs, carry=carry))

    def near(pieces):
        return [p for r, parts in enumerate(pieces) if r and r & (r - 1) == 0 for p in parts]

    def far(pieces):
        return [p for r, parts in enumerate(pieces) if r & (r - 1) for p in parts]

    kept = shape((units, rows), low)
    piece = shape((width, half), low)
    runs, back, passed = [], [None] * blocks, [None] * blocks

    def cores(parts, name):
        return [partner(part, "tensor", 1, name) for part in parts]

    x_parts, gy_parts = [], []

    def hidden_units(r, x_mine, x_other, gy_mine, gy_other):
        x_parts.append(x_other + x_mine)
        gy_parts.append(gy_other + gy_mine)
        runs.append(
            ordered(
                functools.partial(hidden_kernel, len(x_mine)),
                [kept, kept, kept, piece, piece],
                gy_parts[-1] + x_parts[-1] + [gate_t, up_t, down_own, gate_own, up_own],
                scratch=[pltpu.VMEM((width, rows), low), pltpu.VMEM((rows, width), low)],
            )
        )
        return runs[-1][3]

    def add_back(members, carry, needs=()):
        results = ordered(
            pair_kernel,
            [piece] * len(members),
            [value for r in members for value in (runs[r][4], passed[r])],
            needs=needs,
            carry=carry,
        )
        for r, value in zip(members, results):
            back[r] = partner(value, "blk", r, "back") if r else value
        return results[len(members) :]

    def hidden_weight(transposed, left, parts, first, shares):
        counts = [len(part) // 2 for part in parts]
        columns = sum(shares)
        dims = (columns, rows) if transposed else (rows, columns)
        return ordered(
            functools.partial(weight_kernel, transposed, first, counts, len(shares)),
            [shape((share // 128 * units, 128), low) for share in shares],
            [run[left] for run in runs] + sum(parts, []),
            scratch=[pltpu.VMEM((blocks,) + dims, low)],
        )

    def tick(ops, needs=(), carry=()):
        given, outs, listed = [], [], []
        for kind, *args in ops:
            spans = [arg if isinstance(arg, tuple) else (arg, 0, None) for arg in args]
            named, size = [], 0
            for value, start, count in spans:
                if isinstance(value, int):
                    entry, total = (False, value), outs[value].shape[0]
                else:
                    found = [i for i, known in enumerate(given) if known is value]
                    if not found:
                        given.append(value)
                    entry = (True, found[0] if found else len(given) - 1)
                    total = value.shape[0]
                count = total if count is None else count
                named.append(entry + (start, count))
                size = size + count if kind == "cat" else count
            listed.append((kind, named))
            outs.append(shape((size, 128), low))
        return ordered(
            functools.partial(tick_kernel, listed),
            outs,
            [place] + given,
            in_specs=[in_smem] + [in_vmem] * len(given),
            needs=needs,
            carry=carry,
        )

    x_near = {r: partner(normed_two, "blk", r, "x") for r in range(1, blocks) if r & (r - 1) == 0}
    other = hidden_units(
        0, [normed_two], cores([normed_two], "x_core"), [grad_y_mine], [grad_y_other]
    )
    other, *arrived = wait([other] + list(x_near.values()))
    passed[0] = partner(other, "tensor", 1, "back_core")
    x_near = dict(zip(x_near, arrived))
    x_mine = relay_far(x_near, normed_two, "x")
    gy_mine = relay_far(gy_near, grad_y_mine, "gy")
    x_other = {r: cores(parts, "x_core") for r, parts in x_mine.items() if r in x_near}
    gy_other = {r: cores(parts, "gy_core") for r, parts in gy_mine.items() if r in x_near}
    waiting, out_of = [], list(range(1, blocks))
    for i, r in enumerate(out_of):
        other = hidden_units(r, x_mine[r], x_other[r], gy_mine[r], gy_other[r])
        ready = [k for k in out_of if k not in x_near] if i == 0 else []
        fars = [part for k in ready for part in x_mine[k] + gy_mine[k]]
        if i == 0:
            other, *fars = wait([other] + fars)
        else:
            other, *fars = add_back([out_of[i - 1]], [other])
        passed[r] = partner(other, "tensor", 1, "back_core")
        for k in ready:
            count = len(x_mine[k])
            x_mine[k], fars = fars[:count], fars[count:]
            count = len(gy_mine[k])
            gy_mine[k], fars = fars[:count], fars[count:]
            x_other[k] = cores(x_mine[k], "x_core")
            gy_other[k] = cores(gy_mine[k], "gy_core")
    cut_at = width // 2 // 128 * 128
    (d1,) = hidden_weight(False, 0, gy_parts, 0, [cut_at])
    d1_swap = swap(d1, "swap_d1")
    (d2,) = hidden_weight(False, 0, gy_parts, cut_at, [width - cut_at])
    layer_other, *layer_mine = ordered(
        functools.partial(project_kernel, blocks),
        [shape((blocks, width, half), low)] + [piece] * blocks,
        [down_t] + [run[0] for run in runs],
    )
    d2, layer_other = add_back(
        [blocks - 1, 0], [d2, layer_other], needs=back[1 : blocks - 1] + [d1_swap]
    )
    (d1_sum,) = tick([("add", d1, d1_swap)])
    d1_cross, d2_swap = cross(d1_sum, "cross_d1"), swap(d2, "swap_d2")
    layer_passed = partner(layer_other, "tensor", 1, "layer_core")
    g1, g2 = hidden_weight(True, 1, x_parts, 0, [cut_at, width - cut_at])
    u1, u2 = hidden_weight(True, 2, x_parts, 0, [cut_at, width - cut_at])
    d1_sum, d2_sum, d1_g1 = tick(
        [("add", d1_sum, d1_cross), ("add", d2, d2_swap), ("pick", g1, 0)], needs=back[1:]
    )
    grad_mid, grad_mid_low, grad_gain_two = ordered(
        grad_middle_kernel,
        [shape((width, half), wide), piece, shape((1, width), wide)],
        [hidden, gain_two, grad_y_mine] + back,
    )
    *layer_pieces, grad_mid_low, d1_g1, d2_sum = ordered(
        add_kernel, [piece] * blocks, [layer_passed] + layer_mine, carry=[grad_mid_low, d1_g1, d2_sum]
    )
    grad_mid_other = partner(grad_mid_low, "tensor", 1, "mid_core")
    layer_pieces = scatter_blocks(layer_pieces, "layer")
    d1_g1_swap, d2_cross = swap(d1_g1, "swap_d1_g1"), cross(d2_sum, "cross_d2")

    grad_out, delta = ordered(
        back_enter_kernel,
        [shape((q_width, rows), low), shape((heads + 1, rows), wide)],
        [place, grad_mid_low, grad_mid_other, w_out, out_t],
        scratch=[pltpu.VMEM((width, rows), low)],
        in_specs=[in_smem] + [in_vmem] * 4,
    )

    grad_q, *grad_kv = ordered(
        functools.partial(attend_back_kernel, blocks),
        [shape((q_width, rows), low)] + [shape((rows, 2 * HEAD_DIM), low)] * blocks,
        [lengths, place, grad_out, delta, log_total, q_t, cosine, sine] + kv_blocks,
        scratch=[
            pltpu.VMEM((blocks, rows, 2 * HEAD_DIM), low),
            pltpu.VMEM((rows, rows), wide),
            pltpu.VMEM((q_width, rows), wide),
            pltpu.VMEM((HEAD_DIM, heads * rows), low),
            pltpu.VMEM((HEAD_DIM, heads * rows), low),
            pltpu.VMEM((rows, heads * rows), low),
            pltpu.VMEM((rows, heads * rows), low),
            pltpu.VMEM((blocks, rows, 2 * HEAD_DIM), low),
            pltpu.VMEM((2, rows, rows), wide),
            pltpu.VMEM((2, rows, rows), wide),
        ],
        in_specs=[in_smem] * 2 + [in_vmem] * (6 + blocks),
    )
    pack_rows = -(-(2 * q_width + 2 * HEAD_DIM + 3) // (16 * blocks)) * 16 * blocks
    share = pack_rows // blocks
    stack_rows = share * (width // 128)

    def query_back():
        return ordered(
            query_kernel,
            [
                shape((q_width, width), low),
                shape((width, rows), wide),
                shape((16, q_width), wide),
                shape((q_width, width), low),
            ],
            [place, normed_t, grad_q, w_query.T, grad_mid_low, grad_mid_other, out_t],
            scratch=[pltpu.VMEM((width, rows), low)],
            in_specs=[in_smem] + [in_vmem] * 6,
        )

    def key_back(kv_pieces, starts):
        return ordered(
            functools.partial(key_kernel, blocks, starts),
            [shape((stack_rows, 128), low)] * blocks + [shape((width, half), wide), shape((width, half), low)],
            [
                place, normed_t, tokens_t, normed_part, w_key.T, w_value.T, cosine, sine,
                grad_w_query, grad_b_query, grad_w_out, grad_gain_two,
            ] + kv_pieces,
            scratch=[pltpu.VMEM((width, rows), wide), pltpu.VMEM((pack_rows, width), low)],
            in_specs=[in_smem] + [in_vmem] * (11 + blocks),
        )

    def sum_share(pieces, starts):
        (own,) = ordered(
            functools.partial(share_kernel, starts), [shape((stack_rows, 128), low)], pieces
        )
        return own

    def leave(normed_mine, normed_passed):
        (grad_half,) = ordered(
            leave_kernel,
            [shape((half, width), low)],
            [place, tokens_t, normed_mine, normed_passed, norm1_gain.reshape(1, width), grad_mid],
            in_specs=[in_smem] + [in_vmem] * 5,
        )
        return grad_half

    def join(mine, other, kind):
        (whole,) = ordered(
            join_kernel,
            [shape((rows, width), kind)],
            [place, mine.astype(kind), other.astype(kind)],
            in_specs=[in_smem] + [in_vmem] * 2,
        )
        return whole

    def layer_leave():
        (layer_half,) = ordered(layer_kernel, [shape((half, width), low)], [hidden] + layer_pieces)
        return layer_half

    def unpack(pieces, sources):
        return ordered(
            functools.partial(unpack_kernel, share, sources),
            [
                shape((q_width, width), wide),
                shape((HEAD_DIM, width), wide),
                shape((HEAD_DIM, width), wide),
                shape((q_width, width), wide),
                shape((pack_rows - 2 * q_width - 2 * HEAD_DIM, width), wide),
            ],
            [place] + pieces,
            scratch=[pltpu.VMEM((blocks, stack_rows, 128), wide), pltpu.VMEM((pack_rows, width), wide)],
            in_specs=[in_smem] + [in_vmem] * len(pieces),
        )

    if blocks != 4:
        kv_pieces = scatter_blocks(grad_kv, "grad_kv")
        grad_w_query, normed_part, grad_b_query, grad_w_out = query_back()
        *shares, normed_mine, normed_other = key_back(kv_pieces, [0] * blocks)
        layer_half = layer_leave()
        layer_out = join(layer_half, partner(layer_half, "tensor", 1, "rows_core"), low)
        grad_half = leave(normed_mine, partner(normed_other, "tensor", 1, "normed_core"))
        grad_tokens = join(grad_half, partner(grad_half, "tensor", 1, "rows_core"), wide)
        own_share = sum_share(scatter_blocks(shares, "shares"), [0] * blocks)
        own_share = lax.psum(own_share, "dp")
        pieces = gather_blocks(own_share, "all_share")
        grad_w_query, grad_w_key, grad_w_value, grad_w_out, small = unpack(
            pieces, [(r, 0, stack_rows, 0) for r in range(blocks)]
        )

        def gather_weight(first, second, transposed):
            stacked = lax.psum(jnp.concatenate([first, second], axis=0), "dp")
            every = lax.all_gather(stacked, "blk").reshape(blocks, width // 128, units, 128)
            order = (1, 3, 0, 2) if transposed else (0, 2, 1, 3)
            dims = (width, blocks * units) if transposed else (blocks * units, width)
            return every.transpose(order).reshape(dims).astype(wide)

        grad_w_down = gather_weight(d1, d2, False)
        grad_w_gate = gather_weight(g1, g2, True)
        grad_w_up = gather_weight(u1, u2, True)
    else:
        r1, r2 = d1.shape[0], d2.shape[0]
        h1, h2 = r1 // 2, r2 // 2

        def both_ways(x_buffer, y_buffer, name):
            return partner(x_buffer, "blk", 1, name + "_x"), partner(y_buffer, "blk", 2, name + "_y")

        d1_all, g1_sum, d2_sum, d2_g2, x1, y1, kv_far = tick(
            [
                ("pick", d1_g1_swap, d1_sum),
                ("add", g1, d1_g1_swap),
                ("add", d2_sum, d2_cross),
                ("pick", g2, 2),
                ("cat", 0, grad_kv[1]),
                ("cat", 0, grad_kv[2]),
            ],
            needs=layer_pieces[1:],
            carry=[grad_kv[3]],
        )
        x1, y1 = both_ways(x1, y1, "d1")
        kv_far = partner(kv_far, "blk", 3, "grad_kv")
        d2_g2_swap, g1_cross = swap(d2_g2, "swap_d2_g2"), cross(g1_sum, "cross_g1")
        grad_w_query, normed_part, grad_b_query, grad_w_out = query_back()
        layer_half = layer_leave()
        d2_all, g2_sum, g1_sum, g1_u1, x2, y2, layer_half = tick(
            [
                ("pick", d2_g2_swap, d2_sum),
                ("add", g2, d2_g2_swap),
                ("add", g1_sum, g1_cross),
                ("pick", u1, 2),
                ("cat", 0, (y1, h1, h1)),
                ("cat", 0, (x1, 0, h1)),
            ],
            needs=[x1, y1, kv_far],
            carry=[layer_half],
        )
        x2, y2 = both_ways(x2, y2, "d2")
        g1_u1_swap, g2_cross = swap(g1_u1, "swap_g1_u1"), cross(g2_sum, "cross_g2")
        layer_passed = partner(layer_half, "tensor", 1, "rows_core")
        *shares, normed_mine, normed_other = key_back([grad_kv[0], x1, y1, kv_far], [0, r1, r1, 0])
        g1_all, u1_sum, g2_sum, g2_u2, x3, y3, share_far, normed_other = tick(
            [
                ("pick", g1_u1_swap, g1_sum),
                ("add", u1, g1_u1_swap),
                ("add", g2_sum, g2_cross),
                ("pick", u2, 2),
                ("cat", 0, (y2, h2, h2), shares[1]),
                ("cat", 0, (x2, 0, h2), shares[2]),
            ],
            needs=[x2, y2],
            carry=[shares[3], normed_other],
        )
        x3, y3 = both_ways(x3, y3, "g1")
        share_far = partner(share_far, "blk", 3, "shares")
        g2_u2_swap, u1_cross = swap(g2_u2, "swap_g2_u2"), cross(u1_sum, "cross_u1")
        normed_passed = partner(normed_other, "tensor", 1, "normed_core")
        layer_out = join(layer_half, layer_passed, low)
        grad_half = leave(normed_mine, normed_passed)
        own_share = sum_share([shares[0], x3, y3, share_far], [0, r1 + h2, r1 + h2, 0])
        g2_all, u2_sum, u1_sum, x4, y4, own_share, grad_half = tick(
            [
                ("pick", g2_u2_swap, g2_sum),
                ("add", u2, g2_u2_swap),
                ("add", u1_sum, u1_cross),
                ("cat", 0, (y3, h1, h1)),
                ("cat", 0, (x3, 0, h1)),
            ],
            carry=[own_share, grad_half],
        )
        x4, y4 = both_ways(x4, y4, "g2")
        share_swap = swap(own_share, "swap_share")
        u1_swap, u2_cross = swap(u1_sum, "swap_u1"), cross(u2_sum, "cross_u2")
        grad_passed = partner(grad_half, "tensor", 1, "rows_core")
        d_shares = [(d1_all, x1, y1, (y2, r2), (x2, r2)), (d2_all, x2, y2, (y3, r1), (x3, r1))]
        grad_w_down, *last = place_shares(place, d_shares, units, False, width, 0, None, last)
        u1_all, u2_sum, own_share, x5, y5 = tick(
            [
                ("pick", u1_swap, u1_sum),
                ("add", u2_sum, u2_cross),
                ("add", own_share, share_swap),
                ("cat", 0, (y4, h2, h2)),
                ("cat", 0, (x4, 0, h2)),
            ],
            needs=[x4, y4],
        )
        x5, y5 = both_ways(x5, y5, "u1")
        u2_swap, share_swap = swap(u2_sum, "swap_u2"), partner(own_share, "dp", 2, "share_far")
        u2_all, own_share, x6, y6 = tick(
            [
                ("pick", u2_swap, u2_sum),
                ("add", own_share, share_swap),
                ("cat", 0, (y5, h1, h1), 1),
                ("cat", 0, (x5, 0, h1), 1),
            ],
            needs=[x5, y5],
        )
        x6, y6 = both_ways(x6, y6, "u2")
        grad_tokens = join(grad_half, grad_passed, wide)
        g_shares = [(g1_all, x3, y3, (y4, r2), (x4, r2)), (g2_all, x4, y4, (y5, r1), (x5, r1))]
        grad_w_gate, *last = place_shares(place, g_shares, units, True, width, 0, None, last)
        first_half = stack_rows // 32 * 16
        share_at = r2 + h1
        far = tick(
            [
                ("cat", (y6, share_at + first_half, stack_rows - first_half)),
                ("cat", (x6, share_at, first_half)),
                ("cat", (y6, h2, h2)),
                ("cat", (x6, 0, h2)),
            ],
        )
        share_x, share_y = both_ways(far[0], far[1], "far_share")
        x7, y7 = both_ways(far[2], far[3], "far_u2")
        u_shares = [(u1_all, x5, y5, (y6, r2), (x6, r2)), (u2_all, x6, y6, (y7, 0), (x7, 0))]
        grad_w_up, *last = place_shares(place, u_shares[:1], units, True, width, 0, None, last)
        grad_w_query, grad_w_key, grad_w_value, grad_w_out, small = unpack(
            [own_share, x6, y6, share_y, share_x],
            [
                (0, 0, stack_rows, 0),
                (1, 0, stack_rows, share_at),
                (2, 0, stack_rows, share_at),
                (3, 0, first_half, 0),
                (3, first_half, stack_rows - first_half, 0),
            ],
        )
        grad_w_up, _ = place_shares(
            place, u_shares[1:], units, True, width, cut_at, grad_w_up, [small]
        )
    gains = small[:2]
    gains = gains + partner(gains, "tensor", 1, "gains_core")
    grad_b = small[2]
    return (
        layer_out,
        grad_tokens,
        gains[0],
        grad_w_query.T,
        grad_b[:q_width],
        grad_w_key.T,
        grad_b[q_width : q_width + HEAD_DIM],
        grad_w_value.T,
        grad_b[q_width + HEAD_DIM : q_width + 2 * HEAD_DIM],
        grad_w_out,
        gains[1],
        grad_w_gate,
        grad_w_up,
        grad_w_down,
    )


def solution(mesh):
    placed = (
        P(("dp", "blk"), None),
        P("dp", None),
        P(),
        P(None, "tensor"),
        P("tensor"),
        P(None, "tensor"),
        P("tensor"),
        P(None, "tensor"),
        P("tensor"),
        P("tensor", None),
        P(),
        P(None, "tensor"),
        P(None, "tensor"),
        P("tensor", None),
        P(("dp", "blk"), None),
    )
    return jax.shard_map(
        local,
        mesh=mesh,
        in_specs=placed,
        out_specs=(
            P(("dp", "blk"), None),
            P(("dp", "blk"), None),
            P(),
            P(None, "tensor"),
            P("tensor"),
            P(None, "tensor"),
            P("tensor"),
            P(None, "tensor"),
            P("tensor"),
            P("tensor", None),
            P(),
            P(None, "tensor"),
            P(None, "tensor"),
            P("tensor", None),
        ),
        check_vma=False,
    )
```

```python
import functools
import math

import jax
import jax.numpy as jnp
from jax import lax
from jax.experimental import pallas as pl
from jax.experimental.pallas import tpu as pltpu
from jax.sharding import PartitionSpec as P

HEAD_DIM = 64

epsilon = 1e-06
rope_base = 1000000.0
masked_value = -1e30

low = jnp.bfloat16
wide = jnp.float32
vmem_limit = 40 * 1024 * 1024


def dot_nn(left, right):
    return lax.dot_general(left, right, (((1,), (0,)), ((), ())), preferred_element_type=wide)


def dot_nt(left, right):
    return lax.dot_general(left, right, (((1,), (1,)), ((), ())), preferred_element_type=wide)


def dot_tn(left, right):
    return lax.dot_general(left, right, (((0,), (0,)), ((), ())), preferred_element_type=wide)


def partner(value, axis, step, name):
    count = lax.axis_size(axis)
    with jax.named_scope(name):
        return lax.ppermute(value, axis, [(i, i ^ step) for i in range(count)])


def gather_blocks(piece, name):
    count = lax.axis_size("blk")
    return [piece] + [partner(piece, "blk", r, name) for r in range(1, count)]


def relay_far(near, own, name):
    count = lax.axis_size("blk")
    rows = own.shape[0]
    halved = rows % 32 == 0
    cuts = [slice(0, rows // 2), slice(rows // 2, rows)] if halved else [slice(0, rows)]
    pieces = {}
    for r in range(1, count):
        if r in near:
            pieces[r] = [near[r]]
            continue
        low_bit = r & -r
        high_bit = 1 << (r.bit_length() - 1)
        pieces[r] = []
        for i, (bit, rows_cut) in enumerate(zip((high_bit, low_bit), cuts)):
            source = pieces[r ^ bit]
            part = source[i] if len(source) > 1 else source[0][rows_cut]
            pieces[r].append(partner(part, "blk", bit, name + "_relay"))
    return pieces


def gather_relayed(piece, name):
    count = lax.axis_size("blk")
    near = {r: partner(piece, "blk", r, name) for r in range(1, count) if r & (r - 1) == 0}
    pieces = relay_far(near, piece, name)
    return [[piece]] + [pieces[r] for r in range(1, count)]


def scatter_blocks(pieces, name):
    return [pieces[0]] + [partner(pieces[r], "blk", r, name) for r in range(1, len(pieces))]


def swap(value, name):
    with jax.named_scope(name):
        return lax.ppermute(value, "dp", [(0, 1), (1, 0), (2, 3), (3, 2)])


def cross(value, name):
    with jax.named_scope(name):
        return lax.ppermute(value, "dp", [(1, 2), (2, 1)])


def call(body, outs, ins, scratch=(), in_specs=None, after=(), carry=(), moves=None):
    anywhere = pl.BlockSpec(memory_space=pl.ANY)
    whole = pl.BlockSpec(memory_space=pltpu.VMEM)
    in_specs = list(in_specs or [anywhere if moves else whole] * len(ins))
    given, waited, made = len(ins), len(after) + len(carry), len(outs)

    def run(*refs):
        results = given + waited
        body(*refs[:given], *refs[results : results + made], *refs[results + made + len(carry) :])

    return pl.pallas_call(
        run,
        name=getattr(body, "func", body).__name__,
        out_shape=tuple(outs) + tuple(shape(value.shape, value.dtype) for value in carry),
        in_specs=in_specs + [anywhere] * waited,
        out_specs=tuple([anywhere if moves == "all" else whole] * made + [anywhere] * len(carry)),
        scratch_shapes=list(scratch),
        input_output_aliases={given + len(after) + i: made + i for i in range(len(carry))},
        cost_estimate=pl.CostEstimate(flops=0, bytes_accessed=0, transcendentals=0),
        compiler_params=pltpu.CompilerParams(vmem_limit_bytes=vmem_limit),
    )(*ins, *after, *carry)


def shape(dims, kind):
    return jax.ShapeDtypeStruct(dims, kind)


in_smem = pl.BlockSpec(memory_space=pltpu.SMEM)
in_vmem = pl.BlockSpec(memory_space=pltpu.VMEM)
in_hbm = pl.BlockSpec(memory_space=pltpu.HBM)


def arriving(pairs, sems):
    copies = []
    for i, (source, target) in enumerate(pairs):
        copies.append(pltpu.make_async_copy(source, target, sems.at[i]))
        copies[-1].start()
    return copies


def as_row(column):
    return jnp.broadcast_to(column, (column.shape[0], 128)).T[:1]


def as_column(row):
    width = row.shape[1]
    padded = -(-width // 128) * 128
    row = row.astype(wide)
    if padded != width:
        row = jnp.concatenate([row, jnp.zeros((1, padded - width), wide)], axis=1)
    return jnp.broadcast_to(row, (128, padded)).T[:width, :1]


def segment_start(lengths_ref, rows):
    start = jnp.zeros_like(rows)
    end = jnp.int32(0)
    for i in range(lengths_ref.shape[1]):
        end = end + lengths_ref[0, i]
        start = jnp.where(rows >= end, end, start)
    return start


def rotate(pair, cosine, sine):
    half = HEAD_DIM // 2
    first, second = pair[:half], pair[half:]
    return jnp.concatenate(
        [first * cosine - second * sine, second * cosine + first * sine], axis=0
    )


def enter_kernel(
    lengths_ref, place_ref, small_ref, turn_ref, tokens_in, wq_in, wk_in, wv_in,
    q_ref, kv_ref, normed_ref, tokens_t_ref, cos_ref, sin_ref, tokens_ref, wq_ref, wk_ref, wv_ref, sems,
):
    ins = (tokens_in, wq_in, wk_in, wv_in)
    copies = arriving(zip(ins, (tokens_ref, wq_ref, wk_ref, wv_ref)), sems)
    rows, width = tokens_ref.shape
    q_width = wq_ref.shape[0]
    small = small_ref[...].astype(wide)
    gain = small[:, :width]
    bias = as_column(small[:, width:])
    copies[0].wait()
    hidden = tokens_ref[...].astype(wide)
    inverse = lax.rsqrt(jnp.mean(hidden * hidden, axis=1, keepdims=True) + epsilon)
    normed = (hidden * inverse * gain).astype(low)
    tokens_t_ref[...] = hidden.T.astype(low)
    normed_ref[...] = normed.astype(wide).T.astype(low)
    index = place_ref[0] * rows + lax.broadcasted_iota(jnp.int32, (1, rows), 1)
    position = (index - segment_start(lengths_ref, index)).astype(wide)
    angles = turn_ref[...] * position
    cosine, sine = jnp.cos(angles), jnp.sin(angles)
    cos_ref[...] = cosine
    sin_ref[...] = sine
    for copy in copies[1:]:
        copy.wait()
    q_lin = dot_nt(wq_ref[...], normed) + bias[:q_width]
    for h in range(q_lin.shape[0] // HEAD_DIM):
        head = rotate(q_lin[h * HEAD_DIM : (h + 1) * HEAD_DIM], cosine, sine)
        q_ref[h * HEAD_DIM : (h + 1) * HEAD_DIM, :] = head.astype(low) * low(HEAD_DIM**-0.5)
    k_lin = dot_nt(wk_ref[...], normed) + bias[q_width : q_width + HEAD_DIM]
    v_lin = dot_nt(wv_ref[...], normed) + bias[q_width + HEAD_DIM :]
    kv_ref[...] = jnp.concatenate([rotate(k_lin, cosine, sine), v_lin], axis=0).T.astype(low)


def weights_kernel(
    whole_down, lengths_ref, place_ref, gate_in, up_in, down_in, cotangent_in,
    gate_t_ref, gate_own_ref, up_t_ref, up_own_ref, down_t_ref, down_ref, mine_ref, other_ref,
    gate_ref, up_ref, cotangent_ref, turned_ref, grad_ref, sems,
):
    units = gate_t_ref.shape[0]
    hidden = gate_in.shape[1]
    window = turned_ref.shape[0]
    first = place_ref[0] * units
    base = pl.multiple_of(jnp.minimum(first // 128 * 128, hidden - window), 128)
    down_rows = down_in.at[pl.ds(pl.multiple_of(first, 16), units), :] if whole_down else down_in
    copies = arriving(
        [
            (gate_in.at[:, pl.ds(base, window)], gate_ref),
            (up_in.at[:, pl.ds(base, window)], up_ref),
            (cotangent_in, cotangent_ref),
            (down_rows, down_ref),
        ],
        sems,
    )
    for copy, ref, turned, own in (
        (copies[0], gate_ref, gate_t_ref, gate_own_ref),
        (copies[1], up_ref, up_t_ref, up_own_ref),
    ):
        copy.wait()
        turned_ref[...] = ref[...].astype(wide).T
        part = turned_ref[pl.ds(pl.multiple_of(first - base, 8), units), :]
        turned[...] = part.astype(low)
        own[...] = part.T.astype(low)
    copies[2].wait()
    rows = cotangent_ref.shape[0]
    half = rows // 2
    row = place_ref[0] * rows + lax.broadcasted_iota(jnp.int32, (rows, 1), 0)
    end = jnp.int32(0)
    for i in range(lengths_ref.shape[1]):
        end = end + lengths_ref[0, i]
    grad_ref[...] = jnp.where(row < end, cotangent_ref[...].astype(wide), 0.0)
    core = place_ref[1]
    mine_ref[...] = grad_ref[pl.ds(pl.multiple_of(core * half, half), half), :].astype(low)
    other_ref[...] = grad_ref[pl.ds(pl.multiple_of((1 - core) * half, half), half), :].astype(low)
    copies[3].wait()
    down_t_ref[...] = down_ref[...].astype(wide).T.astype(low)


def mask_bias(key_base, key_rows, q_index, q_start):
    keys = key_base + lax.broadcasted_iota(jnp.int32, (key_rows, q_index.shape[1]), 0)
    return jnp.where((keys >= q_start) & (keys <= q_index), 0.0, masked_value)


def first_row(lengths_ref, row):
    start = jnp.int32(0)
    end = jnp.int32(0)
    for i in range(lengths_ref.shape[1]):
        end = end + lengths_ref[0, i]
        start = jnp.where(row >= end, end, start)
    return start


def attend_kernel(blocks, lengths_ref, place_ref, q_ref, w_out_ref, *refs):
    kv_refs = refs[:blocks]
    out_ref, log_ref, mine_ref, other_ref, kv_ref, acc_ref, max_ref, bias_ref, part_ref, score_ref = refs[blocks:]
    rows = q_ref.shape[1]
    heads = q_ref.shape[0] // HEAD_DIM
    own, core = place_ref[0], place_ref[1]
    for r in range(blocks):
        kv_ref[r] = kv_refs[r][...]
    q_index = own * rows + lax.broadcasted_iota(jnp.int32, (1, rows), 1)
    q_start = segment_start(lengths_ref, q_index)
    acc_ref[...] = jnp.zeros_like(acc_ref)
    max_ref[...] = jnp.full_like(max_ref, masked_value)

    def visit(block, carry):
        pair = kv_ref[block ^ own]
        keys = pair[:, :HEAD_DIM]
        values = pair.astype(wide).T[HEAD_DIM:].astype(low)
        values = jnp.concatenate([values, jnp.ones((16, rows), low)], axis=0)
        bias_ref[...] = mask_bias(block * rows, rows, q_index, q_start)

        def scores(h):
            score_ref[h % 2] = dot_nn(keys, q_ref[h * HEAD_DIM : (h + 1) * HEAD_DIM, :])

        def gather(h, weight, shrink):
            acc_ref[h] = acc_ref[h] * shrink + dot_nn(values, weight)

        scores(0)
        waiting = None
        for h in range(heads):
            if h + 1 < heads:
                scores(h + 1)
            masked = score_ref[h % 2] + bias_ref[...]
            old = max_ref[h : h + 1, :]
            new = jnp.maximum(old, jnp.max(masked, axis=0, keepdims=True))
            weight = jnp.exp(masked - new).astype(low)
            max_ref[h : h + 1, :] = new
            if waiting is not None:
                gather(*waiting)
            waiting = (h, weight, jnp.exp(old - new))
        gather(*waiting)
        return carry

    lax.fori_loop(first_row(lengths_ref, own * rows) // rows, own + 1, visit, 0)
    for h in range(heads):
        total = acc_ref[h, HEAD_DIM : HEAD_DIM + 1, :]
        out_ref[h * HEAD_DIM : (h + 1) * HEAD_DIM, :] = acc_ref[h, :HEAD_DIM, :] / total
        log_ref[h : h + 1, :] = max_ref[h : h + 1, :] + jnp.log(total)
    part_ref[...] = dot_tn(w_out_ref[...], out_ref[...].astype(low))
    half = mine_ref.shape[1]
    mine_ref[...] = part_ref[:, pl.ds(pl.multiple_of(core * half, half), half)]
    other_ref[...] = part_ref[:, pl.ds(pl.multiple_of((1 - core) * half, half), half)].astype(low)


def middle_kernel(place_ref, tokens_ref, part_ref, passed_ref, gain_ref, hidden_ref, normed_ref):
    half = hidden_ref.shape[1]
    mine = pl.ds(pl.multiple_of(place_ref[1] * half, half), half)
    hidden = tokens_ref[:, mine].astype(wide) + part_ref[...] + passed_ref[...].astype(wide)
    hidden_ref[...] = hidden
    inverse = lax.rsqrt(jnp.mean(hidden * hidden, axis=0, keepdims=True) + epsilon)
    normed_ref[...] = (hidden * inverse * as_column(gain_ref[...])).astype(low)


def hidden_kernel(parts, *refs):
    gy_refs, x_refs, refs = refs[: 2 * parts], refs[2 * parts : 4 * parts], refs[4 * parts :]
    gate_t_ref, up_t_ref, down_ref, gate_ref, up_ref = refs[:5]
    mixed_ref, grad_gate_ref, grad_up_ref, other_ref, mine_ref, x_ref, gy_ref = refs[5:]
    half = other_ref.shape[1]
    row = 0
    for k in range(2):
        at = 0
        for x, gy in zip(x_refs[k * parts : (k + 1) * parts], gy_refs[k * parts : (k + 1) * parts]):
            x_ref[at : at + x.shape[0], k * half : (k + 1) * half] = x[...]
            gy_ref[row : row + gy.shape[0], :] = gy[...]
            at += x.shape[0]
            row += gy.shape[0]
    x = x_ref[...]
    gate = dot_nn(gate_t_ref[...], x)
    up = dot_nn(up_t_ref[...], x)
    grad_mixed = dot_nt(down_ref[...], gy_ref[...])
    sigmoid = 1.0 / (1.0 + jnp.exp(-gate))
    silu = gate * sigmoid
    mixed_ref[...] = (silu * up).astype(low)
    grad_gate = (grad_mixed * up * sigmoid * (1.0 + gate * (1.0 - sigmoid))).astype(low)
    grad_up = (grad_mixed * silu).astype(low)
    grad_gate_ref[...] = grad_gate
    grad_up_ref[...] = grad_up
    back = (dot_nn(gate_ref[...], grad_gate) + dot_nn(up_ref[...], grad_up)).astype(low)
    other_ref[...] = back[:, :half]
    mine_ref[...] = back[:, half:]


def weight_kernel(transposed, first, counts, outputs, *refs):
    blocks = len(counts)
    lefts, parts, out_refs, right_ref = refs[:blocks], refs[blocks : -outputs - 1], refs[-outputs - 1 : -1], refs[-1]
    units = lefts[0].shape[0]
    columns = sum(ref.shape[0] for ref in out_refs) // units * 128
    last = first + columns
    total, at = None, 0
    for r in range(blocks):
        row = 0
        for k in range(2):
            place = 0
            for part in parts[at : at + counts[r]]:
                if transposed:
                    half = part.shape[1]
                    start, end = max(place, first), min(place + part.shape[0], last)
                    if start < end:
                        right_ref[r, start - first : end - first, k * half : (k + 1) * half] = part[
                            start - place : end - place, :
                        ]
                    place += part.shape[0]
                else:
                    right_ref[r, row : row + part.shape[0], :] = part[:, first:last]
                    row += part.shape[0]
            at += counts[r]
        left, right = lefts[r][...], right_ref[r]
        product = dot_nt(left, right) if transposed else dot_nn(left, right)
        total = product if total is None else total + product
    at = 0
    for out_ref in out_refs:
        for t in range(out_ref.shape[0] // units):
            out_ref[t * units : (t + 1) * units, :] = total[:, at : at + 128].astype(low)
            at += 128


def project_kernel(blocks, weight_ref, *refs):
    other_ref, mine_refs = refs[blocks], refs[blocks + 1 :]
    half = other_ref.shape[2]
    for r in range(blocks):
        part = dot_nn(weight_ref[...], refs[r][...]).astype(low)
        other_ref[r] = part[:, :half]
        mine_refs[r][...] = part[:, half:]


def add_kernel(*refs):
    count = (len(refs) - 1) // 2
    for i in range(count):
        refs[1 + count + i][...] = (refs[1 + i][...].astype(wide) + refs[0][i].astype(wide)).astype(low)


def pair_kernel(*refs):
    count = len(refs) // 3
    for i in range(count):
        refs[2 * count + i][...] = (refs[2 * i][...].astype(wide) + refs[2 * i + 1][...].astype(wide)).astype(low)


def join_kernel(place_ref, mine_ref, other_ref, out_ref):
    half = mine_ref.shape[0]
    core = place_ref[1]
    out_ref[pl.ds(pl.multiple_of(core * half, half), half), :] = mine_ref[...].astype(out_ref.dtype)
    out_ref[pl.ds(pl.multiple_of((1 - core) * half, half), half), :] = other_ref[...].astype(out_ref.dtype)


def wait_kernel(*refs):
    pass


def tick_kernel(ops, place_ref, *refs):
    ins, outs = refs[: -len(ops)], refs[-len(ops) :]
    end = (place_ref[2] == 0) | (place_ref[2] == 3)
    for (kind, args), out_ref in zip(ops, outs):
        sources = [(ins if given else outs)[i] for given, i, *_ in args]
        if kind == "add":
            out_ref[...] = (sources[0][...].astype(wide) + sources[1][...].astype(wide)).astype(low)
        elif kind == "pick":
            out_ref[...] = jnp.where(end, sources[0][...], sources[1][...])
        else:
            at = 0
            for source, (_, _, start, rows) in zip(sources, args):
                out_ref[at : at + rows, :] = source[start : start + rows, :]
                at += rows


def sum_blocks(refs, starts=None, rows=None):
    total = None
    for i, ref in enumerate(refs):
        value = ref[...] if starts is None else ref[starts[i] : starts[i] + rows, :]
        total = value.astype(wide) if total is None else total + value.astype(wide)
    return total


def layer_kernel(hidden_ref, *refs):
    out_ref = refs[-1]
    out_ref[...] = (hidden_ref[...] + sum_blocks(refs[:-1])).T.astype(low)


def grad_middle_kernel(hidden_ref, gain_ref, gy_ref, *refs):
    grad_ref, grad_low_ref, grad_gain_ref = refs[-3:]
    hidden = hidden_ref[...]
    inverse = lax.rsqrt(jnp.mean(hidden * hidden, axis=0, keepdims=True) + epsilon)
    grad_normed = sum_blocks(refs[:-3])
    weighted = as_column(gain_ref[...]) * grad_normed
    inner = jnp.mean(weighted * hidden, axis=0, keepdims=True)
    grad = inverse * weighted - hidden * (inverse * inverse * inverse * inner)
    grad = grad + gy_ref[...].astype(wide).T
    grad_ref[...] = grad
    grad_low_ref[...] = grad.astype(low)
    grad_gain_ref[...] = as_row(jnp.sum(grad_normed * hidden * inverse, axis=1, keepdims=True))


def back_enter_kernel(
    place_ref, gm_mine_ref, gm_other_ref, w_out_ref, out_ref, go_ref, delta_ref, gm_ref
):
    half = gm_mine_ref.shape[1]
    core = place_ref[1]
    gm_ref[:, pl.ds(pl.multiple_of(core * half, half), half)] = gm_mine_ref[...]
    gm_ref[:, pl.ds(pl.multiple_of((1 - core) * half, half), half)] = gm_other_ref[...]
    grad_out = dot_nn(w_out_ref[...], gm_ref[...]).astype(low)
    go_ref[...] = grad_out
    product = grad_out.astype(wide) * out_ref[...]
    for h in range(product.shape[0] // HEAD_DIM):
        delta_ref[h : h + 1, :] = jnp.sum(
            product[h * HEAD_DIM : (h + 1) * HEAD_DIM], axis=0, keepdims=True
        )


def attend_back_kernel(
    blocks, tile, lengths_ref, place_ref, go_ref, delta_ref, log_ref, q_ref, cos_ref, sin_ref, *refs,
):
    kv_refs, refs = refs[:blocks], refs[blocks:]
    (grad_q_ref, *grad_kv_refs), refs = refs[: blocks + 1], refs[blocks + 1 :]
    kv_ref, bias_ref, dq_ref, q_all_ref, go_all_ref, weight_ref, grad_ref, grad_kv_ref, score_ref, grad_weight_ref = refs
    rows = q_ref.shape[1]
    heads = grad_q_ref.shape[0] // HEAD_DIM
    own = place_ref[0]
    parts = rows // tile

    def lanes(h):
        return slice(h * rows, (h + 1) * rows)

    def span(h):
        return slice(h * HEAD_DIM, (h + 1) * HEAD_DIM)

    for r in range(blocks):
        kv_ref[r] = kv_refs[r][...]
        grad_kv_ref[r] = jnp.zeros_like(grad_kv_ref[r])
    for h in range(heads):
        q_all_ref[:, lanes(h)] = q_ref[span(h), :]
        go_all_ref[:, lanes(h)] = go_ref[span(h), :]
    dq_ref[...] = jnp.zeros_like(dq_ref)
    q_index = own * rows + lax.broadcasted_iota(jnp.int32, (1, rows), 1)
    q_start = segment_start(lengths_ref, q_index)

    def visit(block, carry):
        part = pl.multiple_of(block % parts * tile, tile)
        at = ((block // parts) ^ own, pl.ds(part, tile), slice(None))
        pair = kv_ref[at]
        keys = pair[:, :HEAD_DIM]
        values = pair[:, HEAD_DIM:]
        keys_t = pair.astype(wide).T[:HEAD_DIM].astype(low)
        bias_ref[...] = mask_bias(block * tile, tile, q_index, q_start)

        def products(h):
            score_ref[h % 2] = dot_nn(keys, q_all_ref[:, lanes(h)])
            grad_weight_ref[h % 2] = dot_nn(values, go_all_ref[:, lanes(h)])

        products(0)
        for h in range(heads):
            if h + 1 < heads:
                products(h + 1)
            weight = jnp.exp(score_ref[h % 2] + bias_ref[...] - log_ref[h : h + 1, :])
            grad = (weight * (grad_weight_ref[h % 2] - delta_ref[h : h + 1, :])).astype(low)
            weight_ref[:, lanes(h)] = weight.astype(low)
            grad_ref[:, lanes(h)] = grad
            dq_ref[span(h), :] += dot_nn(keys_t, grad)
        grad_keys = dot_nt(grad_ref[...], q_all_ref[...])
        grad_values = dot_nt(weight_ref[...], go_all_ref[...])
        grad_kv_ref[at] = jnp.concatenate([grad_keys, grad_values], axis=1).astype(low)
        return carry

    lax.fori_loop(first_row(lengths_ref, own * rows) // tile, (own + 1) * parts, visit, 0)
    for r in range(blocks):
        grad_kv_refs[r][...] = grad_kv_ref[r]
    for h in range(heads):
        turned = rotate(dq_ref[span(h), :] * HEAD_DIM**-0.5, cos_ref[...], -sin_ref[...])
        grad_q_ref[span(h), :] = turned.astype(low)


def query_kernel(
    place_ref, normed_ref, grad_q_ref, wq_ref, gm_mine_ref, gm_other_ref, out_ref,
    grad_wq_ref, part_ref, grad_bq_ref, grad_w_out_ref, gm_ref,
):
    half = gm_mine_ref.shape[1]
    core = place_ref[1]
    gm_ref[:, pl.ds(pl.multiple_of(core * half, half), half)] = gm_mine_ref[...]
    gm_ref[:, pl.ds(pl.multiple_of((1 - core) * half, half), half)] = gm_other_ref[...]
    grad_w_out_ref[...] = dot_nt(out_ref[...].astype(low), gm_ref[...]).astype(low)
    grad_q = grad_q_ref[...]
    grad_wq_ref[...] = dot_nt(grad_q, normed_ref[...]).astype(low)
    part_ref[...] = dot_tn(wq_ref[...], grad_q)
    grad_bq_ref[...] = dot_nt(jnp.ones((16, grad_q.shape[1]), low), grad_q)


def key_kernel(
    blocks, starts, place_ref, normed_ref, tokens_ref, part_ref, wk_ref, wv_ref, cos_ref, sin_ref,
    grad_wq_ref, grad_bq_ref, grad_w_out_ref, grad_gain_two_ref, *refs,
):
    kv_refs, share_refs, (mine_ref, other_ref, sum_ref, pack_ref) = refs[:blocks], refs[blocks : 2 * blocks], refs[2 * blocks :]
    both = sum_blocks(kv_refs, starts, tokens_ref.shape[1]).T
    both = jnp.concatenate(
        [rotate(both[:HEAD_DIM], cos_ref[...], -sin_ref[...]), both[HEAD_DIM:]], axis=0
    ).astype(low)
    total = part_ref[...] + dot_tn(wk_ref[...], both[:HEAD_DIM]) + dot_tn(wv_ref[...], both[HEAD_DIM:])
    sum_ref[...] = total
    half = mine_ref.shape[1]
    core = place_ref[1]
    mine_ref[...] = sum_ref[:, pl.ds(pl.multiple_of(core * half, half), half)]
    other_ref[...] = sum_ref[:, pl.ds(pl.multiple_of((1 - core) * half, half), half)].astype(low)
    hidden = tokens_ref[...].astype(wide)
    inverse = lax.rsqrt(jnp.mean(hidden * hidden, axis=0, keepdims=True) + epsilon)
    q_width, width = grad_wq_ref.shape
    kv_width = both.shape[0]
    at = 0
    pack_ref[at : at + q_width, :] = grad_wq_ref[...]
    at += q_width
    pack_ref[at : at + kv_width, :] = dot_nt(both, normed_ref[...]).astype(low)
    at += kv_width
    pack_ref[at : at + q_width, :] = grad_w_out_ref[...]
    at += q_width
    grad_gain = as_row(jnp.sum(total * (hidden * inverse), axis=1, keepdims=True))
    grad_bkv = dot_nt(jnp.ones((16, both.shape[1]), low), both)[:1]
    biases = jnp.concatenate(
        [grad_bq_ref[:1, :], grad_bkv, jnp.zeros((1, width - q_width - kv_width), wide)], axis=1
    )
    small = jnp.concatenate(
        [grad_gain, grad_gain_two_ref[...], biases, jnp.zeros((pack_ref.shape[0] - at - 3, width), wide)], axis=0
    )
    pack_ref[at:, :] = small.astype(low)
    share = pack_ref.shape[0] // blocks
    for r in range(blocks):
        start = pl.multiple_of((place_ref[0] ^ r) * share, share)
        for t in range(width // 128):
            share_refs[r][t * share : (t + 1) * share, :] = pack_ref[pl.ds(start, share), t * 128 : (t + 1) * 128]


def share_kernel(starts, *refs):
    refs[-1][...] = sum_blocks(refs[:-1], starts, refs[-1].shape[0]).astype(low)


def unpack_kernel(share, sources, place_ref, *refs):
    pieces, outs, (stack_ref, pack_ref) = refs[: len(sources)], refs[len(sources) : -2], refs[-2:]
    for ref, (r, first, rows, start) in zip(pieces, sources):
        stack_ref[r, first : first + rows, :] = ref[start : start + rows, :].astype(wide)
    for r in range(stack_ref.shape[0]):
        at = pl.ds(pl.multiple_of((place_ref[0] ^ r) * share, 8), share)
        for t in range(stack_ref.shape[1] // share):
            pack_ref[at, t * 128 : (t + 1) * 128] = stack_ref[r, t * share : (t + 1) * share, :]
    at = 0
    for out_ref in outs:
        out_ref[...] = pack_ref[at : at + out_ref.shape[0], :]
        at += out_ref.shape[0]


def leave_kernel(place_ref, tokens_ref, mine_ref, passed_ref, gain_ref, grad_mid_ref, out_ref):
    half = mine_ref.shape[1]
    hidden = tokens_ref[:, pl.ds(pl.multiple_of(place_ref[1] * half, half), half)].astype(wide)
    inverse = lax.rsqrt(jnp.mean(hidden * hidden, axis=0, keepdims=True) + epsilon)
    weighted = as_column(gain_ref[...]) * (mine_ref[...] + passed_ref[...].astype(wide))
    inner = jnp.mean(weighted * hidden, axis=0, keepdims=True)
    grad = grad_mid_ref[...] + inverse * weighted - hidden * (inverse * inverse * inverse * inner)
    out_ref[...] = grad.T.astype(low)


def place_kernel(transposed, tiles, place_ref, refs, out_ref, all_ref):
    own_ref, near_x_ref, near_y_ref, *far_refs = refs
    step, tiles = tiles
    units = own_ref.shape[0]
    half = units // 2
    for r, ref in enumerate((own_ref, near_x_ref, near_y_ref)):
        start = pl.multiple_of((place_ref[0] ^ r) * units, 8)
        all_ref[pl.ds(start, units), :] = ref[...].astype(wide)
    for k in range(2):
        start = pl.multiple_of((place_ref[0] ^ 3) * units + k * half, 8)
        part = 2 * step + k

        @pl.when(part < tiles)
        def _(start=start, k=k):
            all_ref[pl.ds(start, half), :] = far_refs[k][...].astype(wide)

        @pl.when(part >= tiles)
        def _(start=start, k=k):
            all_ref[pl.ds(start, half), :] = far_refs[2 + k][...].astype(wide)

    if transposed:
        out_ref[...] = all_ref[...].T


def place_shares(place, shares, units, transposed, width, at, whole, last):
    tile, half = 128, units // 2
    counts = [share[0].shape[0] // units for share in shares]
    begins = [sum(counts[:i]) for i in range(len(counts))]
    first = at // tile
    ins, specs = [place], [in_smem]
    for (own, near_x, near_y, far_y, far_x), tiles, begin in zip(shares, counts, begins):

        def step_of(i, tiles=tiles, begin=begin):
            return jnp.clip(i - begin, 0, tiles - 1)

        def halves(start, k, later, tiles=tiles, step_of=step_of):
            def index(i):
                part = 2 * step_of(i) + k - (tiles if later else 0)
                return (start // half + jnp.clip(part, 0, tiles - 1), 0)

            return pl.BlockSpec((half, tile), index)

        ins += [own, near_x, near_y, far_y[0], far_y[0], far_x[0], far_x[0]]
        specs += [pl.BlockSpec((units, tile), lambda i, step_of=step_of: (step_of(i), 0))] * 3
        specs += [halves(far_y[1], k, False) for k in range(2)]
        specs += [halves(far_x[1], k, True) for k in range(2)]
    ins += last
    specs += [pl.BlockSpec(memory_space=pl.ANY)] * len(last)
    aliases = {}
    if whole is not None:
        aliases = {len(ins): 0}
        ins.append(whole)
        specs.append(pl.BlockSpec(memory_space=pl.ANY))

    def body(*refs):
        out_ref, token_ref = refs[len(ins) : len(ins) + 2]
        all_ref = refs[-1] if transposed else out_ref
        token_ref[...] = jnp.zeros_like(token_ref)
        for n, (tiles, begin) in enumerate(zip(counts, begins)):
            step = pl.program_id(0) - begin

            @pl.when((step >= 0) & (step < tiles))
            def _(n=n, step=step, tiles=tiles):
                place_kernel(transposed, (step, tiles), refs[0], refs[1 + 7 * n : 8 + 7 * n], out_ref, all_ref)

    if transposed:
        dims = (width, 4 * units)
        out_spec = pl.BlockSpec((tile, 4 * units), lambda i: (i + first, 0))
        scratch = [pltpu.VMEM((4 * units, tile), wide)]
    else:
        dims = (4 * units, width)
        out_spec = pl.BlockSpec((4 * units, tile), lambda i: (0, i + first))
        scratch = []
    return pl.pallas_call(
        body,
        name="place_kernel",
        out_shape=(shape(dims, wide), shape((8, 128), wide)),
        grid=(sum(counts),),
        in_specs=specs,
        out_specs=(out_spec, pl.BlockSpec((8, 128), lambda i: (0, 0))),
        scratch_shapes=scratch,
        input_output_aliases=aliases,
        cost_estimate=pl.CostEstimate(flops=0, bytes_accessed=0, transcendentals=0),
        compiler_params=pltpu.CompilerParams(vmem_limit_bytes=vmem_limit),
    )(*ins)


def local(
    tokens,
    lengths,
    norm1_gain,
    w_query,
    b_query,
    w_key,
    b_key,
    w_value,
    b_value,
    w_out,
    norm2_gain,
    w_gate,
    w_up,
    w_down,
    cotangent,
):
    rows, width = tokens.shape
    half = rows // 2
    blocks = lax.axis_size("blk")
    own_block = lax.axis_index("blk")
    own_core = lax.axis_index("tensor")
    q_width = w_query.shape[1]
    heads = q_width // HEAD_DIM
    units = w_gate.shape[1] // blocks
    place = jnp.stack([own_block, own_core, lax.axis_index("dp")]).astype(jnp.int32)
    gain_two = norm2_gain.reshape(1, width)
    key_tile = rows // 2

    half_dim = HEAD_DIM // 2
    turn = (rope_base ** (-2.0 * jnp.arange(half_dim, dtype=wide) / HEAD_DIM)).reshape(half_dim, 1)
    small = jnp.concatenate([norm1_gain, b_query, b_key, b_value]).reshape(1, -1)
    q_t, key_value, normed_t, tokens_t, cosine, sine = call(
        enter_kernel,
        [
            shape((q_width, rows), low),
            shape((rows, 2 * HEAD_DIM), low),
            shape((width, rows), low),
            shape((width, rows), low),
            shape((half_dim, rows), wide),
            shape((half_dim, rows), wide),
        ],
        [lengths, place, small, turn, tokens, w_query.T, w_key.T, w_value.T],
        [
            pltpu.VMEM((rows, width), low),
            pltpu.VMEM((q_width, width), low),
            pltpu.VMEM((HEAD_DIM, width), low),
            pltpu.VMEM((HEAD_DIM, width), low),
            pltpu.SemaphoreType.DMA((4,)),
        ],
        in_specs=[in_smem] * 2 + [in_vmem] * 2 + [in_hbm] * 4,
    )
    kv_blocks = gather_blocks(key_value, "kv")

    window = -(-(units + 127) // 128) * 128
    whole_down = units % 16 == 0
    down = w_down if whole_down else lax.dynamic_slice_in_dim(w_down, own_block * units, units, 0)
    gate_t, gate_own, up_t, up_own, down_t, down_own, grad_y_mine, grad_y_other = call(
        functools.partial(weights_kernel, whole_down),
        [
            shape((units, width), low),
            shape((width, units), low),
            shape((units, width), low),
            shape((width, units), low),
            shape((width, units), low),
            shape((units, width), low),
            shape((half, width), low),
            shape((half, width), low),
        ],
        [lengths, place, w_gate, w_up, down, cotangent],
        [
            pltpu.VMEM((width, window), low),
            pltpu.VMEM((width, window), low),
            pltpu.VMEM((rows, width), low),
            pltpu.VMEM((window, width), wide),
            pltpu.VMEM((rows, width), wide),
            pltpu.SemaphoreType.DMA((4,)),
        ],
        in_specs=[in_smem] * 2 + [in_hbm] * 4,
        after=[q_t],
    )
    gy_near = {r: partner(grad_y_mine, "blk", r, "gy") for r in range(1, blocks) if r & (r - 1) == 0}

    out_t, log_total, part_mine, part_other = call(
        functools.partial(attend_kernel, blocks),
        [
            shape((q_width, rows), wide),
            shape((heads + 1, rows), wide),
            shape((width, half), wide),
            shape((width, half), low),
        ],
        [lengths, place, q_t, w_out] + kv_blocks,
        [
            pltpu.VMEM((blocks, rows, 2 * HEAD_DIM), low),
            pltpu.VMEM((heads, HEAD_DIM + 16, rows), wide),
            pltpu.VMEM((heads + 1, rows), wide),
            pltpu.VMEM((rows, rows), wide),
            pltpu.VMEM((width, rows), wide),
            pltpu.VMEM((2, rows, rows), wide),
        ],
        in_specs=[in_smem] * 2 + [in_vmem] * (2 + blocks),
        after=[gate_t],
    )
    hidden, normed_two = call(
        middle_kernel,
        [shape((width, half), wide), shape((width, half), low)],
        [place, tokens_t, part_mine, partner(part_other, "tensor", 1, "part_core"), gain_two],
        in_specs=[in_smem] + [in_vmem] * 4,
        after=list(gy_near.values()),
    )

    last = [normed_two]

    def ordered(body, outs, ins, needs=(), **more):
        nonlocal last
        carry = more.get("carry", ())
        after = [v for v in last + list(needs) if not any(v is c for c in carry)]
        results = call(body, outs, ins, after=after, **more)
        last = [results[0]]
        return results

    def wait(carry, needs=()):
        return list(ordered(wait_kernel, [], [], needs=needs, carry=carry))

    def near(pieces):
        return [p for r, parts in enumerate(pieces) if r and r & (r - 1) == 0 for p in parts]

    def far(pieces):
        return [p for r, parts in enumerate(pieces) if r & (r - 1) for p in parts]

    kept = shape((units, rows), low)
    piece = shape((width, half), low)
    runs, back, passed = [], [None] * blocks, [None] * blocks

    def cores(parts, name):
        return [partner(part, "tensor", 1, name) for part in parts]

    x_parts, gy_parts = [], []

    def hidden_units(r, x_mine, x_other, gy_mine, gy_other):
        x_parts.append(x_other + x_mine)
        gy_parts.append(gy_other + gy_mine)
        runs.append(
            ordered(
                functools.partial(hidden_kernel, len(x_mine)),
                [kept, kept, kept, piece, piece],
                gy_parts[-1] + x_parts[-1] + [gate_t, up_t, down_own, gate_own, up_own],
                scratch=[pltpu.VMEM((width, rows), low), pltpu.VMEM((rows, width), low)],
            )
        )
        return runs[-1][3]

    def add_back(members, carry, needs=()):
        results = ordered(
            pair_kernel,
            [piece] * len(members),
            [value for r in members for value in (runs[r][4], passed[r])],
            needs=needs,
            carry=carry,
        )
        for r, value in zip(members, results):
            back[r] = partner(value, "blk", r, "back") if r else value
        return results[len(members) :]

    def hidden_weight(transposed, left, parts, first, shares):
        counts = [len(part) // 2 for part in parts]
        columns = sum(shares)
        dims = (columns, rows) if transposed else (rows, columns)
        return ordered(
            functools.partial(weight_kernel, transposed, first, counts, len(shares)),
            [shape((share // 128 * units, 128), low) for share in shares],
            [run[left] for run in runs] + sum(parts, []),
            scratch=[pltpu.VMEM((blocks,) + dims, low)],
        )

    def tick(ops, needs=(), carry=()):
        given, outs, listed = [], [], []
        for kind, *args in ops:
            spans = [arg if isinstance(arg, tuple) else (arg, 0, None) for arg in args]
            named, size = [], 0
            for value, start, count in spans:
                if isinstance(value, int):
                    entry, total = (False, value), outs[value].shape[0]
                else:
                    found = [i for i, known in enumerate(given) if known is value]
                    if not found:
                        given.append(value)
                    entry = (True, found[0] if found else len(given) - 1)
                    total = value.shape[0]
                count = total if count is None else count
                named.append(entry + (start, count))
                size = size + count if kind == "cat" else count
            listed.append((kind, named))
            outs.append(shape((size, 128), low))
        return ordered(
            functools.partial(tick_kernel, listed),
            outs,
            [place] + given,
            in_specs=[in_smem] + [in_vmem] * len(given),
            needs=needs,
            carry=carry,
        )

    x_near = {r: partner(normed_two, "blk", r, "x") for r in range(1, blocks) if r & (r - 1) == 0}
    other = hidden_units(
        0, [normed_two], cores([normed_two], "x_core"), [grad_y_mine], [grad_y_other]
    )
    other, *arrived = wait([other] + list(x_near.values()))
    passed[0] = partner(other, "tensor", 1, "back_core")
    x_near = dict(zip(x_near, arrived))
    x_mine = relay_far(x_near, normed_two, "x")
    gy_mine = relay_far(gy_near, grad_y_mine, "gy")
    x_other = {r: cores(parts, "x_core") for r, parts in x_mine.items() if r in x_near}
    gy_other = {r: cores(parts, "gy_core") for r, parts in gy_mine.items() if r in x_near}
    others = [hidden_units(r, x_mine[r], x_other[r], gy_mine[r], gy_other[r]) for r in x_near]
    fars = [r for r in x_mine if r not in x_near]
    parts = [part for r in fars for part in x_mine[r] + gy_mine[r]]
    results = wait(others + parts)
    for r in x_near:
        passed[r] = partner(results.pop(0), "tensor", 1, "back_core")
    for r in fars:
        x_mine[r] = [results.pop(0) for _ in x_mine[r]]
        gy_mine[r] = [results.pop(0) for _ in gy_mine[r]]
        x_other[r], gy_other[r] = cores(x_mine[r], "x_core"), cores(gy_mine[r], "gy_core")
    others = [hidden_units(r, x_mine[r], x_other[r], gy_mine[r], gy_other[r]) for r in fars]
    for r, other in zip(fars, add_back(list(x_near), others)):
        passed[r] = partner(other, "tensor", 1, "back_core")
    if len(fars) > 1:
        add_back(fars[:-1], [])
    cut_at = width // 2 // 128 * 128
    (d1,) = hidden_weight(False, 0, gy_parts, 0, [cut_at])
    d1_swap = swap(d1, "swap_d1")
    (d2,) = hidden_weight(False, 0, gy_parts, cut_at, [width - cut_at])
    layer_other, *layer_mine = ordered(
        functools.partial(project_kernel, blocks),
        [shape((blocks, width, half), low)] + [piece] * blocks,
        [down_t] + [run[0] for run in runs],
    )
    d2, layer_other = add_back(
        [blocks - 1, 0], [d2, layer_other], needs=back[1 : blocks - 1] + [d1_swap]
    )
    (d1_sum,) = tick([("add", d1, d1_swap)])
    d1_cross, d2_swap = cross(d1_sum, "cross_d1"), swap(d2, "swap_d2")
    layer_passed = partner(layer_other, "tensor", 1, "layer_core")
    g1, g2 = hidden_weight(True, 1, x_parts, 0, [cut_at, width - cut_at])
    u1, u2 = hidden_weight(True, 2, x_parts, 0, [cut_at, width - cut_at])
    d1_sum, d2_sum, d1_g1 = tick(
        [("add", d1_sum, d1_cross), ("add", d2, d2_swap), ("pick", g1, 0)], needs=back[1:]
    )
    grad_mid, grad_mid_low, grad_gain_two = ordered(
        grad_middle_kernel,
        [shape((width, half), wide), piece, shape((1, width), wide)],
        [hidden, gain_two, grad_y_mine] + back,
    )
    *layer_pieces, grad_mid_low, d1_g1, d2_sum = ordered(
        add_kernel, [piece] * blocks, [layer_passed] + layer_mine, carry=[grad_mid_low, d1_g1, d2_sum]
    )
    grad_mid_other = partner(grad_mid_low, "tensor", 1, "mid_core")
    layer_pieces = scatter_blocks(layer_pieces, "layer")
    d1_g1_swap, d2_cross = swap(d1_g1, "swap_d1_g1"), cross(d2_sum, "cross_d2")

    grad_out, delta = ordered(
        back_enter_kernel,
        [shape((q_width, rows), low), shape((heads + 1, rows), wide)],
        [place, grad_mid_low, grad_mid_other, w_out, out_t],
        scratch=[pltpu.VMEM((width, rows), low)],
        in_specs=[in_smem] + [in_vmem] * 4,
    )

    grad_q, *grad_kv = ordered(
        functools.partial(attend_back_kernel, blocks, key_tile),
        [shape((q_width, rows), low)] + [shape((rows, 2 * HEAD_DIM), low)] * blocks,
        [lengths, place, grad_out, delta, log_total, q_t, cosine, sine] + kv_blocks,
        scratch=[
            pltpu.VMEM((blocks, rows, 2 * HEAD_DIM), low),
            pltpu.VMEM((key_tile, rows), wide),
            pltpu.VMEM((q_width, rows), wide),
            pltpu.VMEM((HEAD_DIM, heads * rows), low),
            pltpu.VMEM((HEAD_DIM, heads * rows), low),
            pltpu.VMEM((key_tile, heads * rows), low),
            pltpu.VMEM((key_tile, heads * rows), low),
            pltpu.VMEM((blocks, rows, 2 * HEAD_DIM), low),
            pltpu.VMEM((2, key_tile, rows), wide),
            pltpu.VMEM((2, key_tile, rows), wide),
        ],
        in_specs=[in_smem] * 2 + [in_vmem] * (6 + blocks),
    )
    pack_rows = -(-(2 * q_width + 2 * HEAD_DIM + 3) // (16 * blocks)) * 16 * blocks
    share = pack_rows // blocks
    stack_rows = share * (width // 128)

    def query_back():
        return ordered(
            query_kernel,
            [
                shape((q_width, width), low),
                shape((width, rows), wide),
                shape((16, q_width), wide),
                shape((q_width, width), low),
            ],
            [place, normed_t, grad_q, w_query.T, grad_mid_low, grad_mid_other, out_t],
            scratch=[pltpu.VMEM((width, rows), low)],
            in_specs=[in_smem] + [in_vmem] * 6,
        )

    def key_back(kv_pieces, starts):
        return ordered(
            functools.partial(key_kernel, blocks, starts),
            [shape((stack_rows, 128), low)] * blocks + [shape((width, half), wide), shape((width, half), low)],
            [
                place, normed_t, tokens_t, normed_part, w_key.T, w_value.T, cosine, sine,
                grad_w_query, grad_b_query, grad_w_out, grad_gain_two,
            ] + kv_pieces,
            scratch=[pltpu.VMEM((width, rows), wide), pltpu.VMEM((pack_rows, width), low)],
            in_specs=[in_smem] + [in_vmem] * (11 + blocks),
        )

    def sum_share(pieces, starts):
        (own,) = ordered(
            functools.partial(share_kernel, starts), [shape((stack_rows, 128), low)], pieces
        )
        return own

    def leave(normed_mine, normed_passed):
        (grad_half,) = ordered(
            leave_kernel,
            [shape((half, width), low)],
            [place, tokens_t, normed_mine, normed_passed, norm1_gain.reshape(1, width), grad_mid],
            in_specs=[in_smem] + [in_vmem] * 5,
        )
        return grad_half

    def join(mine, other, kind):
        (whole,) = ordered(
            join_kernel,
            [shape((rows, width), kind)],
            [place, mine.astype(kind), other.astype(kind)],
            in_specs=[in_smem] + [in_vmem] * 2,
        )
        return whole

    def layer_leave():
        (layer_half,) = ordered(layer_kernel, [shape((half, width), low)], [hidden] + layer_pieces)
        return layer_half

    def unpack(pieces, sources):
        return ordered(
            functools.partial(unpack_kernel, share, sources),
            [
                shape((q_width, width), wide),
                shape((HEAD_DIM, width), wide),
                shape((HEAD_DIM, width), wide),
                shape((q_width, width), wide),
                shape((pack_rows - 2 * q_width - 2 * HEAD_DIM, width), wide),
            ],
            [place] + pieces,
            scratch=[pltpu.VMEM((blocks, stack_rows, 128), wide), pltpu.VMEM((pack_rows, width), wide)],
            in_specs=[in_smem] + [in_vmem] * len(pieces),
        )

    if blocks != 4:
        kv_pieces = scatter_blocks(grad_kv, "grad_kv")
        grad_w_query, normed_part, grad_b_query, grad_w_out = query_back()
        *shares, normed_mine, normed_other = key_back(kv_pieces, [0] * blocks)
        layer_half = layer_leave()
        layer_out = join(layer_half, partner(layer_half, "tensor", 1, "rows_core"), low)
        grad_half = leave(normed_mine, partner(normed_other, "tensor", 1, "normed_core"))
        grad_tokens = join(grad_half, partner(grad_half, "tensor", 1, "rows_core"), wide)
        own_share = sum_share(scatter_blocks(shares, "shares"), [0] * blocks)
        own_share = lax.psum(own_share, "dp")
        pieces = gather_blocks(own_share, "all_share")
        grad_w_query, grad_w_key, grad_w_value, grad_w_out, small = unpack(
            pieces, [(r, 0, stack_rows, 0) for r in range(blocks)]
        )

        def gather_weight(first, second, transposed):
            stacked = lax.psum(jnp.concatenate([first, second], axis=0), "dp")
            every = lax.all_gather(stacked, "blk").reshape(blocks, width // 128, units, 128)
            order = (1, 3, 0, 2) if transposed else (0, 2, 1, 3)
            dims = (width, blocks * units) if transposed else (blocks * units, width)
            return every.transpose(order).reshape(dims).astype(wide)

        grad_w_down = gather_weight(d1, d2, False)
        grad_w_gate = gather_weight(g1, g2, True)
        grad_w_up = gather_weight(u1, u2, True)
    else:
        r1, r2 = d1.shape[0], d2.shape[0]
        h1, h2 = r1 // 2, r2 // 2

        def both_ways(x_buffer, y_buffer, name):
            return partner(x_buffer, "blk", 1, name + "_x"), partner(y_buffer, "blk", 2, name + "_y")

        d1_all, g1_sum, d2_sum, d2_g2, x1, y1, kv_far = tick(
            [
                ("pick", d1_g1_swap, d1_sum),
                ("add", g1, d1_g1_swap),
                ("add", d2_sum, d2_cross),
                ("pick", g2, 2),
                ("cat", 0, grad_kv[1]),
                ("cat", 0, grad_kv[2]),
            ],
            needs=layer_pieces[1:],
            carry=[grad_kv[3]],
        )
        x1, y1 = both_ways(x1, y1, "d1")
        kv_far = partner(kv_far, "blk", 3, "grad_kv")
        d2_g2_swap, g1_cross = swap(d2_g2, "swap_d2_g2"), cross(g1_sum, "cross_g1")
        grad_w_query, normed_part, grad_b_query, grad_w_out = query_back()
        layer_half = layer_leave()
        d2_all, g2_sum, g1_sum, g1_u1, x2, y2, layer_half = tick(
            [
                ("pick", d2_g2_swap, d2_sum),
                ("add", g2, d2_g2_swap),
                ("add", g1_sum, g1_cross),
                ("pick", u1, 2),
                ("cat", 0, (y1, h1, h1)),
                ("cat", 0, (x1, 0, h1)),
            ],
            needs=[x1, y1, kv_far],
            carry=[layer_half],
        )
        x2, y2 = both_ways(x2, y2, "d2")
        g1_u1_swap, g2_cross = swap(g1_u1, "swap_g1_u1"), cross(g2_sum, "cross_g2")
        layer_passed = partner(layer_half, "tensor", 1, "rows_core")
        *shares, normed_mine, normed_other = key_back([grad_kv[0], x1, y1, kv_far], [0, r1, r1, 0])
        g1_all, u1_sum, g2_sum, g2_u2, x3, y3, share_far, normed_other = tick(
            [
                ("pick", g1_u1_swap, g1_sum),
                ("add", u1, g1_u1_swap),
                ("add", g2_sum, g2_cross),
                ("pick", u2, 2),
                ("cat", 0, (y2, h2, h2), shares[1]),
                ("cat", 0, (x2, 0, h2), shares[2]),
            ],
            needs=[x2, y2],
            carry=[shares[3], normed_other],
        )
        x3, y3 = both_ways(x3, y3, "g1")
        share_far = partner(share_far, "blk", 3, "shares")
        g2_u2_swap, u1_cross = swap(g2_u2, "swap_g2_u2"), cross(u1_sum, "cross_u1")
        normed_passed = partner(normed_other, "tensor", 1, "normed_core")
        layer_out = join(layer_half, layer_passed, low)
        grad_half = leave(normed_mine, normed_passed)
        own_share = sum_share([shares[0], x3, y3, share_far], [0, r1 + h2, r1 + h2, 0])
        g2_all, u2_sum, u1_sum, x4, y4, own_share, grad_half = tick(
            [
                ("pick", g2_u2_swap, g2_sum),
                ("add", u2, g2_u2_swap),
                ("add", u1_sum, u1_cross),
                ("cat", 0, (y3, h1, h1)),
                ("cat", 0, (x3, 0, h1)),
            ],
            carry=[own_share, grad_half],
        )
        x4, y4 = both_ways(x4, y4, "g2")
        share_swap = swap(own_share, "swap_share")
        u1_swap, u2_cross = swap(u1_sum, "swap_u1"), cross(u2_sum, "cross_u2")
        grad_passed = partner(grad_half, "tensor", 1, "rows_core")
        d_shares = [(d1_all, x1, y1, (y2, r2), (x2, r2)), (d2_all, x2, y2, (y3, r1), (x3, r1))]
        grad_w_down, *last = place_shares(place, d_shares, units, False, width, 0, None, last)
        u1_all, u2_sum, own_share, x5, y5 = tick(
            [
                ("pick", u1_swap, u1_sum),
                ("add", u2_sum, u2_cross),
                ("add", own_share, share_swap),
                ("cat", 0, (y4, h2, h2)),
                ("cat", 0, (x4, 0, h2)),
            ],
            needs=[x4, y4],
        )
        x5, y5 = both_ways(x5, y5, "u1")
        u2_swap, share_swap = swap(u2_sum, "swap_u2"), partner(own_share, "dp", 2, "share_far")
        u2_all, own_share, x6, y6 = tick(
            [
                ("pick", u2_swap, u2_sum),
                ("add", own_share, share_swap),
                ("cat", 0, (y5, h1, h1), 1),
                ("cat", 0, (x5, 0, h1), 1),
            ],
            needs=[x5, y5],
        )
        x6, y6 = both_ways(x6, y6, "u2")
        grad_tokens = join(grad_half, grad_passed, wide)
        g_shares = [(g1_all, x3, y3, (y4, r2), (x4, r2)), (g2_all, x4, y4, (y5, r1), (x5, r1))]
        grad_w_gate, *last = place_shares(place, g_shares, units, True, width, 0, None, last)
        first_half = stack_rows // 32 * 16
        share_at = r2 + h1
        far = tick(
            [
                ("cat", (y6, share_at + first_half, stack_rows - first_half)),
                ("cat", (x6, share_at, first_half)),
                ("cat", (y6, h2, h2)),
                ("cat", (x6, 0, h2)),
            ],
        )
        share_x, share_y = both_ways(far[0], far[1], "far_share")
        x7, y7 = both_ways(far[2], far[3], "far_u2")
        u_shares = [(u1_all, x5, y5, (y6, r2), (x6, r2)), (u2_all, x6, y6, (y7, 0), (x7, 0))]
        grad_w_up, *last = place_shares(place, u_shares[:1], units, True, width, 0, None, last)
        grad_w_query, grad_w_key, grad_w_value, grad_w_out, small = unpack(
            [own_share, x6, y6, share_y, share_x],
            [
                (0, 0, stack_rows, 0),
                (1, 0, stack_rows, share_at),
                (2, 0, stack_rows, share_at),
                (3, 0, first_half, 0),
                (3, first_half, stack_rows - first_half, 0),
            ],
        )
        grad_w_up, _ = place_shares(
            place, u_shares[1:], units, True, width, cut_at, grad_w_up, [small]
        )
    gains = small[:2]
    gains = gains + partner(gains, "tensor", 1, "gains_core")
    grad_b = small[2]
    return (
        layer_out,
        grad_tokens,
        gains[0],
        grad_w_query.T,
        grad_b[:q_width],
        grad_w_key.T,
        grad_b[q_width : q_width + HEAD_DIM],
        grad_w_value.T,
        grad_b[q_width + HEAD_DIM : q_width + 2 * HEAD_DIM],
        grad_w_out,
        gains[1],
        grad_w_gate,
        grad_w_up,
        grad_w_down,
    )


def solution(mesh):
    placed = (
        P(("dp", "blk"), None),
        P("dp", None),
        P(),
        P(None, "tensor"),
        P("tensor"),
        P(None, "tensor"),
        P("tensor"),
        P(None, "tensor"),
        P("tensor"),
        P("tensor", None),
        P(),
        P(None, "tensor"),
        P(None, "tensor"),
        P("tensor", None),
        P(("dp", "blk"), None),
    )
    return jax.shard_map(
        local,
        mesh=mesh,
        in_specs=placed,
        out_specs=(
            P(("dp", "blk"), None),
            P(("dp", "blk"), None),
            P(),
            P(None, "tensor"),
            P("tensor"),
            P(None, "tensor"),
            P("tensor"),
            P(None, "tensor"),
            P("tensor"),
            P("tensor", None),
            P(),
            P(None, "tensor"),
            P(None, "tensor"),
            P("tensor", None),
        ),
        check_vma=False,
    )
```

```python
import functools
import math

import jax
import jax.numpy as jnp
from jax import lax
from jax.experimental import pallas as pl
from jax.experimental.pallas import tpu as pltpu
from jax.sharding import PartitionSpec as P

HEAD_DIM = 64

epsilon = 1e-06
rope_base = 1000000.0
masked_value = -1e30

low = jnp.bfloat16
wide = jnp.float32
vmem_limit = 34 * 1024 * 1024


def dot_nn(left, right):
    return lax.dot_general(left, right, (((1,), (0,)), ((), ())), preferred_element_type=wide)


def dot_nt(left, right):
    return lax.dot_general(left, right, (((1,), (1,)), ((), ())), preferred_element_type=wide)


def dot_tn(left, right):
    return lax.dot_general(left, right, (((0,), (0,)), ((), ())), preferred_element_type=wide)


def partner(value, axis, step, name):
    count = lax.axis_size(axis)
    with jax.named_scope(name):
        return lax.ppermute(value, axis, [(i, i ^ step) for i in range(count)])


def gather_blocks(piece, name):
    count = lax.axis_size("blk")
    return [piece] + [partner(piece, "blk", r, name) for r in range(1, count)]


def relay_far(near, own, name):
    count = lax.axis_size("blk")
    rows = own.shape[0]
    halved = rows % 32 == 0
    cuts = [slice(0, rows // 2), slice(rows // 2, rows)] if halved else [slice(0, rows)]
    pieces = {}
    for r in range(1, count):
        if r in near:
            pieces[r] = [near[r]]
            continue
        low_bit = r & -r
        high_bit = 1 << (r.bit_length() - 1)
        pieces[r] = []
        for i, (bit, rows_cut) in enumerate(zip((high_bit, low_bit), cuts)):
            source = pieces[r ^ bit]
            part = source[i] if len(source) > 1 else source[0][rows_cut]
            pieces[r].append(partner(part, "blk", bit, name + "_relay"))
    return pieces


def gather_relayed(piece, name):
    count = lax.axis_size("blk")
    near = {r: partner(piece, "blk", r, name) for r in range(1, count) if r & (r - 1) == 0}
    pieces = relay_far(near, piece, name)
    return [[piece]] + [pieces[r] for r in range(1, count)]


def scatter_blocks(pieces, name):
    return [pieces[0]] + [partner(pieces[r], "blk", r, name) for r in range(1, len(pieces))]


def swap(value, name):
    with jax.named_scope(name):
        return lax.ppermute(value, "dp", [(0, 1), (1, 0), (2, 3), (3, 2)])


def cross(value, name):
    with jax.named_scope(name):
        return lax.ppermute(value, "dp", [(1, 2), (2, 1)])


def call(body, outs, ins, scratch=(), in_specs=None, after=(), carry=(), moves=None):
    anywhere = pl.BlockSpec(memory_space=pl.ANY)
    whole = pl.BlockSpec(memory_space=pltpu.VMEM)
    in_specs = list(in_specs or [anywhere if moves else whole] * len(ins))
    given, waited, made = len(ins), len(after) + len(carry), len(outs)

    def run(*refs):
        results = given + waited
        body(*refs[:given], *refs[results : results + made], *refs[results + made + len(carry) :])

    return pl.pallas_call(
        run,
        name=getattr(body, "func", body).__name__,
        out_shape=tuple(outs) + tuple(shape(value.shape, value.dtype) for value in carry),
        in_specs=in_specs + [anywhere] * waited,
        out_specs=tuple([anywhere if moves == "all" else whole] * made + [anywhere] * len(carry)),
        scratch_shapes=list(scratch),
        input_output_aliases={given + len(after) + i: made + i for i in range(len(carry))},
        cost_estimate=pl.CostEstimate(flops=0, bytes_accessed=0, transcendentals=0),
        compiler_params=pltpu.CompilerParams(vmem_limit_bytes=vmem_limit),
    )(*ins, *after, *carry)


def shape(dims, kind):
    return jax.ShapeDtypeStruct(dims, kind)


in_smem = pl.BlockSpec(memory_space=pltpu.SMEM)
in_vmem = pl.BlockSpec(memory_space=pltpu.VMEM)
in_hbm = pl.BlockSpec(memory_space=pltpu.HBM)


def arriving(pairs, sems):
    copies = []
    for i, (source, target) in enumerate(pairs):
        copies.append(pltpu.make_async_copy(source, target, sems.at[i]))
        copies[-1].start()
    return copies


def as_row(column):
    return jnp.broadcast_to(column, (column.shape[0], 128)).T[:1]


def as_column(row):
    width = row.shape[1]
    padded = -(-width // 128) * 128
    row = row.astype(wide)
    if padded != width:
        row = jnp.concatenate([row, jnp.zeros((1, padded - width), wide)], axis=1)
    return jnp.broadcast_to(row, (128, padded)).T[:width, :1]


def segment_start(lengths_ref, rows):
    start = jnp.zeros_like(rows)
    end = jnp.int32(0)
    for i in range(lengths_ref.shape[1]):
        end = end + lengths_ref[0, i]
        start = jnp.where(rows >= end, end, start)
    return start


def rotate(pair, cosine, sine):
    half = HEAD_DIM // 2
    first, second = pair[:half], pair[half:]
    return jnp.concatenate(
        [first * cosine - second * sine, second * cosine + first * sine], axis=0
    )


def enter_kernel(
    lengths_ref, place_ref, small_ref, turn_ref, tokens_in, wq_in, wk_in, wv_in,
    q_ref, kv_ref, normed_ref, tokens_t_ref, cos_ref, sin_ref, tokens_ref, wq_ref, wk_ref, wv_ref, sems,
):
    ins = (tokens_in, wq_in, wk_in, wv_in)
    copies = arriving(zip(ins, (tokens_ref, wq_ref, wk_ref, wv_ref)), sems)
    rows, width = tokens_ref.shape
    q_width = wq_ref.shape[0]
    small = small_ref[...].astype(wide)
    gain = small[:, :width]
    bias = as_column(small[:, width:])
    copies[0].wait()
    hidden = tokens_ref[...].astype(wide)
    inverse = lax.rsqrt(jnp.mean(hidden * hidden, axis=1, keepdims=True) + epsilon)
    normed = (hidden * inverse * gain).astype(low)
    tokens_t_ref[...] = hidden.T.astype(low)
    normed_ref[...] = normed.astype(wide).T.astype(low)
    index = place_ref[0] * rows + lax.broadcasted_iota(jnp.int32, (1, rows), 1)
    position = (index - segment_start(lengths_ref, index)).astype(wide)
    angles = turn_ref[...] * position
    cosine, sine = jnp.cos(angles), jnp.sin(angles)
    cos_ref[...] = cosine
    sin_ref[...] = sine
    for copy in copies[1:]:
        copy.wait()
    q_lin = dot_nt(wq_ref[...], normed) + bias[:q_width]
    for h in range(q_lin.shape[0] // HEAD_DIM):
        head = rotate(q_lin[h * HEAD_DIM : (h + 1) * HEAD_DIM], cosine, sine)
        q_ref[h * HEAD_DIM : (h + 1) * HEAD_DIM, :] = head.astype(low) * low(HEAD_DIM**-0.5)
    k_lin = dot_nt(wk_ref[...], normed) + bias[q_width : q_width + HEAD_DIM]
    v_lin = dot_nt(wv_ref[...], normed) + bias[q_width + HEAD_DIM :]
    kv_ref[...] = jnp.concatenate([rotate(k_lin, cosine, sine), v_lin], axis=0).T.astype(low)


def weights_kernel(
    whole_down, lengths_ref, place_ref, gate_in, up_in, down_in, cotangent_in,
    gate_t_ref, gate_own_ref, up_t_ref, up_own_ref, down_t_ref, down_ref, mine_ref, other_ref,
    gate_ref, up_ref, cotangent_ref, turned_ref, grad_ref, sems,
):
    units = gate_t_ref.shape[0]
    hidden = gate_in.shape[1]
    window = turned_ref.shape[0]
    first = place_ref[0] * units
    base = pl.multiple_of(jnp.minimum(first // 128 * 128, hidden - window), 128)
    down_rows = down_in.at[pl.ds(pl.multiple_of(first, 16), units), :] if whole_down else down_in
    copies = arriving(
        [
            (gate_in.at[:, pl.ds(base, window)], gate_ref),
            (up_in.at[:, pl.ds(base, window)], up_ref),
            (cotangent_in, cotangent_ref),
            (down_rows, down_ref),
        ],
        sems,
    )
    for copy, ref, turned, own in (
        (copies[0], gate_ref, gate_t_ref, gate_own_ref),
        (copies[1], up_ref, up_t_ref, up_own_ref),
    ):
        copy.wait()
        turned_ref[...] = ref[...].astype(wide).T
        part = turned_ref[pl.ds(pl.multiple_of(first - base, 8), units), :]
        turned[...] = part.astype(low)
        own[...] = part.T.astype(low)
    copies[2].wait()
    rows = cotangent_ref.shape[0]
    half = rows // 2
    row = place_ref[0] * rows + lax.broadcasted_iota(jnp.int32, (rows, 1), 0)
    end = jnp.int32(0)
    for i in range(lengths_ref.shape[1]):
        end = end + lengths_ref[0, i]
    grad_ref[...] = jnp.where(row < end, cotangent_ref[...].astype(wide), 0.0)
    core = place_ref[1]
    mine_ref[...] = grad_ref[pl.ds(pl.multiple_of(core * half, half), half), :].astype(low)
    other_ref[...] = grad_ref[pl.ds(pl.multiple_of((1 - core) * half, half), half), :].astype(low)
    copies[3].wait()
    down_t_ref[...] = down_ref[...].astype(wide).T.astype(low)


def mask_bias(key_base, key_rows, q_index, q_start):
    keys = key_base + lax.broadcasted_iota(jnp.int32, (key_rows, q_index.shape[1]), 0)
    return jnp.where((keys >= q_start) & (keys <= q_index), 0.0, masked_value)


def first_row(lengths_ref, row):
    start = jnp.int32(0)
    end = jnp.int32(0)
    for i in range(lengths_ref.shape[1]):
        end = end + lengths_ref[0, i]
        start = jnp.where(row >= end, end, start)
    return start


def attend_kernel(blocks, lengths_ref, place_ref, q_ref, w_out_ref, *refs):
    kv_refs = refs[:blocks]
    out_ref, log_ref, mine_ref, other_ref, kv_ref, acc_ref, max_ref, bias_ref, part_ref, score_ref = refs[blocks:]
    rows = q_ref.shape[1]
    heads = q_ref.shape[0] // HEAD_DIM
    own, core = place_ref[0], place_ref[1]
    for r in range(blocks):
        kv_ref[r] = kv_refs[r][...]
    q_index = own * rows + lax.broadcasted_iota(jnp.int32, (1, rows), 1)
    q_start = segment_start(lengths_ref, q_index)
    acc_ref[...] = jnp.zeros_like(acc_ref)
    max_ref[...] = jnp.full_like(max_ref, masked_value)

    def visit(block, carry):
        pair = kv_ref[block ^ own]
        keys = pair[:, :HEAD_DIM]
        values = pair.astype(wide).T[HEAD_DIM:].astype(low)
        values = jnp.concatenate([values, jnp.ones((16, rows), low)], axis=0)
        bias_ref[...] = mask_bias(block * rows, rows, q_index, q_start)

        def scores(h):
            score_ref[h % 2] = dot_nn(keys, q_ref[h * HEAD_DIM : (h + 1) * HEAD_DIM, :])

        def gather(h, weight, shrink):
            acc_ref[h] = acc_ref[h] * shrink + dot_nn(values, weight)

        scores(0)
        waiting = None
        for h in range(heads):
            if h + 1 < heads:
                scores(h + 1)
            masked = score_ref[h % 2] + bias_ref[...]
            old = max_ref[h : h + 1, :]
            new = jnp.maximum(old, jnp.max(masked, axis=0, keepdims=True))
            weight = jnp.exp(masked - new).astype(low)
            max_ref[h : h + 1, :] = new
            if waiting is not None:
                gather(*waiting)
            waiting = (h, weight, jnp.exp(old - new))
        gather(*waiting)
        return carry

    lax.fori_loop(first_row(lengths_ref, own * rows) // rows, own + 1, visit, 0)
    for h in range(heads):
        total = acc_ref[h, HEAD_DIM : HEAD_DIM + 1, :]
        out_ref[h * HEAD_DIM : (h + 1) * HEAD_DIM, :] = acc_ref[h, :HEAD_DIM, :] / total
        log_ref[h : h + 1, :] = max_ref[h : h + 1, :] + jnp.log(total)
    part_ref[...] = dot_tn(w_out_ref[...], out_ref[...].astype(low))
    half = mine_ref.shape[1]
    mine_ref[...] = part_ref[:, pl.ds(pl.multiple_of(core * half, half), half)]
    other_ref[...] = part_ref[:, pl.ds(pl.multiple_of((1 - core) * half, half), half)].astype(low)


def middle_kernel(place_ref, tokens_ref, part_ref, passed_ref, gain_ref, hidden_ref, normed_ref):
    half = hidden_ref.shape[1]
    mine = pl.ds(pl.multiple_of(place_ref[1] * half, half), half)
    hidden = tokens_ref[:, mine].astype(wide) + part_ref[...] + passed_ref[...].astype(wide)
    hidden_ref[...] = hidden
    inverse = lax.rsqrt(jnp.mean(hidden * hidden, axis=0, keepdims=True) + epsilon)
    normed_ref[...] = (hidden * inverse * as_column(gain_ref[...])).astype(low)


def hidden_kernel(parts, *refs):
    gy_refs, x_refs, refs = refs[: 2 * parts], refs[2 * parts : 4 * parts], refs[4 * parts :]
    gate_t_ref, up_t_ref, down_ref, gate_ref, up_ref = refs[:5]
    mixed_ref, grad_gate_ref, grad_up_ref, other_ref, mine_ref, x_ref, gy_ref = refs[5:]
    half = other_ref.shape[1]
    row = 0
    for k in range(2):
        at = 0
        for x, gy in zip(x_refs[k * parts : (k + 1) * parts], gy_refs[k * parts : (k + 1) * parts]):
            x_ref[at : at + x.shape[0], k * half : (k + 1) * half] = x[...]
            gy_ref[row : row + gy.shape[0], :] = gy[...]
            at += x.shape[0]
            row += gy.shape[0]
    x = x_ref[...]
    gate = dot_nn(gate_t_ref[...], x)
    up = dot_nn(up_t_ref[...], x)
    grad_mixed = dot_nt(down_ref[...], gy_ref[...])
    sigmoid = 1.0 / (1.0 + jnp.exp(-gate))
    silu = gate * sigmoid
    mixed_ref[...] = (silu * up).astype(low)
    grad_gate = (grad_mixed * up * sigmoid * (1.0 + gate * (1.0 - sigmoid))).astype(low)
    grad_up = (grad_mixed * silu).astype(low)
    grad_gate_ref[...] = grad_gate
    grad_up_ref[...] = grad_up
    back = (dot_nn(gate_ref[...], grad_gate) + dot_nn(up_ref[...], grad_up)).astype(low)
    other_ref[...] = back[:, :half]
    mine_ref[...] = back[:, half:]


def weight_kernel(transposed, first, counts, outputs, *refs):
    blocks = len(counts)
    lefts, parts, out_refs, right_ref = refs[:blocks], refs[blocks : -outputs - 1], refs[-outputs - 1 : -1], refs[-1]
    units = lefts[0].shape[0]
    columns = sum(ref.shape[0] for ref in out_refs) // units * 128
    last = first + columns
    total, at = None, 0
    for r in range(blocks):
        row = 0
        for k in range(2):
            place = 0
            for part in parts[at : at + counts[r]]:
                if transposed:
                    half = part.shape[1]
                    start, end = max(place, first), min(place + part.shape[0], last)
                    if start < end:
                        right_ref[r, start - first : end - first, k * half : (k + 1) * half] = part[
                            start - place : end - place, :
                        ]
                    place += part.shape[0]
                else:
                    right_ref[r, row : row + part.shape[0], :] = part[:, first:last]
                    row += part.shape[0]
            at += counts[r]
        left, right = lefts[r][...], right_ref[r]
        product = dot_nt(left, right) if transposed else dot_nn(left, right)
        total = product if total is None else total + product
    at = 0
    for out_ref in out_refs:
        for t in range(out_ref.shape[0] // units):
            out_ref[t * units : (t + 1) * units, :] = total[:, at : at + 128].astype(low)
            at += 128


def project_kernel(blocks, weight_ref, *refs):
    other_ref, mine_refs = refs[blocks], refs[blocks + 1 :]
    half = other_ref.shape[2]
    for r in range(blocks):
        part = dot_nn(weight_ref[...], refs[r][...]).astype(low)
        other_ref[r] = part[:, :half]
        mine_refs[r][...] = part[:, half:]


def add_kernel(*refs):
    count = (len(refs) - 1) // 2
    for i in range(count):
        refs[1 + count + i][...] = (refs[1 + i][...].astype(wide) + refs[0][i].astype(wide)).astype(low)


def pair_kernel(*refs):
    count = len(refs) // 3
    for i in range(count):
        refs[2 * count + i][...] = (refs[2 * i][...].astype(wide) + refs[2 * i + 1][...].astype(wide)).astype(low)


def join_kernel(place_ref, mine_ref, other_ref, out_ref):
    half = mine_ref.shape[0]
    core = place_ref[1]
    out_ref[pl.ds(pl.multiple_of(core * half, half), half), :] = mine_ref[...].astype(out_ref.dtype)
    out_ref[pl.ds(pl.multiple_of((1 - core) * half, half), half), :] = other_ref[...].astype(out_ref.dtype)


def wait_kernel(*refs):
    pass


def tick_kernel(ops, place_ref, *refs):
    ins, outs = refs[: -len(ops)], refs[-len(ops) :]
    end = (place_ref[2] == 0) | (place_ref[2] == 3)
    for (kind, args), out_ref in zip(ops, outs):
        sources = [(ins if given else outs)[i] for given, i, *_ in args]
        if kind == "add":
            out_ref[...] = (sources[0][...].astype(wide) + sources[1][...].astype(wide)).astype(low)
        elif kind == "pick":
            out_ref[...] = jnp.where(end, sources[0][...], sources[1][...])
        else:
            at = 0
            for source, (_, _, start, rows) in zip(sources, args):
                out_ref[at : at + rows, :] = source[start : start + rows, :]
                at += rows


def sum_blocks(refs, starts=None, rows=None):
    total = None
    for i, ref in enumerate(refs):
        value = ref[...] if starts is None else ref[starts[i] : starts[i] + rows, :]
        total = value.astype(wide) if total is None else total + value.astype(wide)
    return total


def layer_kernel(hidden_ref, *refs):
    out_ref = refs[-1]
    out_ref[...] = (hidden_ref[...] + sum_blocks(refs[:-1])).T.astype(low)


def grad_middle_kernel(hidden_ref, gain_ref, gy_ref, *refs):
    grad_ref, grad_low_ref, grad_gain_ref = refs[-3:]
    hidden = hidden_ref[...]
    inverse = lax.rsqrt(jnp.mean(hidden * hidden, axis=0, keepdims=True) + epsilon)
    grad_normed = sum_blocks(refs[:-3])
    weighted = as_column(gain_ref[...]) * grad_normed
    inner = jnp.mean(weighted * hidden, axis=0, keepdims=True)
    grad = inverse * weighted - hidden * (inverse * inverse * inverse * inner)
    grad = grad + gy_ref[...].astype(wide).T
    grad_ref[...] = grad
    grad_low_ref[...] = grad.astype(low)
    grad_gain_ref[...] = as_row(jnp.sum(grad_normed * hidden * inverse, axis=1, keepdims=True))


def back_enter_kernel(
    place_ref, gm_mine_ref, gm_other_ref, w_out_ref, out_ref, go_ref, delta_ref, gm_ref
):
    half = gm_mine_ref.shape[1]
    core = place_ref[1]
    gm_ref[:, pl.ds(pl.multiple_of(core * half, half), half)] = gm_mine_ref[...]
    gm_ref[:, pl.ds(pl.multiple_of((1 - core) * half, half), half)] = gm_other_ref[...]
    grad_out = dot_nn(w_out_ref[...], gm_ref[...]).astype(low)
    go_ref[...] = grad_out
    product = grad_out.astype(wide) * out_ref[...]
    for h in range(product.shape[0] // HEAD_DIM):
        delta_ref[h : h + 1, :] = jnp.sum(
            product[h * HEAD_DIM : (h + 1) * HEAD_DIM], axis=0, keepdims=True
        )


def attend_back_kernel(
    blocks, tile, lengths_ref, place_ref, go_ref, delta_ref, log_ref, q_ref, cos_ref, sin_ref, *refs,
):
    kv_refs, refs = refs[:blocks], refs[blocks:]
    (grad_q_ref, *grad_kv_refs), refs = refs[: blocks + 1], refs[blocks + 1 :]
    kv_ref, bias_ref, dq_ref, q_all_ref, go_all_ref, weight_ref, grad_ref, grad_kv_ref, score_ref, grad_weight_ref = refs
    rows = q_ref.shape[1]
    heads = grad_q_ref.shape[0] // HEAD_DIM
    own = place_ref[0]
    parts = rows // tile

    def lanes(h):
        return slice(h * rows, (h + 1) * rows)

    def span(h):
        return slice(h * HEAD_DIM, (h + 1) * HEAD_DIM)

    for r in range(blocks):
        kv_ref[r] = kv_refs[r][...]
        grad_kv_ref[r] = jnp.zeros_like(grad_kv_ref[r])
    for h in range(heads):
        q_all_ref[:, lanes(h)] = q_ref[span(h), :]
        go_all_ref[:, lanes(h)] = go_ref[span(h), :]
    dq_ref[...] = jnp.zeros_like(dq_ref)
    q_index = own * rows + lax.broadcasted_iota(jnp.int32, (1, rows), 1)
    q_start = segment_start(lengths_ref, q_index)

    def visit(block, carry):
        part = pl.multiple_of(block % parts * tile, tile)
        at = ((block // parts) ^ own, pl.ds(part, tile), slice(None))
        pair = kv_ref[at]
        keys = pair[:, :HEAD_DIM]
        values = pair[:, HEAD_DIM:]
        keys_t = pair.astype(wide).T[:HEAD_DIM].astype(low)
        bias_ref[...] = mask_bias(block * tile, tile, q_index, q_start)

        def products(h):
            score_ref[h % 2] = dot_nn(keys, q_all_ref[:, lanes(h)])
            grad_weight_ref[h % 2] = dot_nn(values, go_all_ref[:, lanes(h)])

        products(0)
        for h in range(heads):
            if h + 1 < heads:
                products(h + 1)
            weight = jnp.exp(score_ref[h % 2] + bias_ref[...] - log_ref[h : h + 1, :])
            grad = (weight * (grad_weight_ref[h % 2] - delta_ref[h : h + 1, :])).astype(low)
            weight_ref[:, lanes(h)] = weight.astype(low)
            grad_ref[:, lanes(h)] = grad
            dq_ref[span(h), :] += dot_nn(keys_t, grad)
        grad_keys = dot_nt(grad_ref[...], q_all_ref[...])
        grad_values = dot_nt(weight_ref[...], go_all_ref[...])
        grad_kv_ref[at] = jnp.concatenate([grad_keys, grad_values], axis=1).astype(low)
        return carry

    lax.fori_loop(first_row(lengths_ref, own * rows) // tile, (own + 1) * parts, visit, 0)
    for r in range(blocks):
        grad_kv_refs[r][...] = grad_kv_ref[r]
    for h in range(heads):
        turned = rotate(dq_ref[span(h), :] * HEAD_DIM**-0.5, cos_ref[...], -sin_ref[...])
        grad_q_ref[span(h), :] = turned.astype(low)


def query_kernel(
    place_ref, normed_ref, grad_q_ref, wq_ref, gm_mine_ref, gm_other_ref, out_ref,
    grad_wq_ref, part_ref, grad_bq_ref, grad_w_out_ref, gm_ref,
):
    half = gm_mine_ref.shape[1]
    core = place_ref[1]
    gm_ref[:, pl.ds(pl.multiple_of(core * half, half), half)] = gm_mine_ref[...]
    gm_ref[:, pl.ds(pl.multiple_of((1 - core) * half, half), half)] = gm_other_ref[...]
    grad_w_out_ref[...] = dot_nt(out_ref[...].astype(low), gm_ref[...]).astype(low)
    grad_q = grad_q_ref[...]
    grad_wq_ref[...] = dot_nt(grad_q, normed_ref[...]).astype(low)
    part_ref[...] = dot_tn(wq_ref[...], grad_q)
    grad_bq_ref[...] = dot_nt(jnp.ones((16, grad_q.shape[1]), low), grad_q)


def key_kernel(
    blocks, starts, place_ref, normed_ref, tokens_ref, part_ref, wk_ref, wv_ref, cos_ref, sin_ref,
    grad_wq_ref, grad_bq_ref, grad_w_out_ref, grad_gain_two_ref, *refs,
):
    kv_refs, share_refs, (mine_ref, other_ref, sum_ref, pack_ref) = refs[:blocks], refs[blocks : 2 * blocks], refs[2 * blocks :]
    both = sum_blocks(kv_refs, starts, tokens_ref.shape[1]).T
    both = jnp.concatenate(
        [rotate(both[:HEAD_DIM], cos_ref[...], -sin_ref[...]), both[HEAD_DIM:]], axis=0
    ).astype(low)
    total = part_ref[...] + dot_tn(wk_ref[...], both[:HEAD_DIM]) + dot_tn(wv_ref[...], both[HEAD_DIM:])
    sum_ref[...] = total
    half = mine_ref.shape[1]
    core = place_ref[1]
    mine_ref[...] = sum_ref[:, pl.ds(pl.multiple_of(core * half, half), half)]
    other_ref[...] = sum_ref[:, pl.ds(pl.multiple_of((1 - core) * half, half), half)].astype(low)
    hidden = tokens_ref[...].astype(wide)
    inverse = lax.rsqrt(jnp.mean(hidden * hidden, axis=0, keepdims=True) + epsilon)
    q_width, width = grad_wq_ref.shape
    kv_width = both.shape[0]
    at = 0
    pack_ref[at : at + q_width, :] = grad_wq_ref[...]
    at += q_width
    pack_ref[at : at + kv_width, :] = dot_nt(both, normed_ref[...]).astype(low)
    at += kv_width
    pack_ref[at : at + q_width, :] = grad_w_out_ref[...]
    at += q_width
    grad_gain = as_row(jnp.sum(total * (hidden * inverse), axis=1, keepdims=True))
    grad_bkv = dot_nt(jnp.ones((16, both.shape[1]), low), both)[:1]
    biases = jnp.concatenate(
        [grad_bq_ref[:1, :], grad_bkv, jnp.zeros((1, width - q_width - kv_width), wide)], axis=1
    )
    small = jnp.concatenate(
        [grad_gain, grad_gain_two_ref[...], biases, jnp.zeros((pack_ref.shape[0] - at - 3, width), wide)], axis=0
    )
    pack_ref[at:, :] = small.astype(low)
    share = pack_ref.shape[0] // blocks
    for r in range(blocks):
        start = pl.multiple_of((place_ref[0] ^ r) * share, share)
        for t in range(width // 128):
            share_refs[r][t * share : (t + 1) * share, :] = pack_ref[pl.ds(start, share), t * 128 : (t + 1) * 128]


def share_kernel(starts, *refs):
    refs[-1][...] = sum_blocks(refs[:-1], starts, refs[-1].shape[0]).astype(low)


def unpack_kernel(share, sources, place_ref, *refs):
    pieces, outs, (stack_ref, pack_ref) = refs[: len(sources)], refs[len(sources) : -2], refs[-2:]
    for ref, (r, first, rows, start) in zip(pieces, sources):
        stack_ref[r, first : first + rows, :] = ref[start : start + rows, :].astype(wide)
    for r in range(stack_ref.shape[0]):
        at = pl.ds(pl.multiple_of((place_ref[0] ^ r) * share, 8), share)
        for t in range(stack_ref.shape[1] // share):
            pack_ref[at, t * 128 : (t + 1) * 128] = stack_ref[r, t * share : (t + 1) * share, :]
    at = 0
    for out_ref in outs:
        out_ref[...] = pack_ref[at : at + out_ref.shape[0], :]
        at += out_ref.shape[0]


def leave_kernel(place_ref, tokens_ref, mine_ref, passed_ref, gain_ref, grad_mid_ref, out_ref):
    half = mine_ref.shape[1]
    hidden = tokens_ref[:, pl.ds(pl.multiple_of(place_ref[1] * half, half), half)].astype(wide)
    inverse = lax.rsqrt(jnp.mean(hidden * hidden, axis=0, keepdims=True) + epsilon)
    weighted = as_column(gain_ref[...]) * (mine_ref[...] + passed_ref[...].astype(wide))
    inner = jnp.mean(weighted * hidden, axis=0, keepdims=True)
    grad = grad_mid_ref[...] + inverse * weighted - hidden * (inverse * inverse * inverse * inner)
    out_ref[...] = grad.T.astype(low)


def place_kernel(transposed, tiles, place_ref, refs, out_ref, all_ref):
    own_ref, near_x_ref, near_y_ref, *far_refs = refs
    step, tiles = tiles
    units = own_ref.shape[0]
    half = units // 2
    for r, ref in enumerate((own_ref, near_x_ref, near_y_ref)):
        start = pl.multiple_of((place_ref[0] ^ r) * units, 8)
        all_ref[pl.ds(start, units), :] = ref[...].astype(wide)
    for k in range(2):
        start = pl.multiple_of((place_ref[0] ^ 3) * units + k * half, 8)
        part = 2 * step + k

        @pl.when(part < tiles)
        def _(start=start, k=k):
            all_ref[pl.ds(start, half), :] = far_refs[k][...].astype(wide)

        @pl.when(part >= tiles)
        def _(start=start, k=k):
            all_ref[pl.ds(start, half), :] = far_refs[2 + k][...].astype(wide)

    if transposed:
        out_ref[...] = all_ref[...].T


def place_shares(place, shares, units, transposed, width, at, whole, last):
    tile, half = 128, units // 2
    counts = [share[0].shape[0] // units for share in shares]
    begins = [sum(counts[:i]) for i in range(len(counts))]
    first = at // tile
    ins, specs = [place], [in_smem]
    for (own, near_x, near_y, far_y, far_x), tiles, begin in zip(shares, counts, begins):

        def step_of(i, tiles=tiles, begin=begin):
            return jnp.clip(i - begin, 0, tiles - 1)

        def halves(start, k, later, tiles=tiles, step_of=step_of):
            def index(i):
                part = 2 * step_of(i) + k - (tiles if later else 0)
                return (start // half + jnp.clip(part, 0, tiles - 1), 0)

            return pl.BlockSpec((half, tile), index)

        ins += [own, near_x, near_y, far_y[0], far_y[0], far_x[0], far_x[0]]
        specs += [pl.BlockSpec((units, tile), lambda i, step_of=step_of: (step_of(i), 0))] * 3
        specs += [halves(far_y[1], k, False) for k in range(2)]
        specs += [halves(far_x[1], k, True) for k in range(2)]
    ins += last
    specs += [pl.BlockSpec(memory_space=pl.ANY)] * len(last)
    aliases = {}
    if whole is not None:
        aliases = {len(ins): 0}
        ins.append(whole)
        specs.append(pl.BlockSpec(memory_space=pl.ANY))

    def body(*refs):
        out_ref, token_ref = refs[len(ins) : len(ins) + 2]
        all_ref = refs[-1] if transposed else out_ref
        token_ref[...] = jnp.zeros_like(token_ref)
        for n, (tiles, begin) in enumerate(zip(counts, begins)):
            step = pl.program_id(0) - begin

            @pl.when((step >= 0) & (step < tiles))
            def _(n=n, step=step, tiles=tiles):
                place_kernel(transposed, (step, tiles), refs[0], refs[1 + 7 * n : 8 + 7 * n], out_ref, all_ref)

    if transposed:
        dims = (width, 4 * units)
        out_spec = pl.BlockSpec((tile, 4 * units), lambda i: (i + first, 0))
        scratch = [pltpu.VMEM((4 * units, tile), wide)]
    else:
        dims = (4 * units, width)
        out_spec = pl.BlockSpec((4 * units, tile), lambda i: (0, i + first))
        scratch = []
    return pl.pallas_call(
        body,
        name="place_kernel",
        out_shape=(shape(dims, wide), shape((8, 128), wide)),
        grid=(sum(counts),),
        in_specs=specs,
        out_specs=(out_spec, pl.BlockSpec((8, 128), lambda i: (0, 0))),
        scratch_shapes=scratch,
        input_output_aliases=aliases,
        cost_estimate=pl.CostEstimate(flops=0, bytes_accessed=0, transcendentals=0),
        compiler_params=pltpu.CompilerParams(vmem_limit_bytes=vmem_limit),
    )(*ins)


def local(
    tokens,
    lengths,
    norm1_gain,
    w_query,
    b_query,
    w_key,
    b_key,
    w_value,
    b_value,
    w_out,
    norm2_gain,
    w_gate,
    w_up,
    w_down,
    cotangent,
):
    rows, width = tokens.shape
    half = rows // 2
    blocks = lax.axis_size("blk")
    own_block = lax.axis_index("blk")
    own_core = lax.axis_index("tensor")
    q_width = w_query.shape[1]
    heads = q_width // HEAD_DIM
    units = w_gate.shape[1] // blocks
    place = jnp.stack([own_block, own_core, lax.axis_index("dp")]).astype(jnp.int32)
    gain_two = norm2_gain.reshape(1, width)
    key_tile = rows // 2

    half_dim = HEAD_DIM // 2
    turn = (rope_base ** (-2.0 * jnp.arange(half_dim, dtype=wide) / HEAD_DIM)).reshape(half_dim, 1)
    small = jnp.concatenate([norm1_gain, b_query, b_key, b_value]).reshape(1, -1)
    q_t, key_value, normed_t, tokens_t, cosine, sine = call(
        enter_kernel,
        [
            shape((q_width, rows), low),
            shape((rows, 2 * HEAD_DIM), low),
            shape((width, rows), low),
            shape((width, rows), low),
            shape((half_dim, rows), wide),
            shape((half_dim, rows), wide),
        ],
        [lengths, place, small, turn, tokens, w_query.T, w_key.T, w_value.T],
        [
            pltpu.VMEM((rows, width), low),
            pltpu.VMEM((q_width, width), low),
            pltpu.VMEM((HEAD_DIM, width), low),
            pltpu.VMEM((HEAD_DIM, width), low),
            pltpu.SemaphoreType.DMA((4,)),
        ],
        in_specs=[in_smem] * 2 + [in_vmem] * 2 + [in_hbm] * 4,
    )
    kv_blocks = gather_blocks(key_value, "kv")

    window = -(-(units + 127) // 128) * 128
    whole_down = units % 16 == 0
    down = w_down if whole_down else lax.dynamic_slice_in_dim(w_down, own_block * units, units, 0)
    gate_t, gate_own, up_t, up_own, down_t, down_own, grad_y_mine, grad_y_other = call(
        functools.partial(weights_kernel, whole_down),
        [
            shape((units, width), low),
            shape((width, units), low),
            shape((units, width), low),
            shape((width, units), low),
            shape((width, units), low),
            shape((units, width), low),
            shape((half, width), low),
            shape((half, width), low),
        ],
        [lengths, place, w_gate, w_up, down, cotangent],
        [
            pltpu.VMEM((width, window), low),
            pltpu.VMEM((width, window), low),
            pltpu.VMEM((rows, width), low),
            pltpu.VMEM((window, width), wide),
            pltpu.VMEM((rows, width), wide),
            pltpu.SemaphoreType.DMA((4,)),
        ],
        in_specs=[in_smem] * 2 + [in_hbm] * 4,
        after=[q_t],
    )
    gy_near = {r: partner(grad_y_mine, "blk", r, "gy") for r in range(1, blocks) if r & (r - 1) == 0}

    out_t, log_total, part_mine, part_other = call(
        functools.partial(attend_kernel, blocks),
        [
            shape((q_width, rows), wide),
            shape((heads + 1, rows), wide),
            shape((width, half), wide),
            shape((width, half), low),
        ],
        [lengths, place, q_t, w_out] + kv_blocks,
        [
            pltpu.VMEM((blocks, rows, 2 * HEAD_DIM), low),
            pltpu.VMEM((heads, HEAD_DIM + 16, rows), wide),
            pltpu.VMEM((heads + 1, rows), wide),
            pltpu.VMEM((rows, rows), wide),
            pltpu.VMEM((width, rows), wide),
            pltpu.VMEM((2, rows, rows), wide),
        ],
        in_specs=[in_smem] * 2 + [in_vmem] * (2 + blocks),
        after=[gate_t],
    )
    hidden, normed_two = call(
        middle_kernel,
        [shape((width, half), wide), shape((width, half), low)],
        [place, tokens_t, part_mine, partner(part_other, "tensor", 1, "part_core"), gain_two],
        in_specs=[in_smem] + [in_vmem] * 4,
        after=list(gy_near.values()),
    )

    last = [normed_two]

    def ordered(body, outs, ins, needs=(), **more):
        nonlocal last
        carry = more.get("carry", ())
        after = [v for v in last + list(needs) if not any(v is c for c in carry)]
        results = call(body, outs, ins, after=after, **more)
        last = [results[0]]
        return results

    def wait(carry, needs=()):
        return list(ordered(wait_kernel, [], [], needs=needs, carry=carry))

    def near(pieces):
        return [p for r, parts in enumerate(pieces) if r and r & (r - 1) == 0 for p in parts]

    def far(pieces):
        return [p for r, parts in enumerate(pieces) if r & (r - 1) for p in parts]

    kept = shape((units, rows), low)
    piece = shape((width, half), low)
    runs, back, passed = [], [None] * blocks, [None] * blocks

    def cores(parts, name):
        return [partner(part, "tensor", 1, name) for part in parts]

    x_parts, gy_parts = [], []

    def hidden_units(r, x_mine, x_other, gy_mine, gy_other):
        x_parts.append(x_other + x_mine)
        gy_parts.append(gy_other + gy_mine)
        runs.append(
            ordered(
                functools.partial(hidden_kernel, len(x_mine)),
                [kept, kept, kept, piece, piece],
                gy_parts[-1] + x_parts[-1] + [gate_t, up_t, down_own, gate_own, up_own],
                scratch=[pltpu.VMEM((width, rows), low), pltpu.VMEM((rows, width), low)],
            )
        )
        return runs[-1][3]

    def add_back(members, carry, needs=()):
        results = ordered(
            pair_kernel,
            [piece] * len(members),
            [value for r in members for value in (runs[r][4], passed[r])],
            needs=needs,
            carry=carry,
        )
        for r, value in zip(members, results):
            back[r] = partner(value, "blk", r, "back") if r else value
        return results[len(members) :]

    def hidden_weight(transposed, left, parts, first, shares):
        counts = [len(part) // 2 for part in parts]
        columns = sum(shares)
        dims = (columns, rows) if transposed else (rows, columns)
        return ordered(
            functools.partial(weight_kernel, transposed, first, counts, len(shares)),
            [shape((share // 128 * units, 128), low) for share in shares],
            [run[left] for run in runs] + sum(parts, []),
            scratch=[pltpu.VMEM((blocks,) + dims, low)],
        )

    def tick(ops, needs=(), carry=()):
        given, outs, listed = [], [], []
        for kind, *args in ops:
            spans = [arg if isinstance(arg, tuple) else (arg, 0, None) for arg in args]
            named, size = [], 0
            for value, start, count in spans:
                if isinstance(value, int):
                    entry, total = (False, value), outs[value].shape[0]
                else:
                    found = [i for i, known in enumerate(given) if known is value]
                    if not found:
                        given.append(value)
                    entry = (True, found[0] if found else len(given) - 1)
                    total = value.shape[0]
                count = total if count is None else count
                named.append(entry + (start, count))
                size = size + count if kind == "cat" else count
            listed.append((kind, named))
            outs.append(shape((size, 128), low))
        return ordered(
            functools.partial(tick_kernel, listed),
            outs,
            [place] + given,
            in_specs=[in_smem] + [in_vmem] * len(given),
            needs=needs,
            carry=carry,
        )

    x_near = {r: partner(normed_two, "blk", r, "x") for r in range(1, blocks) if r & (r - 1) == 0}
    other = hidden_units(
        0, [normed_two], cores([normed_two], "x_core"), [grad_y_mine], [grad_y_other]
    )
    other, *arrived = wait([other] + list(x_near.values()))
    passed[0] = partner(other, "tensor", 1, "back_core")
    x_near = dict(zip(x_near, arrived))
    x_mine = relay_far(x_near, normed_two, "x")
    gy_mine = relay_far(gy_near, grad_y_mine, "gy")
    x_other = {r: cores(parts, "x_core") for r, parts in x_mine.items() if r in x_near}
    gy_other = {r: cores(parts, "gy_core") for r, parts in gy_mine.items() if r in x_near}
    others = [hidden_units(r, x_mine[r], x_other[r], gy_mine[r], gy_other[r]) for r in x_near]
    fars = [r for r in x_mine if r not in x_near]
    parts = [part for r in fars for part in x_mine[r] + gy_mine[r]]
    results = wait(others + parts)
    for r in x_near:
        passed[r] = partner(results.pop(0), "tensor", 1, "back_core")
    for r in fars:
        x_mine[r] = [results.pop(0) for _ in x_mine[r]]
        gy_mine[r] = [results.pop(0) for _ in gy_mine[r]]
        x_other[r], gy_other[r] = cores(x_mine[r], "x_core"), cores(gy_mine[r], "gy_core")
    others = [hidden_units(r, x_mine[r], x_other[r], gy_mine[r], gy_other[r]) for r in fars]
    for r, other in zip(fars, add_back(list(x_near), others)):
        passed[r] = partner(other, "tensor", 1, "back_core")
    if len(fars) > 1:
        add_back(fars[:-1], [])
    cut_at = width // 2 // 128 * 128
    (d1,) = hidden_weight(False, 0, gy_parts, 0, [cut_at])
    d1_swap = swap(d1, "swap_d1")
    (d2,) = hidden_weight(False, 0, gy_parts, cut_at, [width - cut_at])
    layer_other, *layer_mine = ordered(
        functools.partial(project_kernel, blocks),
        [shape((blocks, width, half), low)] + [piece] * blocks,
        [down_t] + [run[0] for run in runs],
    )
    d2, layer_other = add_back(
        [blocks - 1, 0], [d2, layer_other], needs=back[1 : blocks - 1] + [d1_swap]
    )
    (d1_sum,) = tick([("add", d1, d1_swap)])
    d1_cross, d2_swap = cross(d1_sum, "cross_d1"), swap(d2, "swap_d2")
    layer_passed = partner(layer_other, "tensor", 1, "layer_core")
    g1, g2 = hidden_weight(True, 1, x_parts, 0, [cut_at, width - cut_at])
    u1, u2 = hidden_weight(True, 2, x_parts, 0, [cut_at, width - cut_at])
    d1_sum, d2_sum, d1_g1 = tick(
        [("add", d1_sum, d1_cross), ("add", d2, d2_swap), ("pick", g1, 0)], needs=back[1:]
    )
    grad_mid, grad_mid_low, grad_gain_two = ordered(
        grad_middle_kernel,
        [shape((width, half), wide), piece, shape((1, width), wide)],
        [hidden, gain_two, grad_y_mine] + back,
    )
    *layer_pieces, grad_mid_low, d1_g1, d2_sum = ordered(
        add_kernel, [piece] * blocks, [layer_passed] + layer_mine, carry=[grad_mid_low, d1_g1, d2_sum]
    )
    grad_mid_other = partner(grad_mid_low, "tensor", 1, "mid_core")
    layer_pieces = scatter_blocks(layer_pieces, "layer")
    d1_g1_swap, d2_cross = swap(d1_g1, "swap_d1_g1"), cross(d2_sum, "cross_d2")

    grad_out, delta = ordered(
        back_enter_kernel,
        [shape((q_width, rows), low), shape((heads + 1, rows), wide)],
        [place, grad_mid_low, grad_mid_other, w_out, out_t],
        scratch=[pltpu.VMEM((width, rows), low)],
        in_specs=[in_smem] + [in_vmem] * 4,
    )

    grad_q, *grad_kv = ordered(
        functools.partial(attend_back_kernel, blocks, key_tile),
        [shape((q_width, rows), low)] + [shape((rows, 2 * HEAD_DIM), low)] * blocks,
        [lengths, place, grad_out, delta, log_total, q_t, cosine, sine] + kv_blocks,
        scratch=[
            pltpu.VMEM((blocks, rows, 2 * HEAD_DIM), low),
            pltpu.VMEM((key_tile, rows), wide),
            pltpu.VMEM((q_width, rows), wide),
            pltpu.VMEM((HEAD_DIM, heads * rows), low),
            pltpu.VMEM((HEAD_DIM, heads * rows), low),
            pltpu.VMEM((key_tile, heads * rows), low),
            pltpu.VMEM((key_tile, heads * rows), low),
            pltpu.VMEM((blocks, rows, 2 * HEAD_DIM), low),
            pltpu.VMEM((2, key_tile, rows), wide),
            pltpu.VMEM((2, key_tile, rows), wide),
        ],
        in_specs=[in_smem] * 2 + [in_vmem] * (6 + blocks),
    )
    pack_rows = -(-(2 * q_width + 2 * HEAD_DIM + 3) // (16 * blocks)) * 16 * blocks
    share = pack_rows // blocks
    stack_rows = share * (width // 128)

    def query_back():
        return ordered(
            query_kernel,
            [
                shape((q_width, width), low),
                shape((width, rows), wide),
                shape((16, q_width), wide),
                shape((q_width, width), low),
            ],
            [place, normed_t, grad_q, w_query.T, grad_mid_low, grad_mid_other, out_t],
            scratch=[pltpu.VMEM((width, rows), low)],
            in_specs=[in_smem] + [in_vmem] * 6,
        )

    def key_back(kv_pieces, starts):
        return ordered(
            functools.partial(key_kernel, blocks, starts),
            [shape((stack_rows, 128), low)] * blocks + [shape((width, half), wide), shape((width, half), low)],
            [
                place, normed_t, tokens_t, normed_part, w_key.T, w_value.T, cosine, sine,
                grad_w_query, grad_b_query, grad_w_out, grad_gain_two,
            ] + kv_pieces,
            scratch=[pltpu.VMEM((width, rows), wide), pltpu.VMEM((pack_rows, width), low)],
            in_specs=[in_smem] + [in_vmem] * (11 + blocks),
        )

    def sum_share(pieces, starts):
        (own,) = ordered(
            functools.partial(share_kernel, starts), [shape((stack_rows, 128), low)], pieces
        )
        return own

    def leave(normed_mine, normed_passed):
        (grad_half,) = ordered(
            leave_kernel,
            [shape((half, width), low)],
            [place, tokens_t, normed_mine, normed_passed, norm1_gain.reshape(1, width), grad_mid],
            in_specs=[in_smem] + [in_vmem] * 5,
        )
        return grad_half

    def join(mine, other, kind):
        (whole,) = ordered(
            join_kernel,
            [shape((rows, width), kind)],
            [place, mine.astype(kind), other.astype(kind)],
            in_specs=[in_smem] + [in_vmem] * 2,
        )
        return whole

    def layer_leave():
        (layer_half,) = ordered(layer_kernel, [shape((half, width), low)], [hidden] + layer_pieces)
        return layer_half

    def unpack(pieces, sources):
        return ordered(
            functools.partial(unpack_kernel, share, sources),
            [
                shape((q_width, width), wide),
                shape((HEAD_DIM, width), wide),
                shape((HEAD_DIM, width), wide),
                shape((q_width, width), wide),
                shape((pack_rows - 2 * q_width - 2 * HEAD_DIM, width), wide),
            ],
            [place] + pieces,
            scratch=[pltpu.VMEM((blocks, stack_rows, 128), wide), pltpu.VMEM((pack_rows, width), wide)],
            in_specs=[in_smem] + [in_vmem] * len(pieces),
        )

    if blocks != 4:
        kv_pieces = scatter_blocks(grad_kv, "grad_kv")
        grad_w_query, normed_part, grad_b_query, grad_w_out = query_back()
        *shares, normed_mine, normed_other = key_back(kv_pieces, [0] * blocks)
        layer_half = layer_leave()
        layer_out = join(layer_half, partner(layer_half, "tensor", 1, "rows_core"), low)
        grad_half = leave(normed_mine, partner(normed_other, "tensor", 1, "normed_core"))
        grad_tokens = join(grad_half, partner(grad_half, "tensor", 1, "rows_core"), wide)
        own_share = sum_share(scatter_blocks(shares, "shares"), [0] * blocks)
        own_share = lax.psum(own_share, "dp")
        pieces = gather_blocks(own_share, "all_share")
        grad_w_query, grad_w_key, grad_w_value, grad_w_out, small = unpack(
            pieces, [(r, 0, stack_rows, 0) for r in range(blocks)]
        )

        def gather_weight(first, second, transposed):
            stacked = lax.psum(jnp.concatenate([first, second], axis=0), "dp")
            every = lax.all_gather(stacked, "blk").reshape(blocks, width // 128, units, 128)
            order = (1, 3, 0, 2) if transposed else (0, 2, 1, 3)
            dims = (width, blocks * units) if transposed else (blocks * units, width)
            return every.transpose(order).reshape(dims).astype(wide)

        grad_w_down = gather_weight(d1, d2, False)
        grad_w_gate = gather_weight(g1, g2, True)
        grad_w_up = gather_weight(u1, u2, True)
    else:
        r1, r2 = d1.shape[0], d2.shape[0]
        h1, h2 = r1 // 2, r2 // 2

        def both_ways(x_buffer, y_buffer, name):
            return partner(x_buffer, "blk", 1, name + "_x"), partner(y_buffer, "blk", 2, name + "_y")

        d1_all, g1_sum, d2_sum, d2_g2, x1, y1, kv_far = tick(
            [
                ("pick", d1_g1_swap, d1_sum),
                ("add", g1, d1_g1_swap),
                ("add", d2_sum, d2_cross),
                ("pick", g2, 2),
                ("cat", 0, grad_kv[1]),
                ("cat", 0, grad_kv[2]),
            ],
            needs=layer_pieces[1:],
            carry=[grad_kv[3]],
        )
        x1, y1 = both_ways(x1, y1, "d1")
        kv_far = partner(kv_far, "blk", 3, "grad_kv")
        d2_g2_swap, g1_cross = swap(d2_g2, "swap_d2_g2"), cross(g1_sum, "cross_g1")
        grad_w_query, normed_part, grad_b_query, grad_w_out = query_back()
        layer_half = layer_leave()
        d2_all, g2_sum, g1_sum, g1_u1, x2, y2, layer_half = tick(
            [
                ("pick", d2_g2_swap, d2_sum),
                ("add", g2, d2_g2_swap),
                ("add", g1_sum, g1_cross),
                ("pick", u1, 2),
                ("cat", 0, (y1, h1, h1)),
                ("cat", 0, (x1, 0, h1)),
            ],
            needs=[x1, y1, kv_far],
            carry=[layer_half],
        )
        x2, y2 = both_ways(x2, y2, "d2")
        g1_u1_swap, g2_cross = swap(g1_u1, "swap_g1_u1"), cross(g2_sum, "cross_g2")
        layer_passed = partner(layer_half, "tensor", 1, "rows_core")
        *shares, normed_mine, normed_other = key_back([grad_kv[0], x1, y1, kv_far], [0, r1, r1, 0])
        g1_all, u1_sum, g2_sum, g2_u2, x3, y3, share_far, normed_other = tick(
            [
                ("pick", g1_u1_swap, g1_sum),
                ("add", u1, g1_u1_swap),
                ("add", g2_sum, g2_cross),
                ("pick", u2, 2),
                ("cat", 0, (y2, h2, h2), shares[1]),
                ("cat", 0, (x2, 0, h2), shares[2]),
            ],
            needs=[x2, y2],
            carry=[shares[3], normed_other],
        )
        x3, y3 = both_ways(x3, y3, "g1")
        share_far = partner(share_far, "blk", 3, "shares")
        g2_u2_swap, u1_cross = swap(g2_u2, "swap_g2_u2"), cross(u1_sum, "cross_u1")
        normed_passed = partner(normed_other, "tensor", 1, "normed_core")
        layer_out = join(layer_half, layer_passed, low)
        grad_half = leave(normed_mine, normed_passed)
        own_share = sum_share([shares[0], x3, y3, share_far], [0, r1 + h2, r1 + h2, 0])
        g2_all, u2_sum, u1_sum, x4, y4, own_share, grad_half = tick(
            [
                ("pick", g2_u2_swap, g2_sum),
                ("add", u2, g2_u2_swap),
                ("add", u1_sum, u1_cross),
                ("cat", 0, (y3, h1, h1)),
                ("cat", 0, (x3, 0, h1)),
            ],
            carry=[own_share, grad_half],
        )
        x4, y4 = both_ways(x4, y4, "g2")
        share_swap = swap(own_share, "swap_share")
        u1_swap, u2_cross = swap(u1_sum, "swap_u1"), cross(u2_sum, "cross_u2")
        grad_passed = partner(grad_half, "tensor", 1, "rows_core")
        d_shares = [(d1_all, x1, y1, (y2, r2), (x2, r2)), (d2_all, x2, y2, (y3, r1), (x3, r1))]
        grad_w_down, *last = place_shares(place, d_shares, units, False, width, 0, None, last)
        u1_all, u2_sum, own_share, x5, y5 = tick(
            [
                ("pick", u1_swap, u1_sum),
                ("add", u2_sum, u2_cross),
                ("add", own_share, share_swap),
                ("cat", 0, (y4, h2, h2)),
                ("cat", 0, (x4, 0, h2)),
            ],
            needs=[x4, y4],
        )
        x5, y5 = both_ways(x5, y5, "u1")
        u2_swap, share_swap = swap(u2_sum, "swap_u2"), partner(own_share, "dp", 2, "share_far")
        u2_all, own_share, x6, y6 = tick(
            [
                ("pick", u2_swap, u2_sum),
                ("add", own_share, share_swap),
                ("cat", 0, (y5, h1, h1), 1),
                ("cat", 0, (x5, 0, h1), 1),
            ],
            needs=[x5, y5],
        )
        x6, y6 = both_ways(x6, y6, "u2")
        grad_tokens = join(grad_half, grad_passed, wide)
        g_shares = [(g1_all, x3, y3, (y4, r2), (x4, r2)), (g2_all, x4, y4, (y5, r1), (x5, r1))]
        grad_w_gate, *last = place_shares(place, g_shares, units, True, width, 0, None, last)
        first_half = stack_rows // 32 * 16
        share_at = r2 + h1
        far = tick(
            [
                ("cat", (y6, share_at + first_half, stack_rows - first_half)),
                ("cat", (x6, share_at, first_half)),
                ("cat", (y6, h2, h2)),
                ("cat", (x6, 0, h2)),
            ],
        )
        share_x, share_y = both_ways(far[0], far[1], "far_share")
        x7, y7 = both_ways(far[2], far[3], "far_u2")
        u_shares = [(u1_all, x5, y5, (y6, r2), (x6, r2)), (u2_all, x6, y6, (y7, 0), (x7, 0))]
        grad_w_up, *last = place_shares(place, u_shares[:1], units, True, width, 0, None, last)
        grad_w_query, grad_w_key, grad_w_value, grad_w_out, small = unpack(
            [own_share, x6, y6, share_y, share_x],
            [
                (0, 0, stack_rows, 0),
                (1, 0, stack_rows, share_at),
                (2, 0, stack_rows, share_at),
                (3, 0, first_half, 0),
                (3, first_half, stack_rows - first_half, 0),
            ],
        )
        grad_w_up, _ = place_shares(
            place, u_shares[1:], units, True, width, cut_at, grad_w_up, [small]
        )
    gains = small[:2]
    gains = gains + partner(gains, "tensor", 1, "gains_core")
    grad_b = small[2]
    return (
        layer_out,
        grad_tokens,
        gains[0],
        grad_w_query.T,
        grad_b[:q_width],
        grad_w_key.T,
        grad_b[q_width : q_width + HEAD_DIM],
        grad_w_value.T,
        grad_b[q_width + HEAD_DIM : q_width + 2 * HEAD_DIM],
        grad_w_out,
        gains[1],
        grad_w_gate,
        grad_w_up,
        grad_w_down,
    )


def solution(mesh):
    placed = (
        P(("dp", "blk"), None),
        P("dp", None),
        P(),
        P(None, "tensor"),
        P("tensor"),
        P(None, "tensor"),
        P("tensor"),
        P(None, "tensor"),
        P("tensor"),
        P("tensor", None),
        P(),
        P(None, "tensor"),
        P(None, "tensor"),
        P("tensor", None),
        P(("dp", "blk"), None),
    )
    return jax.shard_map(
        local,
        mesh=mesh,
        in_specs=placed,
        out_specs=(
            P(("dp", "blk"), None),
            P(("dp", "blk"), None),
            P(),
            P(None, "tensor"),
            P("tensor"),
            P(None, "tensor"),
            P("tensor"),
            P(None, "tensor"),
            P("tensor"),
            P("tensor", None),
            P(),
            P(None, "tensor"),
            P(None, "tensor"),
            P("tensor", None),
        ),
        check_vma=False,
    )
```

```python
import functools
import math

import jax
import jax.numpy as jnp
from jax import lax
from jax.experimental import pallas as pl
from jax.experimental.pallas import tpu as pltpu
from jax.sharding import PartitionSpec as P

HEAD_DIM = 64

epsilon = 1e-06
rope_base = 1000000.0
masked_value = -1e30

low = jnp.bfloat16
wide = jnp.float32
vmem_limit = 34 * 1024 * 1024


def dot_nn(left, right):
    return lax.dot_general(left, right, (((1,), (0,)), ((), ())), preferred_element_type=wide)


def dot_nt(left, right):
    return lax.dot_general(left, right, (((1,), (1,)), ((), ())), preferred_element_type=wide)


def dot_tn(left, right):
    return lax.dot_general(left, right, (((0,), (0,)), ((), ())), preferred_element_type=wide)


def partner(value, axis, step, name):
    count = lax.axis_size(axis)
    with jax.named_scope(name):
        return lax.ppermute(value, axis, [(i, i ^ step) for i in range(count)])


def gather_blocks(piece, name):
    count = lax.axis_size("blk")
    return [piece] + [partner(piece, "blk", r, name) for r in range(1, count)]


def relay_far(near, own, name):
    count = lax.axis_size("blk")
    rows = own.shape[0]
    halved = rows % 32 == 0
    cuts = [slice(0, rows // 2), slice(rows // 2, rows)] if halved else [slice(0, rows)]
    pieces = {}
    for r in range(1, count):
        if r in near:
            pieces[r] = [near[r]]
            continue
        low_bit = r & -r
        high_bit = 1 << (r.bit_length() - 1)
        pieces[r] = []
        for i, (bit, rows_cut) in enumerate(zip((high_bit, low_bit), cuts)):
            source = pieces[r ^ bit]
            part = source[i] if len(source) > 1 else source[0][rows_cut]
            pieces[r].append(partner(part, "blk", bit, name + "_relay"))
    return pieces


def gather_relayed(piece, name):
    count = lax.axis_size("blk")
    near = {r: partner(piece, "blk", r, name) for r in range(1, count) if r & (r - 1) == 0}
    pieces = relay_far(near, piece, name)
    return [[piece]] + [pieces[r] for r in range(1, count)]


def scatter_blocks(pieces, name):
    return [pieces[0]] + [partner(pieces[r], "blk", r, name) for r in range(1, len(pieces))]


def swap(value, name):
    with jax.named_scope(name):
        return lax.ppermute(value, "dp", [(0, 1), (1, 0), (2, 3), (3, 2)])


def cross(value, name):
    with jax.named_scope(name):
        return lax.ppermute(value, "dp", [(1, 2), (2, 1)])


def call(body, outs, ins, scratch=(), in_specs=None, after=(), carry=(), moves=None):
    anywhere = pl.BlockSpec(memory_space=pl.ANY)
    whole = pl.BlockSpec(memory_space=pltpu.VMEM)
    in_specs = list(in_specs or [anywhere if moves else whole] * len(ins))
    given, waited, made = len(ins), len(after) + len(carry), len(outs)

    def run(*refs):
        results = given + waited
        body(*refs[:given], *refs[results : results + made], *refs[results + made + len(carry) :])

    return pl.pallas_call(
        run,
        name=getattr(body, "func", body).__name__,
        out_shape=tuple(outs) + tuple(shape(value.shape, value.dtype) for value in carry),
        in_specs=in_specs + [anywhere] * waited,
        out_specs=tuple([anywhere if moves == "all" else whole] * made + [anywhere] * len(carry)),
        scratch_shapes=list(scratch),
        input_output_aliases={given + len(after) + i: made + i for i in range(len(carry))},
        cost_estimate=pl.CostEstimate(flops=0, bytes_accessed=0, transcendentals=0),
        compiler_params=pltpu.CompilerParams(vmem_limit_bytes=vmem_limit),
    )(*ins, *after, *carry)


def shape(dims, kind):
    return jax.ShapeDtypeStruct(dims, kind)


in_smem = pl.BlockSpec(memory_space=pltpu.SMEM)
in_vmem = pl.BlockSpec(memory_space=pltpu.VMEM)
in_hbm = pl.BlockSpec(memory_space=pltpu.HBM)


def arriving(pairs, sems):
    copies = []
    for i, (source, target) in enumerate(pairs):
        copies.append(pltpu.make_async_copy(source, target, sems.at[i]))
        copies[-1].start()
    return copies


def as_row(column):
    return jnp.broadcast_to(column, (column.shape[0], 128)).T[:1]


def as_column(row):
    width = row.shape[1]
    padded = -(-width // 128) * 128
    row = row.astype(wide)
    if padded != width:
        row = jnp.concatenate([row, jnp.zeros((1, padded - width), wide)], axis=1)
    return jnp.broadcast_to(row, (128, padded)).T[:width, :1]


def segment_start(lengths_ref, rows):
    start = jnp.zeros_like(rows)
    end = jnp.int32(0)
    for i in range(lengths_ref.shape[1]):
        end = end + lengths_ref[0, i]
        start = jnp.where(rows >= end, end, start)
    return start


def rotate(pair, cosine, sine):
    half = HEAD_DIM // 2
    first, second = pair[:half], pair[half:]
    return jnp.concatenate(
        [first * cosine - second * sine, second * cosine + first * sine], axis=0
    )


def enter_kernel(
    lengths_ref, place_ref, small_ref, turn_ref, tokens_in, wq_in, wk_in, wv_in,
    q_ref, kv_ref, normed_ref, tokens_t_ref, cos_ref, sin_ref, tokens_ref, wq_ref, wk_ref, wv_ref, sems,
):
    ins = (tokens_in, wq_in, wk_in, wv_in)
    copies = arriving(zip(ins, (tokens_ref, wq_ref, wk_ref, wv_ref)), sems)
    rows, width = tokens_ref.shape
    q_width = wq_ref.shape[0]
    small = small_ref[...].astype(wide)
    gain = small[:, :width]
    bias = as_column(small[:, width:])
    copies[0].wait()
    hidden = tokens_ref[...].astype(wide)
    inverse = lax.rsqrt(jnp.mean(hidden * hidden, axis=1, keepdims=True) + epsilon)
    normed = (hidden * inverse * gain).astype(low)
    tokens_t_ref[...] = hidden.T.astype(low)
    normed_ref[...] = normed.astype(wide).T.astype(low)
    index = place_ref[0] * rows + lax.broadcasted_iota(jnp.int32, (1, rows), 1)
    position = (index - segment_start(lengths_ref, index)).astype(wide)
    angles = turn_ref[...] * position
    cosine, sine = jnp.cos(angles), jnp.sin(angles)
    cos_ref[...] = cosine
    sin_ref[...] = sine
    for copy in copies[1:]:
        copy.wait()
    q_lin = dot_nt(wq_ref[...], normed) + bias[:q_width]
    for h in range(q_lin.shape[0] // HEAD_DIM):
        head = rotate(q_lin[h * HEAD_DIM : (h + 1) * HEAD_DIM], cosine, sine)
        q_ref[h * HEAD_DIM : (h + 1) * HEAD_DIM, :] = head.astype(low) * low(HEAD_DIM**-0.5)
    k_lin = dot_nt(wk_ref[...], normed) + bias[q_width : q_width + HEAD_DIM]
    v_lin = dot_nt(wv_ref[...], normed) + bias[q_width + HEAD_DIM :]
    kv_ref[...] = jnp.concatenate([rotate(k_lin, cosine, sine), v_lin], axis=0).T.astype(low)


def weights_kernel(
    whole_down, lengths_ref, place_ref, gate_in, up_in, down_in, cotangent_in,
    gate_t_ref, gate_own_ref, up_t_ref, up_own_ref, down_t_ref, down_ref, mine_ref, other_ref,
    gate_ref, up_ref, cotangent_ref, turned_ref, grad_ref, sems,
):
    units = gate_t_ref.shape[0]
    hidden = gate_in.shape[1]
    window = turned_ref.shape[0]
    first = place_ref[0] * units
    base = pl.multiple_of(jnp.minimum(first // 128 * 128, hidden - window), 128)
    down_rows = down_in.at[pl.ds(pl.multiple_of(first, 16), units), :] if whole_down else down_in
    copies = arriving(
        [
            (gate_in.at[:, pl.ds(base, window)], gate_ref),
            (up_in.at[:, pl.ds(base, window)], up_ref),
            (cotangent_in, cotangent_ref),
            (down_rows, down_ref),
        ],
        sems,
    )
    for copy, ref, turned, own in (
        (copies[0], gate_ref, gate_t_ref, gate_own_ref),
        (copies[1], up_ref, up_t_ref, up_own_ref),
    ):
        copy.wait()
        turned_ref[...] = ref[...].astype(wide).T
        part = turned_ref[pl.ds(pl.multiple_of(first - base, 8), units), :]
        turned[...] = part.astype(low)
        own[...] = part.T.astype(low)
    copies[2].wait()
    rows = cotangent_ref.shape[0]
    half = rows // 2
    row = place_ref[0] * rows + lax.broadcasted_iota(jnp.int32, (rows, 1), 0)
    end = jnp.int32(0)
    for i in range(lengths_ref.shape[1]):
        end = end + lengths_ref[0, i]
    grad_ref[...] = jnp.where(row < end, cotangent_ref[...].astype(wide), 0.0)
    core = place_ref[1]
    mine_ref[...] = grad_ref[pl.ds(pl.multiple_of(core * half, half), half), :].astype(low)
    other_ref[...] = grad_ref[pl.ds(pl.multiple_of((1 - core) * half, half), half), :].astype(low)
    copies[3].wait()
    down_t_ref[...] = down_ref[...].astype(wide).T.astype(low)


def mask_bias(key_base, key_rows, q_index, q_start):
    keys = key_base + lax.broadcasted_iota(jnp.int32, (key_rows, q_index.shape[1]), 0)
    return jnp.where((keys >= q_start) & (keys <= q_index), 0.0, masked_value)


def first_row(lengths_ref, row):
    start = jnp.int32(0)
    end = jnp.int32(0)
    for i in range(lengths_ref.shape[1]):
        end = end + lengths_ref[0, i]
        start = jnp.where(row >= end, end, start)
    return start


def attend_kernel(blocks, lengths_ref, place_ref, q_ref, w_out_ref, *refs):
    kv_refs = refs[:blocks]
    out_ref, log_ref, mine_ref, other_ref, kv_ref, acc_ref, max_ref, bias_ref, part_ref, score_ref = refs[blocks:]
    rows = q_ref.shape[1]
    heads = q_ref.shape[0] // HEAD_DIM
    own, core = place_ref[0], place_ref[1]
    for r in range(blocks):
        kv_ref[r] = kv_refs[r][...]
    q_index = own * rows + lax.broadcasted_iota(jnp.int32, (1, rows), 1)
    q_start = segment_start(lengths_ref, q_index)
    acc_ref[...] = jnp.zeros_like(acc_ref)
    max_ref[...] = jnp.full_like(max_ref, masked_value)

    def visit(block, carry):
        pair = kv_ref[block ^ own]
        keys = pair[:, :HEAD_DIM]
        values = pair.astype(wide).T[HEAD_DIM:].astype(low)
        values = jnp.concatenate([values, jnp.ones((16, rows), low)], axis=0)
        bias_ref[...] = mask_bias(block * rows, rows, q_index, q_start)

        def scores(h):
            score_ref[h % 2] = dot_nn(keys, q_ref[h * HEAD_DIM : (h + 1) * HEAD_DIM, :])

        def gather(h, weight, shrink):
            acc_ref[h] = acc_ref[h] * shrink + dot_nn(values, weight)

        scores(0)
        waiting = None
        for h in range(heads):
            if h + 1 < heads:
                scores(h + 1)
            masked = score_ref[h % 2] + bias_ref[...]
            old = max_ref[h : h + 1, :]
            new = jnp.maximum(old, jnp.max(masked, axis=0, keepdims=True))
            weight = jnp.exp(masked - new).astype(low)
            max_ref[h : h + 1, :] = new
            if waiting is not None:
                gather(*waiting)
            waiting = (h, weight, jnp.exp(old - new))
        gather(*waiting)
        return carry

    lax.fori_loop(first_row(lengths_ref, own * rows) // rows, own + 1, visit, 0)
    for h in range(heads):
        total = acc_ref[h, HEAD_DIM : HEAD_DIM + 1, :]
        out_ref[h * HEAD_DIM : (h + 1) * HEAD_DIM, :] = acc_ref[h, :HEAD_DIM, :] / total
        log_ref[h : h + 1, :] = max_ref[h : h + 1, :] + jnp.log(total)
    part_ref[...] = dot_tn(w_out_ref[...], out_ref[...].astype(low))
    half = mine_ref.shape[1]
    mine_ref[...] = part_ref[:, pl.ds(pl.multiple_of(core * half, half), half)]
    other_ref[...] = part_ref[:, pl.ds(pl.multiple_of((1 - core) * half, half), half)].astype(low)


def middle_kernel(place_ref, tokens_ref, part_ref, passed_ref, gain_ref, hidden_ref, normed_ref):
    half = hidden_ref.shape[1]
    mine = pl.ds(pl.multiple_of(place_ref[1] * half, half), half)
    hidden = tokens_ref[:, mine].astype(wide) + part_ref[...] + passed_ref[...].astype(wide)
    hidden_ref[...] = hidden
    inverse = lax.rsqrt(jnp.mean(hidden * hidden, axis=0, keepdims=True) + epsilon)
    normed_ref[...] = (hidden * inverse * as_column(gain_ref[...])).astype(low)


def hidden_kernel(parts, *refs):
    gy_refs, x_refs, refs = refs[: 2 * parts], refs[2 * parts : 4 * parts], refs[4 * parts :]
    gate_t_ref, up_t_ref, down_ref, gate_ref, up_ref = refs[:5]
    mixed_ref, grad_gate_ref, grad_up_ref, other_ref, mine_ref, x_ref, gy_ref = refs[5:]
    half = other_ref.shape[1]
    row = 0
    for k in range(2):
        at = 0
        for x, gy in zip(x_refs[k * parts : (k + 1) * parts], gy_refs[k * parts : (k + 1) * parts]):
            x_ref[at : at + x.shape[0], k * half : (k + 1) * half] = x[...]
            gy_ref[row : row + gy.shape[0], :] = gy[...]
            at += x.shape[0]
            row += gy.shape[0]
    x = x_ref[...]
    gate = dot_nn(gate_t_ref[...], x)
    up = dot_nn(up_t_ref[...], x)
    grad_mixed = dot_nt(down_ref[...], gy_ref[...])
    sigmoid = 1.0 / (1.0 + jnp.exp(-gate))
    silu = gate * sigmoid
    mixed_ref[...] = (silu * up).astype(low)
    grad_gate = (grad_mixed * up * sigmoid * (1.0 + gate * (1.0 - sigmoid))).astype(low)
    grad_up = (grad_mixed * silu).astype(low)
    grad_gate_ref[...] = grad_gate
    grad_up_ref[...] = grad_up
    back = (dot_nn(gate_ref[...], grad_gate) + dot_nn(up_ref[...], grad_up)).astype(low)
    other_ref[...] = back[:, :half]
    mine_ref[...] = back[:, half:]


def weight_kernel(transposed, first, counts, outputs, *refs):
    blocks = len(counts)
    lefts, parts, out_refs, right_ref = refs[:blocks], refs[blocks : -outputs - 1], refs[-outputs - 1 : -1], refs[-1]
    units = lefts[0].shape[0]
    columns = sum(ref.shape[0] for ref in out_refs) // units * 128
    last = first + columns
    total, at = None, 0
    for r in range(blocks):
        row = 0
        for k in range(2):
            place = 0
            for part in parts[at : at + counts[r]]:
                if transposed:
                    half = part.shape[1]
                    start, end = max(place, first), min(place + part.shape[0], last)
                    if start < end:
                        right_ref[r, start - first : end - first, k * half : (k + 1) * half] = part[
                            start - place : end - place, :
                        ]
                    place += part.shape[0]
                else:
                    right_ref[r, row : row + part.shape[0], :] = part[:, first:last]
                    row += part.shape[0]
            at += counts[r]
        left, right = lefts[r][...], right_ref[r]
        product = dot_nt(left, right) if transposed else dot_nn(left, right)
        total = product if total is None else total + product
    at = 0
    for out_ref in out_refs:
        for t in range(out_ref.shape[0] // units):
            out_ref[t * units : (t + 1) * units, :] = total[:, at : at + 128].astype(low)
            at += 128


def project_kernel(blocks, weight_ref, *refs):
    other_ref, mine_refs = refs[blocks], refs[blocks + 1 :]
    half = other_ref.shape[2]
    for r in range(blocks):
        part = dot_nn(weight_ref[...], refs[r][...]).astype(low)
        other_ref[r] = part[:, :half]
        mine_refs[r][...] = part[:, half:]


def add_kernel(*refs):
    count = (len(refs) - 1) // 2
    for i in range(count):
        refs[1 + count + i][...] = (refs[1 + i][...].astype(wide) + refs[0][i].astype(wide)).astype(low)


def pair_kernel(*refs):
    count = len(refs) // 3
    for i in range(count):
        refs[2 * count + i][...] = (refs[2 * i][...].astype(wide) + refs[2 * i + 1][...].astype(wide)).astype(low)


def join_kernel(place_ref, mine_ref, other_ref, out_ref):
    half = mine_ref.shape[0]
    core = place_ref[1]
    out_ref[pl.ds(pl.multiple_of(core * half, half), half), :] = mine_ref[...].astype(out_ref.dtype)
    out_ref[pl.ds(pl.multiple_of((1 - core) * half, half), half), :] = other_ref[...].astype(out_ref.dtype)


def wait_kernel(*refs):
    pass


def tick_kernel(ops, place_ref, *refs):
    ins, outs = refs[: -len(ops)], refs[-len(ops) :]
    end = (place_ref[2] == 0) | (place_ref[2] == 3)
    for (kind, args), out_ref in zip(ops, outs):
        sources = [(ins if given else outs)[i] for given, i, *_ in args]
        if kind == "add":
            out_ref[...] = (sources[0][...].astype(wide) + sources[1][...].astype(wide)).astype(low)
        elif kind == "pick":
            out_ref[...] = jnp.where(end, sources[0][...], sources[1][...])
        else:
            at = 0
            for source, (_, _, start, rows) in zip(sources, args):
                out_ref[at : at + rows, :] = source[start : start + rows, :]
                at += rows


def sum_blocks(refs, starts=None, rows=None):
    total = None
    for i, ref in enumerate(refs):
        value = ref[...] if starts is None else ref[starts[i] : starts[i] + rows, :]
        total = value.astype(wide) if total is None else total + value.astype(wide)
    return total


def layer_kernel(hidden_ref, *refs):
    out_ref = refs[-1]
    out_ref[...] = (hidden_ref[...] + sum_blocks(refs[:-1])).T.astype(low)


def grad_middle_kernel(hidden_ref, gain_ref, gy_ref, *refs):
    grad_ref, grad_low_ref, grad_gain_ref = refs[-3:]
    hidden = hidden_ref[...]
    inverse = lax.rsqrt(jnp.mean(hidden * hidden, axis=0, keepdims=True) + epsilon)
    grad_normed = sum_blocks(refs[:-3])
    weighted = as_column(gain_ref[...]) * grad_normed
    inner = jnp.mean(weighted * hidden, axis=0, keepdims=True)
    grad = inverse * weighted - hidden * (inverse * inverse * inverse * inner)
    grad = grad + gy_ref[...].astype(wide).T
    grad_ref[...] = grad
    grad_low_ref[...] = grad.astype(low)
    grad_gain_ref[...] = as_row(jnp.sum(grad_normed * hidden * inverse, axis=1, keepdims=True))


def back_enter_kernel(
    place_ref, gm_mine_ref, gm_other_ref, w_out_ref, out_ref, go_ref, delta_ref, gm_ref
):
    half = gm_mine_ref.shape[1]
    core = place_ref[1]
    gm_ref[:, pl.ds(pl.multiple_of(core * half, half), half)] = gm_mine_ref[...]
    gm_ref[:, pl.ds(pl.multiple_of((1 - core) * half, half), half)] = gm_other_ref[...]
    grad_out = dot_nn(w_out_ref[...], gm_ref[...]).astype(low)
    go_ref[...] = grad_out
    product = grad_out.astype(wide) * out_ref[...]
    for h in range(product.shape[0] // HEAD_DIM):
        delta_ref[h : h + 1, :] = jnp.sum(
            product[h * HEAD_DIM : (h + 1) * HEAD_DIM], axis=0, keepdims=True
        )


def attend_back_kernel(
    blocks, tile, lengths_ref, place_ref, go_ref, delta_ref, log_ref, q_ref, cos_ref, sin_ref, *refs,
):
    kv_refs, refs = refs[:blocks], refs[blocks:]
    (grad_q_ref, *grad_kv_refs), refs = refs[: blocks + 1], refs[blocks + 1 :]
    kv_ref, bias_ref, dq_ref, q_all_ref, go_all_ref, weight_ref, grad_ref, grad_kv_ref, score_ref, grad_weight_ref = refs
    rows = q_ref.shape[1]
    heads = grad_q_ref.shape[0] // HEAD_DIM
    own = place_ref[0]
    parts = rows // tile

    def lanes(h):
        return slice(h * rows, (h + 1) * rows)

    def span(h):
        return slice(h * HEAD_DIM, (h + 1) * HEAD_DIM)

    for r in range(blocks):
        kv_ref[r] = kv_refs[r][...]
        grad_kv_ref[r] = jnp.zeros_like(grad_kv_ref[r])
    for h in range(heads):
        q_all_ref[:, lanes(h)] = q_ref[span(h), :]
        go_all_ref[:, lanes(h)] = go_ref[span(h), :]
    dq_ref[...] = jnp.zeros_like(dq_ref)
    q_index = own * rows + lax.broadcasted_iota(jnp.int32, (1, rows), 1)
    q_start = segment_start(lengths_ref, q_index)

    def visit(block, carry):
        part = pl.multiple_of(block % parts * tile, tile)
        at = ((block // parts) ^ own, pl.ds(part, tile), slice(None))
        pair = kv_ref[at]
        keys = pair[:, :HEAD_DIM]
        values = pair[:, HEAD_DIM:]
        keys_t = pair.astype(wide).T[:HEAD_DIM].astype(low)
        bias_ref[...] = mask_bias(block * tile, tile, q_index, q_start)

        def products(h):
            score_ref[h % 2] = dot_nn(keys, q_all_ref[:, lanes(h)])
            grad_weight_ref[h % 2] = dot_nn(values, go_all_ref[:, lanes(h)])

        products(0)
        for h in range(heads):
            if h + 1 < heads:
                products(h + 1)
            weight = jnp.exp(score_ref[h % 2] + bias_ref[...] - log_ref[h : h + 1, :])
            grad = (weight * (grad_weight_ref[h % 2] - delta_ref[h : h + 1, :])).astype(low)
            weight_ref[:, lanes(h)] = weight.astype(low)
            grad_ref[:, lanes(h)] = grad
            dq_ref[span(h), :] += dot_nn(keys_t, grad)
        grad_keys = dot_nt(grad_ref[...], q_all_ref[...])
        grad_values = dot_nt(weight_ref[...], go_all_ref[...])
        grad_kv_ref[at] = jnp.concatenate([grad_keys, grad_values], axis=1).astype(low)
        return carry

    lax.fori_loop(first_row(lengths_ref, own * rows) // tile, (own + 1) * parts, visit, 0)
    for r in range(blocks):
        grad_kv_refs[r][...] = grad_kv_ref[r]
    for h in range(heads):
        turned = rotate(dq_ref[span(h), :] * HEAD_DIM**-0.5, cos_ref[...], -sin_ref[...])
        grad_q_ref[span(h), :] = turned.astype(low)


def query_kernel(
    place_ref, normed_ref, grad_q_ref, wq_ref, gm_mine_ref, gm_other_ref, out_ref,
    grad_wq_ref, part_ref, grad_bq_ref, grad_w_out_ref, gm_ref,
):
    half = gm_mine_ref.shape[1]
    core = place_ref[1]
    gm_ref[:, pl.ds(pl.multiple_of(core * half, half), half)] = gm_mine_ref[...]
    gm_ref[:, pl.ds(pl.multiple_of((1 - core) * half, half), half)] = gm_other_ref[...]
    grad_w_out_ref[...] = dot_nt(out_ref[...].astype(low), gm_ref[...]).astype(low)
    grad_q = grad_q_ref[...]
    grad_wq_ref[...] = dot_nt(grad_q, normed_ref[...]).astype(low)
    part_ref[...] = dot_tn(wq_ref[...], grad_q)
    grad_bq_ref[...] = dot_nt(jnp.ones((16, grad_q.shape[1]), low), grad_q)


def key_kernel(
    blocks, starts, place_ref, normed_ref, tokens_ref, part_ref, wk_ref, wv_ref, cos_ref, sin_ref,
    grad_wq_ref, grad_bq_ref, grad_w_out_ref, grad_gain_two_ref, *refs,
):
    kv_refs, share_refs, (mine_ref, other_ref, sum_ref, pack_ref) = refs[:blocks], refs[blocks : 2 * blocks], refs[2 * blocks :]
    both = sum_blocks(kv_refs, starts, tokens_ref.shape[1]).T
    both = jnp.concatenate(
        [rotate(both[:HEAD_DIM], cos_ref[...], -sin_ref[...]), both[HEAD_DIM:]], axis=0
    ).astype(low)
    total = part_ref[...] + dot_tn(wk_ref[...], both[:HEAD_DIM]) + dot_tn(wv_ref[...], both[HEAD_DIM:])
    sum_ref[...] = total
    half = mine_ref.shape[1]
    core = place_ref[1]
    mine_ref[...] = sum_ref[:, pl.ds(pl.multiple_of(core * half, half), half)]
    other_ref[...] = sum_ref[:, pl.ds(pl.multiple_of((1 - core) * half, half), half)].astype(low)
    hidden = tokens_ref[...].astype(wide)
    inverse = lax.rsqrt(jnp.mean(hidden * hidden, axis=0, keepdims=True) + epsilon)
    q_width, width = grad_wq_ref.shape
    kv_width = both.shape[0]
    at = 0
    pack_ref[at : at + q_width, :] = grad_wq_ref[...]
    at += q_width
    pack_ref[at : at + kv_width, :] = dot_nt(both, normed_ref[...]).astype(low)
    at += kv_width
    pack_ref[at : at + q_width, :] = grad_w_out_ref[...]
    at += q_width
    grad_gain = as_row(jnp.sum(total * (hidden * inverse), axis=1, keepdims=True))
    grad_bkv = dot_nt(jnp.ones((16, both.shape[1]), low), both)[:1]
    biases = jnp.concatenate(
        [grad_bq_ref[:1, :], grad_bkv, jnp.zeros((1, width - q_width - kv_width), wide)], axis=1
    )
    small = jnp.concatenate(
        [grad_gain, grad_gain_two_ref[...], biases, jnp.zeros((pack_ref.shape[0] - at - 3, width), wide)], axis=0
    )
    pack_ref[at:, :] = small.astype(low)
    share = pack_ref.shape[0] // blocks
    for r in range(blocks):
        start = pl.multiple_of((place_ref[0] ^ r) * share, share)
        for t in range(width // 128):
            share_refs[r][t * share : (t + 1) * share, :] = pack_ref[pl.ds(start, share), t * 128 : (t + 1) * 128]


def share_kernel(starts, *refs):
    refs[-1][...] = sum_blocks(refs[:-1], starts, refs[-1].shape[0]).astype(low)


def unpack_kernel(share, sources, place_ref, *refs):
    pieces, outs, (stack_ref, pack_ref) = refs[: len(sources)], refs[len(sources) : -2], refs[-2:]
    for ref, (r, first, rows, start) in zip(pieces, sources):
        stack_ref[r, first : first + rows, :] = ref[start : start + rows, :].astype(wide)
    for r in range(stack_ref.shape[0]):
        at = pl.ds(pl.multiple_of((place_ref[0] ^ r) * share, 8), share)
        for t in range(stack_ref.shape[1] // share):
            pack_ref[at, t * 128 : (t + 1) * 128] = stack_ref[r, t * share : (t + 1) * share, :]
    at = 0
    *outs, bias_q_ref, bias_k_ref, bias_v_ref = outs
    for out_ref in outs:
        out_ref[...] = pack_ref[at : at + out_ref.shape[0], :]
        at += out_ref.shape[0]
    start = 0
    for out_ref in (bias_q_ref, bias_k_ref, bias_v_ref):
        out_ref[...] = pack_ref[at : at + 1, start : start + out_ref.shape[1]]
        start += out_ref.shape[1]


def leave_kernel(place_ref, tokens_ref, mine_ref, passed_ref, gain_ref, grad_mid_ref, out_ref):
    half = mine_ref.shape[1]
    hidden = tokens_ref[:, pl.ds(pl.multiple_of(place_ref[1] * half, half), half)].astype(wide)
    inverse = lax.rsqrt(jnp.mean(hidden * hidden, axis=0, keepdims=True) + epsilon)
    weighted = as_column(gain_ref[...]) * (mine_ref[...] + passed_ref[...].astype(wide))
    inner = jnp.mean(weighted * hidden, axis=0, keepdims=True)
    grad = grad_mid_ref[...] + inverse * weighted - hidden * (inverse * inverse * inverse * inner)
    out_ref[...] = grad.T.astype(low)


def place_kernel(transposed, tiles, place_ref, refs, out_ref, all_ref):
    own_ref, near_x_ref, near_y_ref, *far_refs = refs
    step, tiles = tiles
    units = own_ref.shape[0]
    half = units // 2
    for r, ref in enumerate((own_ref, near_x_ref, near_y_ref)):
        start = pl.multiple_of((place_ref[0] ^ r) * units, 8)
        all_ref[pl.ds(start, units), :] = ref[...].astype(wide)
    for k in range(2):
        start = pl.multiple_of((place_ref[0] ^ 3) * units + k * half, 8)
        part = 2 * step + k

        @pl.when(part < tiles)
        def _(start=start, k=k):
            all_ref[pl.ds(start, half), :] = far_refs[k][...].astype(wide)

        @pl.when(part >= tiles)
        def _(start=start, k=k):
            all_ref[pl.ds(start, half), :] = far_refs[2 + k][...].astype(wide)

    if transposed:
        out_ref[...] = all_ref[...].T


def place_shares(place, shares, units, transposed, width, at, whole, last):
    tile, half = 128, units // 2
    counts = [share[0].shape[0] // units for share in shares]
    begins = [sum(counts[:i]) for i in range(len(counts))]
    first = at // tile
    ins, specs = [place], [in_smem]
    for (own, near_x, near_y, far_y, far_x), tiles, begin in zip(shares, counts, begins):

        def step_of(i, tiles=tiles, begin=begin):
            return jnp.clip(i - begin, 0, tiles - 1)

        def halves(start, k, later, tiles=tiles, step_of=step_of):
            def index(i):
                part = 2 * step_of(i) + k - (tiles if later else 0)
                return (start // half + jnp.clip(part, 0, tiles - 1), 0)

            return pl.BlockSpec((half, tile), index)

        ins += [own, near_x, near_y, far_y[0], far_y[0], far_x[0], far_x[0]]
        specs += [pl.BlockSpec((units, tile), lambda i, step_of=step_of: (step_of(i), 0))] * 3
        specs += [halves(far_y[1], k, False) for k in range(2)]
        specs += [halves(far_x[1], k, True) for k in range(2)]
    ins += last
    specs += [pl.BlockSpec(memory_space=pl.ANY)] * len(last)
    aliases = {}
    if whole is not None:
        aliases = {len(ins): 0}
        ins.append(whole)
        specs.append(pl.BlockSpec(memory_space=pl.ANY))

    def body(*refs):
        out_ref, token_ref = refs[len(ins) : len(ins) + 2]
        all_ref = refs[-1] if transposed else out_ref
        token_ref[...] = jnp.zeros_like(token_ref)
        for n, (tiles, begin) in enumerate(zip(counts, begins)):
            step = pl.program_id(0) - begin

            @pl.when((step >= 0) & (step < tiles))
            def _(n=n, step=step, tiles=tiles):
                place_kernel(transposed, (step, tiles), refs[0], refs[1 + 7 * n : 8 + 7 * n], out_ref, all_ref)

    if transposed:
        dims = (width, 4 * units)
        out_spec = pl.BlockSpec((tile, 4 * units), lambda i: (i + first, 0))
        scratch = [pltpu.VMEM((4 * units, tile), wide)]
    else:
        dims = (4 * units, width)
        out_spec = pl.BlockSpec((4 * units, tile), lambda i: (0, i + first))
        scratch = []
    return pl.pallas_call(
        body,
        name="place_kernel",
        out_shape=(shape(dims, wide), shape((8, 128), wide)),
        grid=(sum(counts),),
        in_specs=specs,
        out_specs=(out_spec, pl.BlockSpec((8, 128), lambda i: (0, 0))),
        scratch_shapes=scratch,
        input_output_aliases=aliases,
        cost_estimate=pl.CostEstimate(flops=0, bytes_accessed=0, transcendentals=0),
        compiler_params=pltpu.CompilerParams(vmem_limit_bytes=vmem_limit),
    )(*ins)


def local(
    tokens,
    lengths,
    norm1_gain,
    w_query,
    b_query,
    w_key,
    b_key,
    w_value,
    b_value,
    w_out,
    norm2_gain,
    w_gate,
    w_up,
    w_down,
    cotangent,
):
    rows, width = tokens.shape
    half = rows // 2
    blocks = lax.axis_size("blk")
    own_block = lax.axis_index("blk")
    own_core = lax.axis_index("tensor")
    q_width = w_query.shape[1]
    heads = q_width // HEAD_DIM
    units = w_gate.shape[1] // blocks
    place = jnp.stack([own_block, own_core, lax.axis_index("dp")]).astype(jnp.int32)
    gain_two = norm2_gain.reshape(1, width)
    key_tile = rows // 2

    half_dim = HEAD_DIM // 2
    turn = (rope_base ** (-2.0 * jnp.arange(half_dim, dtype=wide) / HEAD_DIM)).reshape(half_dim, 1)
    small = jnp.concatenate([norm1_gain, b_query, b_key, b_value]).reshape(1, -1)
    q_t, key_value, normed_t, tokens_t, cosine, sine = call(
        enter_kernel,
        [
            shape((q_width, rows), low),
            shape((rows, 2 * HEAD_DIM), low),
            shape((width, rows), low),
            shape((width, rows), low),
            shape((half_dim, rows), wide),
            shape((half_dim, rows), wide),
        ],
        [lengths, place, small, turn, tokens, w_query.T, w_key.T, w_value.T],
        [
            pltpu.VMEM((rows, width), low),
            pltpu.VMEM((q_width, width), low),
            pltpu.VMEM((HEAD_DIM, width), low),
            pltpu.VMEM((HEAD_DIM, width), low),
            pltpu.SemaphoreType.DMA((4,)),
        ],
        in_specs=[in_smem] * 2 + [in_vmem] * 2 + [in_hbm] * 4,
    )
    kv_blocks = gather_blocks(key_value, "kv")

    window = -(-(units + 127) // 128) * 128
    whole_down = units % 16 == 0
    down = w_down if whole_down else lax.dynamic_slice_in_dim(w_down, own_block * units, units, 0)
    gate_t, gate_own, up_t, up_own, down_t, down_own, grad_y_mine, grad_y_other = call(
        functools.partial(weights_kernel, whole_down),
        [
            shape((units, width), low),
            shape((width, units), low),
            shape((units, width), low),
            shape((width, units), low),
            shape((width, units), low),
            shape((units, width), low),
            shape((half, width), low),
            shape((half, width), low),
        ],
        [lengths, place, w_gate, w_up, down, cotangent],
        [
            pltpu.VMEM((width, window), low),
            pltpu.VMEM((width, window), low),
            pltpu.VMEM((rows, width), low),
            pltpu.VMEM((window, width), wide),
            pltpu.VMEM((rows, width), wide),
            pltpu.SemaphoreType.DMA((4,)),
        ],
        in_specs=[in_smem] * 2 + [in_hbm] * 4,
        after=[q_t],
    )
    gy_near = {r: partner(grad_y_mine, "blk", r, "gy") for r in range(1, blocks) if r & (r - 1) == 0}

    out_t, log_total, part_mine, part_other = call(
        functools.partial(attend_kernel, blocks),
        [
            shape((q_width, rows), wide),
            shape((heads + 1, rows), wide),
            shape((width, half), wide),
            shape((width, half), low),
        ],
        [lengths, place, q_t, w_out] + kv_blocks,
        [
            pltpu.VMEM((blocks, rows, 2 * HEAD_DIM), low),
            pltpu.VMEM((heads, HEAD_DIM + 16, rows), wide),
            pltpu.VMEM((heads + 1, rows), wide),
            pltpu.VMEM((rows, rows), wide),
            pltpu.VMEM((width, rows), wide),
            pltpu.VMEM((2, rows, rows), wide),
        ],
        in_specs=[in_smem] * 2 + [in_vmem] * (2 + blocks),
        after=[gate_t],
    )
    hidden, normed_two = call(
        middle_kernel,
        [shape((width, half), wide), shape((width, half), low)],
        [place, tokens_t, part_mine, partner(part_other, "tensor", 1, "part_core"), gain_two],
        in_specs=[in_smem] + [in_vmem] * 4,
        after=list(gy_near.values()),
    )

    last = [normed_two]

    def ordered(body, outs, ins, needs=(), **more):
        nonlocal last
        carry = more.get("carry", ())
        after = [v for v in last + list(needs) if not any(v is c for c in carry)]
        results = call(body, outs, ins, after=after, **more)
        last = [results[0]]
        return results

    def wait(carry, needs=()):
        return list(ordered(wait_kernel, [], [], needs=needs, carry=carry))

    def near(pieces):
        return [p for r, parts in enumerate(pieces) if r and r & (r - 1) == 0 for p in parts]

    def far(pieces):
        return [p for r, parts in enumerate(pieces) if r & (r - 1) for p in parts]

    kept = shape((units, rows), low)
    piece = shape((width, half), low)
    runs, back, passed = [], [None] * blocks, [None] * blocks

    def cores(parts, name):
        return [partner(part, "tensor", 1, name) for part in parts]

    x_parts, gy_parts = [], []

    def hidden_units(r, x_mine, x_other, gy_mine, gy_other):
        x_parts.append(x_other + x_mine)
        gy_parts.append(gy_other + gy_mine)
        runs.append(
            ordered(
                functools.partial(hidden_kernel, len(x_mine)),
                [kept, kept, kept, piece, piece],
                gy_parts[-1] + x_parts[-1] + [gate_t, up_t, down_own, gate_own, up_own],
                scratch=[pltpu.VMEM((width, rows), low), pltpu.VMEM((rows, width), low)],
            )
        )
        return runs[-1][3]

    def add_back(members, carry, needs=()):
        results = ordered(
            pair_kernel,
            [piece] * len(members),
            [value for r in members for value in (runs[r][4], passed[r])],
            needs=needs,
            carry=carry,
        )
        for r, value in zip(members, results):
            back[r] = partner(value, "blk", r, "back") if r else value
        return results[len(members) :]

    def hidden_weight(transposed, left, parts, first, shares):
        counts = [len(part) // 2 for part in parts]
        columns = sum(shares)
        dims = (columns, rows) if transposed else (rows, columns)
        return ordered(
            functools.partial(weight_kernel, transposed, first, counts, len(shares)),
            [shape((share // 128 * units, 128), low) for share in shares],
            [run[left] for run in runs] + sum(parts, []),
            scratch=[pltpu.VMEM((blocks,) + dims, low)],
        )

    def tick(ops, needs=(), carry=()):
        given, outs, listed = [], [], []
        for kind, *args in ops:
            spans = [arg if isinstance(arg, tuple) else (arg, 0, None) for arg in args]
            named, size = [], 0
            for value, start, count in spans:
                if isinstance(value, int):
                    entry, total = (False, value), outs[value].shape[0]
                else:
                    found = [i for i, known in enumerate(given) if known is value]
                    if not found:
                        given.append(value)
                    entry = (True, found[0] if found else len(given) - 1)
                    total = value.shape[0]
                count = total if count is None else count
                named.append(entry + (start, count))
                size = size + count if kind == "cat" else count
            listed.append((kind, named))
            outs.append(shape((size, 128), low))
        return ordered(
            functools.partial(tick_kernel, listed),
            outs,
            [place] + given,
            in_specs=[in_smem] + [in_vmem] * len(given),
            needs=needs,
            carry=carry,
        )

    x_near = {r: partner(normed_two, "blk", r, "x") for r in range(1, blocks) if r & (r - 1) == 0}
    other = hidden_units(
        0, [normed_two], cores([normed_two], "x_core"), [grad_y_mine], [grad_y_other]
    )
    other, *arrived = wait([other] + list(x_near.values()))
    passed[0] = partner(other, "tensor", 1, "back_core")
    x_near = dict(zip(x_near, arrived))
    x_mine = relay_far(x_near, normed_two, "x")
    gy_mine = relay_far(gy_near, grad_y_mine, "gy")
    x_other = {r: cores(parts, "x_core") for r, parts in x_mine.items() if r in x_near}
    gy_other = {r: cores(parts, "gy_core") for r, parts in gy_mine.items() if r in x_near}
    others = [hidden_units(r, x_mine[r], x_other[r], gy_mine[r], gy_other[r]) for r in x_near]
    fars = [r for r in x_mine if r not in x_near]
    parts = [part for r in fars for part in x_mine[r] + gy_mine[r]]
    results = wait(others + parts)
    for r in x_near:
        passed[r] = partner(results.pop(0), "tensor", 1, "back_core")
    for r in fars:
        x_mine[r] = [results.pop(0) for _ in x_mine[r]]
        gy_mine[r] = [results.pop(0) for _ in gy_mine[r]]
        x_other[r], gy_other[r] = cores(x_mine[r], "x_core"), cores(gy_mine[r], "gy_core")
    others = [hidden_units(r, x_mine[r], x_other[r], gy_mine[r], gy_other[r]) for r in fars]
    for r, other in zip(fars, add_back(list(x_near), others)):
        passed[r] = partner(other, "tensor", 1, "back_core")
    if len(fars) > 1:
        add_back(fars[:-1], [])
    cut_at = width // 2 // 128 * 128
    (d1,) = hidden_weight(False, 0, gy_parts, 0, [cut_at])
    d1_swap = swap(d1, "swap_d1")
    (d2,) = hidden_weight(False, 0, gy_parts, cut_at, [width - cut_at])
    layer_other, *layer_mine = ordered(
        functools.partial(project_kernel, blocks),
        [shape((blocks, width, half), low)] + [piece] * blocks,
        [down_t] + [run[0] for run in runs],
    )
    d2, layer_other = add_back(
        [blocks - 1, 0], [d2, layer_other], needs=back[1 : blocks - 1] + [d1_swap]
    )
    (d1_sum,) = tick([("add", d1, d1_swap)])
    d1_cross, d2_swap = cross(d1_sum, "cross_d1"), swap(d2, "swap_d2")
    layer_passed = partner(layer_other, "tensor", 1, "layer_core")
    g1, g2 = hidden_weight(True, 1, x_parts, 0, [cut_at, width - cut_at])
    u1, u2 = hidden_weight(True, 2, x_parts, 0, [cut_at, width - cut_at])
    d1_sum, d2_sum, d1_g1 = tick(
        [("add", d1_sum, d1_cross), ("add", d2, d2_swap), ("pick", g1, 0)], needs=back[1:]
    )
    grad_mid, grad_mid_low, grad_gain_two = ordered(
        grad_middle_kernel,
        [shape((width, half), wide), piece, shape((1, width), wide)],
        [hidden, gain_two, grad_y_mine] + back,
    )
    *layer_pieces, grad_mid_low, d1_g1, d2_sum = ordered(
        add_kernel, [piece] * blocks, [layer_passed] + layer_mine, carry=[grad_mid_low, d1_g1, d2_sum]
    )
    grad_mid_other = partner(grad_mid_low, "tensor", 1, "mid_core")
    layer_pieces = scatter_blocks(layer_pieces, "layer")
    d1_g1_swap, d2_cross = swap(d1_g1, "swap_d1_g1"), cross(d2_sum, "cross_d2")

    grad_out, delta = ordered(
        back_enter_kernel,
        [shape((q_width, rows), low), shape((heads + 1, rows), wide)],
        [place, grad_mid_low, grad_mid_other, w_out, out_t],
        scratch=[pltpu.VMEM((width, rows), low)],
        in_specs=[in_smem] + [in_vmem] * 4,
    )

    grad_q, *grad_kv = ordered(
        functools.partial(attend_back_kernel, blocks, key_tile),
        [shape((q_width, rows), low)] + [shape((rows, 2 * HEAD_DIM), low)] * blocks,
        [lengths, place, grad_out, delta, log_total, q_t, cosine, sine] + kv_blocks,
        scratch=[
            pltpu.VMEM((blocks, rows, 2 * HEAD_DIM), low),
            pltpu.VMEM((key_tile, rows), wide),
            pltpu.VMEM((q_width, rows), wide),
            pltpu.VMEM((HEAD_DIM, heads * rows), low),
            pltpu.VMEM((HEAD_DIM, heads * rows), low),
            pltpu.VMEM((key_tile, heads * rows), low),
            pltpu.VMEM((key_tile, heads * rows), low),
            pltpu.VMEM((blocks, rows, 2 * HEAD_DIM), low),
            pltpu.VMEM((2, key_tile, rows), wide),
            pltpu.VMEM((2, key_tile, rows), wide),
        ],
        in_specs=[in_smem] * 2 + [in_vmem] * (6 + blocks),
    )
    pack_rows = -(-(2 * q_width + 2 * HEAD_DIM + 3) // (16 * blocks)) * 16 * blocks
    share = pack_rows // blocks
    stack_rows = share * (width // 128)

    def query_back():
        return ordered(
            query_kernel,
            [
                shape((q_width, width), low),
                shape((width, rows), wide),
                shape((16, q_width), wide),
                shape((q_width, width), low),
            ],
            [place, normed_t, grad_q, w_query.T, grad_mid_low, grad_mid_other, out_t],
            scratch=[pltpu.VMEM((width, rows), low)],
            in_specs=[in_smem] + [in_vmem] * 6,
        )

    def key_back(kv_pieces, starts):
        return ordered(
            functools.partial(key_kernel, blocks, starts),
            [shape((stack_rows, 128), low)] * blocks + [shape((width, half), wide), shape((width, half), low)],
            [
                place, normed_t, tokens_t, normed_part, w_key.T, w_value.T, cosine, sine,
                grad_w_query, grad_b_query, grad_w_out, grad_gain_two,
            ] + kv_pieces,
            scratch=[pltpu.VMEM((width, rows), wide), pltpu.VMEM((pack_rows, width), low)],
            in_specs=[in_smem] + [in_vmem] * (11 + blocks),
        )

    def sum_share(pieces, starts):
        (own,) = ordered(
            functools.partial(share_kernel, starts), [shape((stack_rows, 128), low)], pieces
        )
        return own

    def leave(normed_mine, normed_passed):
        (grad_half,) = ordered(
            leave_kernel,
            [shape((half, width), low)],
            [place, tokens_t, normed_mine, normed_passed, norm1_gain.reshape(1, width), grad_mid],
            in_specs=[in_smem] + [in_vmem] * 5,
        )
        return grad_half

    def join(mine, other, kind):
        (whole,) = ordered(
            join_kernel,
            [shape((rows, width), kind)],
            [place, mine.astype(kind), other.astype(kind)],
            in_specs=[in_smem] + [in_vmem] * 2,
        )
        return whole

    def layer_leave():
        (layer_half,) = ordered(layer_kernel, [shape((half, width), low)], [hidden] + layer_pieces)
        return layer_half

    def unpack(pieces, sources):
        return ordered(
            functools.partial(unpack_kernel, share, sources),
            [
                shape((q_width, width), wide),
                shape((HEAD_DIM, width), wide),
                shape((HEAD_DIM, width), wide),
                shape((q_width, width), wide),
                shape((2, width), wide),
                shape((1, q_width), wide),
                shape((1, HEAD_DIM), wide),
                shape((1, HEAD_DIM), wide),
            ],
            [place] + pieces,
            scratch=[pltpu.VMEM((blocks, stack_rows, 128), wide), pltpu.VMEM((pack_rows, width), wide)],
            in_specs=[in_smem] + [in_vmem] * len(pieces),
        )

    if blocks != 4:
        kv_pieces = scatter_blocks(grad_kv, "grad_kv")
        grad_w_query, normed_part, grad_b_query, grad_w_out = query_back()
        *shares, normed_mine, normed_other = key_back(kv_pieces, [0] * blocks)
        layer_half = layer_leave()
        layer_out = join(layer_half, partner(layer_half, "tensor", 1, "rows_core"), low)
        grad_half = leave(normed_mine, partner(normed_other, "tensor", 1, "normed_core"))
        grad_tokens = join(grad_half, partner(grad_half, "tensor", 1, "rows_core"), wide)
        own_share = sum_share(scatter_blocks(shares, "shares"), [0] * blocks)
        own_share = lax.psum(own_share, "dp")
        pieces = gather_blocks(own_share, "all_share")
        grad_w_query, grad_w_key, grad_w_value, grad_w_out, gains, *biases = unpack(
            pieces, [(r, 0, stack_rows, 0) for r in range(blocks)]
        )

        def gather_weight(first, second, transposed):
            stacked = lax.psum(jnp.concatenate([first, second], axis=0), "dp")
            every = lax.all_gather(stacked, "blk").reshape(blocks, width // 128, units, 128)
            order = (1, 3, 0, 2) if transposed else (0, 2, 1, 3)
            dims = (width, blocks * units) if transposed else (blocks * units, width)
            return every.transpose(order).reshape(dims).astype(wide)

        grad_w_down = gather_weight(d1, d2, False)
        grad_w_gate = gather_weight(g1, g2, True)
        grad_w_up = gather_weight(u1, u2, True)
    else:
        r1, r2 = d1.shape[0], d2.shape[0]
        h1, h2 = r1 // 2, r2 // 2

        def both_ways(x_buffer, y_buffer, name):
            return partner(x_buffer, "blk", 1, name + "_x"), partner(y_buffer, "blk", 2, name + "_y")

        d1_all, g1_sum, d2_sum, d2_g2, x1, y1, kv_far = tick(
            [
                ("pick", d1_g1_swap, d1_sum),
                ("add", g1, d1_g1_swap),
                ("add", d2_sum, d2_cross),
                ("pick", g2, 2),
                ("cat", 0, grad_kv[1]),
                ("cat", 0, grad_kv[2]),
            ],
            needs=layer_pieces[1:],
            carry=[grad_kv[3]],
        )
        x1, y1 = both_ways(x1, y1, "d1")
        kv_far = partner(kv_far, "blk", 3, "grad_kv")
        d2_g2_swap, g1_cross = swap(d2_g2, "swap_d2_g2"), cross(g1_sum, "cross_g1")
        grad_w_query, normed_part, grad_b_query, grad_w_out = query_back()
        layer_half = layer_leave()
        d2_all, g2_sum, g1_sum, g1_u1, x2, y2, layer_half = tick(
            [
                ("pick", d2_g2_swap, d2_sum),
                ("add", g2, d2_g2_swap),
                ("add", g1_sum, g1_cross),
                ("pick", u1, 2),
                ("cat", 0, (y1, h1, h1)),
                ("cat", 0, (x1, 0, h1)),
            ],
            needs=[x1, y1, kv_far],
            carry=[layer_half],
        )
        x2, y2 = both_ways(x2, y2, "d2")
        g1_u1_swap, g2_cross = swap(g1_u1, "swap_g1_u1"), cross(g2_sum, "cross_g2")
        layer_passed = partner(layer_half, "tensor", 1, "rows_core")
        *shares, normed_mine, normed_other = key_back([grad_kv[0], x1, y1, kv_far], [0, r1, r1, 0])
        g1_all, u1_sum, g2_sum, g2_u2, x3, y3, share_far, normed_other = tick(
            [
                ("pick", g1_u1_swap, g1_sum),
                ("add", u1, g1_u1_swap),
                ("add", g2_sum, g2_cross),
                ("pick", u2, 2),
                ("cat", 0, (y2, h2, h2), shares[1]),
                ("cat", 0, (x2, 0, h2), shares[2]),
            ],
            needs=[x2, y2],
            carry=[shares[3], normed_other],
        )
        x3, y3 = both_ways(x3, y3, "g1")
        share_far = partner(share_far, "blk", 3, "shares")
        g2_u2_swap, u1_cross = swap(g2_u2, "swap_g2_u2"), cross(u1_sum, "cross_u1")
        normed_passed = partner(normed_other, "tensor", 1, "normed_core")
        layer_out = join(layer_half, layer_passed, low)
        grad_half = leave(normed_mine, normed_passed)
        own_share = sum_share([shares[0], x3, y3, share_far], [0, r1 + h2, r1 + h2, 0])
        g2_all, u2_sum, u1_sum, x4, y4, own_share, grad_half = tick(
            [
                ("pick", g2_u2_swap, g2_sum),
                ("add", u2, g2_u2_swap),
                ("add", u1_sum, u1_cross),
                ("cat", 0, (y3, h1, h1)),
                ("cat", 0, (x3, 0, h1)),
            ],
            carry=[own_share, grad_half],
        )
        x4, y4 = both_ways(x4, y4, "g2")
        share_swap = swap(own_share, "swap_share")
        u1_swap, u2_cross = swap(u1_sum, "swap_u1"), cross(u2_sum, "cross_u2")
        grad_passed = partner(grad_half, "tensor", 1, "rows_core")
        d_shares = [(d1_all, x1, y1, (y2, r2), (x2, r2)), (d2_all, x2, y2, (y3, r1), (x3, r1))]
        grad_w_down, *last = place_shares(place, d_shares, units, False, width, 0, None, last)
        u1_all, u2_sum, own_share, x5, y5 = tick(
            [
                ("pick", u1_swap, u1_sum),
                ("add", u2_sum, u2_cross),
                ("add", own_share, share_swap),
                ("cat", 0, (y4, h2, h2)),
                ("cat", 0, (x4, 0, h2)),
            ],
            needs=[x4, y4],
        )
        x5, y5 = both_ways(x5, y5, "u1")
        u2_swap, share_swap = swap(u2_sum, "swap_u2"), partner(own_share, "dp", 2, "share_far")
        u2_all, own_share, x6, y6 = tick(
            [
                ("pick", u2_swap, u2_sum),
                ("add", own_share, share_swap),
                ("cat", 0, (y5, h1, h1), 1),
                ("cat", 0, (x5, 0, h1), 1),
            ],
            needs=[x5, y5],
        )
        x6, y6 = both_ways(x6, y6, "u2")
        grad_tokens = join(grad_half, grad_passed, wide)
        g_shares = [(g1_all, x3, y3, (y4, r2), (x4, r2)), (g2_all, x4, y4, (y5, r1), (x5, r1))]
        grad_w_gate, *last = place_shares(place, g_shares, units, True, width, 0, None, last)
        first_half = stack_rows // 32 * 16
        share_at = r2 + h1
        far = tick(
            [
                ("cat", (y6, share_at + first_half, stack_rows - first_half)),
                ("cat", (x6, share_at, first_half)),
                ("cat", (y6, h2, h2)),
                ("cat", (x6, 0, h2)),
            ],
        )
        share_x, share_y = both_ways(far[0], far[1], "far_share")
        x7, y7 = both_ways(far[2], far[3], "far_u2")
        u_shares = [(u1_all, x5, y5, (y6, r2), (x6, r2)), (u2_all, x6, y6, (y7, 0), (x7, 0))]
        grad_w_up, *last = place_shares(place, u_shares[:1], units, True, width, 0, None, last)
        grad_w_query, grad_w_key, grad_w_value, grad_w_out, gains, *biases = unpack(
            [own_share, x6, y6, share_y, share_x],
            [
                (0, 0, stack_rows, 0),
                (1, 0, stack_rows, share_at),
                (2, 0, stack_rows, share_at),
                (3, 0, first_half, 0),
                (3, first_half, stack_rows - first_half, 0),
            ],
        )
        grad_w_up, _ = place_shares(
            place, u_shares[1:], units, True, width, cut_at, grad_w_up, [gains]
        )
    gains = gains + partner(gains, "tensor", 1, "gains_core")
    grad_b_query, grad_b_key, grad_b_value = (bias.reshape(-1) for bias in biases)
    return (
        layer_out,
        grad_tokens,
        gains[0],
        grad_w_query.T,
        grad_b_query,
        grad_w_key.T,
        grad_b_key,
        grad_w_value.T,
        grad_b_value,
        grad_w_out,
        gains[1],
        grad_w_gate,
        grad_w_up,
        grad_w_down,
    )


def solution(mesh):
    placed = (
        P(("dp", "blk"), None),
        P("dp", None),
        P(),
        P(None, "tensor"),
        P("tensor"),
        P(None, "tensor"),
        P("tensor"),
        P(None, "tensor"),
        P("tensor"),
        P("tensor", None),
        P(),
        P(None, "tensor"),
        P(None, "tensor"),
        P("tensor", None),
        P(("dp", "blk"), None),
    )
    return jax.shard_map(
        local,
        mesh=mesh,
        in_specs=placed,
        out_specs=(
            P(("dp", "blk"), None),
            P(("dp", "blk"), None),
            P(),
            P(None, "tensor"),
            P("tensor"),
            P(None, "tensor"),
            P("tensor"),
            P(None, "tensor"),
            P("tensor"),
            P("tensor", None),
            P(),
            P(None, "tensor"),
            P(None, "tensor"),
            P("tensor", None),
        ),
        check_vma=False,
    )
```
